32 devices in a mesh: ctx: 8 (over y, x, core), fsdp: 4 (over z).
Axes of the slice: x: 2, y: 2, z: 4, core: 2. Of those that a mesh axis runs over, the one named last changes fastest.
Arguments:
- tokens: bfloat16 [4, 1024, 768], P('fsdp', 'ctx'), may hold values from -6 to 6
- cotangent: bfloat16 [4, 1024, 768], P('fsdp', 'ctx'), may hold values from -6 to 6
- att_gain: bfloat16 [768], P('fsdp'), may hold values from 0.25 to 1.75
- att_shift: bfloat16 [768], P('fsdp'), may hold values from -1.75 to 1.75
- ffn_gain: bfloat16 [768], P('fsdp'), may hold values from 0.25 to 1.75
- ffn_shift: bfloat16 [768], P('fsdp'), may hold values from -1.75 to 1.75
- qkv_weight: bfloat16 [768, 2304], P('fsdp'), may hold values from -0.3125 to 0.3125
- qkv_bias: bfloat16 [2304], P('fsdp'), may hold values from -3 to 3
- out_weight: bfloat16 [768, 768], P('fsdp'), may hold values from -0.875 to 0.875
- out_bias: bfloat16 [768], P('fsdp'), may hold values from -3 to 3
- up_weight: bfloat16 [768, 3072], P(None, 'fsdp'), may hold values from -0.21875 to 0.21875
- up_bias: bfloat16 [3072], P('fsdp'), may hold values from -3 to 3
- down_weight: bfloat16 [3072, 768], P('fsdp'), may hold values from -0.109375 to 0.109375
- down_bias: bfloat16 [768], P('fsdp'), may hold values from -3 to 3
Outputs:
- layer_out: bfloat16 [4, 1024, 768], P('fsdp', 'ctx')
- input_grad: float32 [4, 1024, 768], P('fsdp', 'ctx')
- att_dgain: float32 [768], P('fsdp')
- att_dshift: float32 [768], P('fsdp')
- ffn_dgain: float32 [768], P('fsdp')
- ffn_dshift: float32 [768], P('fsdp')
- qkv_dweight: float32 [768, 2304], P('fsdp')
- qkv_dbias: float32 [2304], P('fsdp')
- out_dweight: float32 [768, 768], P('fsdp')
- out_dbias: float32 [768], P('fsdp')
- up_dweight: float32 [768, 3072], P(None, 'fsdp')
- up_dbias: float32 [3072], P('fsdp')
- down_dweight: float32 [3072, 768], P('fsdp')
- down_dbias: float32 [768], P('fsdp')
The draws below stay inside these ranges and needn't reach their ends.
All inputs are finite; a program needn't handle non-finite values.
Results may differ from the reference program's by a relative error of at most 0.012.
The reference program's roundings to bfloat16 on the way count: a program that leaves them out, or rounds other values in their place, can miss the bound.
Values may be sent and summed in bfloat16 or wider, within the bound.
No kernel may reach another device: no remote copies, remote signals or barrier semaphores. Data moves between devices by JAX's collectives and lax.ppermute only.
A program may use at most 192 MiB of HBM per device.

```python
import math
import jax
import jax.numpy as jnp
from jax import lax

D = 768
HEADS = 12
HEAD_DIM = 64
ROT_DIMS = 16
FF = 3072
SEQ_DEV = 128
SEQ = 1024
SEQS = 4
N_CTX = 8


def shard_levels(own_key, dims, shards, low, top_value):
    loudness, own = 1.0, jax.random.fold_in(own_key, 6)
    for position, shards_of in shards:
        heights = jnp.exp(jax.random.uniform(jax.random.fold_in(own, position), (shards_of,), jnp.float32, low / len(shards), top_value / len(shards)))
        loudness = loudness * jnp.repeat(heights, dims[position] // shards_of).reshape([-1 if axis == position else 1 for axis in range(len(dims))])
    return loudness


def gaussian(own_key, extent, scale, bound, split=(), kind=jnp.bfloat16):
    array = scale * jax.random.normal(own_key, extent, jnp.float32)
    if split:
        array = array * shard_levels(own_key, extent, split, -0.22, 0.18)
    return jnp.clip(array, -bound, bound).astype(kind)


def setup_inputs(seed: int = 0) -> dict:
    streams_of = jax.random.split(jax.random.key(seed), 15)
    tokens = gaussian(streams_of[0], (SEQS, SEQ, D), 1.0, 6.0, ((0, 4), (1, 8)))
    cotangent = gaussian(streams_of[1], (SEQS, SEQ, D), 1.0, 6.0, ((0, 4), (1, 8)))
    att_gain = jnp.clip(1.0 + 0.15 * jax.random.normal(streams_of[2], (D,), jnp.float32), 0.25, 1.75).astype(jnp.bfloat16)
    att_shift = gaussian(streams_of[3], (D,), 0.3, 1.75, ((0, 4),))
    ffn_gain = jnp.clip(1.0 + 0.15 * jax.random.normal(streams_of[4], (D,), jnp.float32), 0.25, 1.75).astype(jnp.bfloat16)
    ffn_shift = gaussian(streams_of[5], (D,), 0.3, 1.75, ((0, 4),))
    qkv_weight = gaussian(streams_of[6], (D, 3 * D), (D // 2) ** -0.5, 0.3125, ((0, 4),))
    qkv_bias = gaussian(streams_of[7], (3 * D,), 0.5, 3.0, ((0, 4),))
    out_weight = gaussian(streams_of[8], (D, D), (D // 16) ** -0.5, 0.875, ((0, 4),))
    out_bias = gaussian(streams_of[9], (D,), 0.5, 3.0, ((0, 4),))
    up_weight = gaussian(streams_of[10], (D, FF), D ** -0.5, 0.21875, ((1, 4),))
    up_bias = gaussian(streams_of[11], (FF,), 0.5, 3.0, ((0, 4),))
    down_weight = gaussian(streams_of[12], (FF, D), FF ** -0.5, 0.109375, ((0, 4),))
    down_bias = gaussian(streams_of[13], (D,), 0.5, 3.0, ((0, 4),))
    return dict(tokens=tokens, cotangent=cotangent, att_gain=att_gain, att_shift=att_shift, ffn_gain=ffn_gain, ffn_shift=ffn_shift, qkv_weight=qkv_weight, qkv_bias=qkv_bias, out_weight=out_weight, out_bias=out_bias, up_weight=up_weight, up_bias=up_bias, down_weight=down_weight, down_bias=down_bias)


@jax.custom_vjp
def low(v):
    return lax.optimization_barrier(v.astype(jnp.bfloat16)).astype(jnp.float32)

@jax.custom_vjp
def low_back(v):
    return v

def low_keep(v):
    return (low(v), None)

def low_pass(kept, grad):
    return (grad,)

def back_keep(v):
    return (v, None)

def back_low(kept, grad):
    return (low(grad),)
low.defvjp(low_keep, low_pass)
low_back.defvjp(back_keep, back_low)

def matmul(earlier, update):
    return jnp.dot(earlier, update, precision=lax.Precision.HIGHEST, preferred_element_type=jnp.float32)

def layer_norm(values, norm_gain, norm_shift):
    center = values - lax.optimization_barrier(jnp.mean(values, axis=-1, keepdims=True))
    spread = lax.optimization_barrier(jnp.mean(center * center, axis=-1, keepdims=True))
    return center * lax.rsqrt(spread + 1e-05) * norm_gain + norm_shift

def stored_positions(rows, devices):
    row_order = jnp.arange(rows * devices, dtype=jnp.int32)
    device = row_order // rows
    within = row_order % rows
    half_rows = rows // 2
    return jnp.where(within < half_rows, device * half_rows + within, (2 * devices - 1 - device) * half_rows + within - half_rows).astype(jnp.int32)

def rotary_angles(positions):
    half_rot = ROT_DIMS // 2
    inverse = jnp.power(10000.0, -2.0 * jnp.arange(half_rot, dtype=jnp.float32) / ROT_DIMS)
    return positions.astype(jnp.float32)[:, None] * inverse[None, :]

def rotate(heads, angles):
    half_rot = ROT_DIMS // 2
    cosine = jnp.cos(angles)[:, None, :]
    sine_part = jnp.sin(angles)[:, None, :]
    lower_half = heads[..., :half_rot]
    upper_half = heads[..., half_rot:ROT_DIMS]
    return jnp.concatenate([lower_half * cosine - upper_half * sine_part, upper_half * cosine + lower_half * sine_part, heads[..., ROT_DIMS:]], axis=-1)

def attention(queries, keys_rot, values_proj, positions):
    length = queries.shape[0]
    block_rows = min(512, length)

    def one_block(pieces):
        query_block, query_pos = pieces
        scores = low_back(jnp.einsum('qhd,khd->hqk', query_block, keys_rot, precision=lax.Precision.HIGHEST) / math.sqrt(HEAD_DIM))
        scores = jnp.where(positions[None, None, :] <= query_pos[None, :, None], scores, -1000000000.0)
        row_top = lax.optimization_barrier(jnp.max(scores, axis=-1, keepdims=True))
        log_total = row_top + jnp.log(lax.optimization_barrier(jnp.sum(jnp.exp(scores - row_top), axis=-1, keepdims=True)))
        probability = low(jnp.exp(scores - log_total))
        return jnp.einsum('hqk,khd->qhd', probability, values_proj, precision=lax.Precision.HIGHEST)
    result = lax.map(jax.checkpoint(one_block), (queries.reshape(length // block_rows, block_rows, HEADS, HEAD_DIM), positions.reshape(length // block_rows, block_rows)))
    return result.reshape(length, HEADS * HEAD_DIM)

def layer(values, positions, params):
    att_gain, att_shift, ffn_gain, ffn_shift, qkv_weight, qkv_bias, out_weight, out_bias, up_weight, up_bias, down_weight, down_bias = params
    length = values.shape[0]
    first_in = low(layer_norm(values, att_gain, att_shift))
    second_in = low(layer_norm(values, ffn_gain, ffn_shift))
    joined = low_back(matmul(first_in, qkv_weight) + qkv_bias)
    angles = rotary_angles(positions)
    queries = low(rotate(joined[:, :D].reshape(length, HEADS, HEAD_DIM), angles))
    keys_rot = low(rotate(joined[:, D:2 * D].reshape(length, HEADS, HEAD_DIM), angles))
    values_proj = low(joined[:, 2 * D:].reshape(length, HEADS, HEAD_DIM))
    attended = low_back(low(attention(queries, keys_rot, values_proj, positions)))
    branch_att = matmul(attended, out_weight) + out_bias
    hidden = low_back(matmul(second_in, up_weight) + up_bias)
    active = low(jax.nn.gelu(hidden, approximate=False))
    branch_ffn = matmul(active, down_weight) + down_bias
    return values + branch_att + branch_ffn

def reference(tokens, cotangent, att_gain, att_shift, ffn_gain, ffn_shift, qkv_weight, qkv_bias, out_weight, out_bias, up_weight, up_bias, down_weight, down_bias):
    positions = stored_positions(SEQ_DEV, N_CTX)
    weights = tuple((param.astype(jnp.float32) for param in (att_gain, att_shift, ffn_gain, ffn_shift, qkv_weight, qkv_bias, out_weight, out_bias, up_weight, up_bias, down_weight, down_bias)))

    def forward(values, params):
        return layer(values, positions, params)

    def one_sequence(totals, pieces):
        seq_tokens, seq_cot = pieces
        output, pullback = jax.vjp(forward, seq_tokens.astype(jnp.float32), weights)
        grad_tokens, grad_weights = pullback(seq_cot.astype(jnp.float32))
        totals = tuple((earlier + update for earlier, update in zip(totals, grad_weights)))
        return (totals, (output.astype(jnp.bfloat16), grad_tokens))
    zero_sums = tuple((jnp.zeros(param.shape, jnp.float32) for param in weights))
    totals, (layer_out, input_grad) = lax.scan(one_sequence, zero_sums, (tokens, cotangent))
    return (layer_out, input_grad, totals[0], totals[1], totals[2], totals[3], totals[4], totals[5], totals[6], totals[7], totals[8], totals[9], totals[10], totals[11])
```

```python
import math

import jax
import jax.numpy as jnp
from jax import lax
from jax.experimental import pallas as pl
from jax.experimental.pallas import tpu as pltpu
from jax.sharding import PartitionSpec as P
import numpy as np

HEADS = 12
HEAD_DIM = 64
ROT_DIMS = 16


def layer_norm(values, norm_gain, norm_shift):
    center = values - jnp.mean(values, axis=-1, keepdims=True)
    spread = jnp.mean(center * center, axis=-1, keepdims=True)
    return center * lax.rsqrt(spread + 1e-05) * norm_gain + norm_shift


def exact_gelu(values):
    return jax.nn.gelu(values, approximate=False)


def stored_positions(rows, devices):
    row_order = jnp.arange(rows * devices, dtype=jnp.int32)
    device = row_order // rows
    within = row_order % rows
    half_rows = rows // 2
    return jnp.where(
        within < half_rows,
        device * half_rows + within,
        (2 * devices - 1 - device) * half_rows + within - half_rows,
    )


def rotary_angles(positions):
    half_rot = ROT_DIMS // 2
    inverse = jnp.power(10000.0, -2.0 * jnp.arange(half_rot, dtype=jnp.float32) / ROT_DIMS)
    return positions.astype(jnp.float32)[:, None] * inverse[None, :]


def rotate(heads, angles):
    half_rot = ROT_DIMS // 2
    cosine = jnp.cos(angles)[:, None, :]
    sine_part = jnp.sin(angles)[:, None, :]
    lower_half = heads[..., :half_rot]
    upper_half = heads[..., half_rot:ROT_DIMS]
    return jnp.concatenate(
        [
            lower_half * cosine - upper_half * sine_part,
            upper_half * cosine + lower_half * sine_part,
            heads[..., ROT_DIMS:],
        ],
        axis=-1,
    )


def to_order(stack, ctx_count, half_rows):
    tail = stack.shape[1:]
    shaped = stack.reshape((ctx_count, 2, half_rows) + tail)
    return jnp.concatenate(
        [shaped[:, 0].reshape((-1,) + tail), shaped[::-1, 1].reshape((-1,) + tail)], axis=0
    )


def from_order(stack, ctx_count, half_rows):
    tail = stack.shape[1:]
    middle = stack.shape[0] // 2
    first = stack[:middle].reshape((ctx_count, half_rows) + tail)
    second = stack[middle:].reshape((ctx_count, half_rows) + tail)[::-1]
    return jnp.stack([first, second], axis=1).reshape(stack.shape)


def scores_block(query_heads, key_heads, query_pos, key_pos):
    scores = jnp.einsum(
        "qhd,khd->hqk", query_heads, key_heads, preferred_element_type=jnp.float32
    ) / math.sqrt(HEAD_DIM)
    return jnp.where(key_pos[None, None, :] <= query_pos[None, :, None], scores, -1000000000.0)


def grad_block(
    query_heads, grad_heads, log_total, inner, query_pos, key_heads, value_heads, key_pos
):
    scores = scores_block(query_heads, key_heads, query_pos, key_pos)
    probability = jnp.exp(scores - log_total[:, :, None])
    prob_grad = jnp.einsum(
        "qhd,khd->hqk", grad_heads, value_heads, preferred_element_type=jnp.float32
    )
    score_grad = (probability * (prob_grad - inner[:, :, None])).astype(jnp.bfloat16)
    return (probability.astype(jnp.bfloat16), score_grad)


def shards(
    tokens,
    cotangent,
    att_gain,
    att_shift,
    ffn_gain,
    ffn_shift,
    qkv_weight,
    qkv_bias,
    out_weight,
    out_bias,
    up_weight,
    up_bias,
    down_weight,
    down_bias,
):
    model_width = tokens.shape[-1]
    rows_in = tokens.reshape(-1, model_width)
    grad_rows = cotangent.reshape(-1, model_width)
    own_rows = rows_in.shape[0]
    half_rows = own_rows // 2
    ctx_count = lax.axis_size("ctx")
    ctx_place = lax.axis_index("ctx")
    total_rows = own_rows * ctx_count
    all_pos = stored_positions(own_rows, ctx_count)
    own_pos = lax.dynamic_slice_in_dim(all_pos, ctx_place * own_rows, own_rows, 0)
    (
        gain_attend,
        shift_attend,
        gain_feed,
        shift_feed,
        mat_qkv,
        bias_qkv,
        mat_out,
        bias_out,
        bias_down,
    ) = (
        lax.all_gather(att_gain, "fsdp", axis=0, tiled=True),
        lax.all_gather(att_shift, "fsdp", axis=0, tiled=True),
        lax.all_gather(ffn_gain, "fsdp", axis=0, tiled=True),
        lax.all_gather(ffn_shift, "fsdp", axis=0, tiled=True),
        lax.all_gather(qkv_weight, "fsdp", axis=0, tiled=True),
        lax.all_gather(qkv_bias, "fsdp", axis=0, tiled=True),
        lax.all_gather(out_weight, "fsdp", axis=0, tiled=True),
        lax.all_gather(out_bias, "fsdp", axis=0, tiled=True),
        lax.all_gather(down_bias, "fsdp", axis=0, tiled=True),
    )
    tokens32 = rows_in.astype(jnp.float32)
    grad32 = grad_rows.astype(jnp.float32)
    first_norm, first_back = jax.vjp(
        layer_norm, tokens32, gain_attend.astype(jnp.float32), shift_attend.astype(jnp.float32)
    )
    second_norm, second_back = jax.vjp(
        layer_norm, tokens32, gain_feed.astype(jnp.float32), shift_feed.astype(jnp.float32)
    )
    first_in = first_norm.astype(jnp.bfloat16)
    second_in = second_norm.astype(jnp.bfloat16)
    joined = jnp.dot(first_in, mat_qkv, preferred_element_type=jnp.float32) + bias_qkv.astype(
        jnp.float32
    )
    angles = rotary_angles(own_pos)

    def project_heads(joined_rows):
        queries = rotate(joined_rows[:, :model_width].reshape(own_rows, HEADS, HEAD_DIM), angles)
        keys_rot = rotate(
            joined_rows[:, model_width : 2 * model_width].reshape(own_rows, HEADS, HEAD_DIM), angles
        )
        return (
            queries.reshape(own_rows, model_width),
            keys_rot.reshape(own_rows, model_width),
            joined_rows[:, 2 * model_width :],
        )

    (queries, keys_rot, values_rows), rotary_back = jax.vjp(project_heads, joined)
    query_low = queries.astype(jnp.bfloat16)
    key_low = keys_rot.astype(jnp.bfloat16)
    value_low = values_rows.astype(jnp.bfloat16)
    key_all, value_all = (
        lax.all_gather(key_low, "ctx", axis=0, tiled=True),
        lax.all_gather(value_low, "ctx", axis=0, tiled=True),
    )
    query_heads = query_low.reshape(own_rows, HEADS, HEAD_DIM)
    key_heads = to_order(key_all, ctx_count, half_rows).reshape(total_rows, HEADS, HEAD_DIM)
    value_heads = to_order(value_all, ctx_count, half_rows).reshape(total_rows, HEADS, HEAD_DIM)
    block_keys = min(1024, total_rows)

    def key_piece(block_index):
        start = block_index * block_keys
        return (
            lax.dynamic_slice_in_dim(key_heads, start, block_keys, 0),
            lax.dynamic_slice_in_dim(value_heads, start, block_keys, 0),
            start + jnp.arange(block_keys, dtype=jnp.int32),
        )

    need_low = (ctx_place + 1) * half_rows
    need_high = (2 * ctx_count - ctx_place) * half_rows
    counts = ((need_low + block_keys - 1) // block_keys, (need_high + block_keys - 1) // block_keys)
    query_parts = (query_heads[:half_rows], query_heads[half_rows:])
    pos_parts = (own_pos[:half_rows], own_pos[half_rows:])

    def half_lse(query_half, pos_half, count):

        def lse_step(block_index, carried):
            row_top, exp_total = carried
            key_block, value_skip, key_pos = key_piece(block_index)
            scores = scores_block(query_half, key_block, pos_half, key_pos)
            new_top = jnp.maximum(row_top, jnp.max(scores, axis=-1))
            exp_total = exp_total * jnp.exp(row_top - new_top) + jnp.sum(
                jnp.exp(scores - new_top[:, :, None]), axis=-1
            )
            return (new_top, exp_total)

        start_top = jnp.full((HEADS, half_rows), -1e30, jnp.float32)
        start_sum = jnp.zeros((HEADS, half_rows), jnp.float32)
        row_top, exp_total = lax.fori_loop(0, count, lse_step, (start_top, start_sum))
        return row_top + jnp.log(exp_total)

    lse_parts = [
        half_lse(query_parts[half_index], pos_parts[half_index], counts[half_index])
        for half_index in range(2)
    ]

    def half_mix(query_half, pos_half, lse_half, count):

        def mix_step(block_index, totals):
            key_block, value_block, key_pos = key_piece(block_index)
            scores = scores_block(query_half, key_block, pos_half, key_pos)
            probability = jnp.exp(scores - lse_half[:, :, None]).astype(jnp.bfloat16)
            return totals + jnp.einsum(
                "hqk,khd->qhd", probability, value_block, preferred_element_type=jnp.float32
            )

        return lax.fori_loop(
            0, count, mix_step, jnp.zeros((half_rows, HEADS, HEAD_DIM), jnp.float32)
        )

    attended = jnp.concatenate(
        [
            half_mix(
                query_parts[half_index],
                pos_parts[half_index],
                lse_parts[half_index],
                counts[half_index],
            )
            for half_index in range(2)
        ],
        axis=0,
    )
    attended_low = attended.reshape(own_rows, model_width).astype(jnp.bfloat16)
    branch_att = jnp.dot(
        attended_low, mat_out, preferred_element_type=jnp.float32
    ) + bias_out.astype(jnp.float32)
    second_all, grad_all = (
        lax.all_gather(second_in, "fsdp", axis=0, tiled=True),
        lax.all_gather(grad_rows, "fsdp", axis=0, tiled=True),
    )
    hidden = jnp.dot(second_all, up_weight, preferred_element_type=jnp.float32) + up_bias.astype(
        jnp.float32
    )
    active, gelu_back = jax.vjp(exact_gelu, hidden)
    active_low = active.astype(jnp.bfloat16)
    ffn_part = jnp.dot(active_low, down_weight, preferred_element_type=jnp.float32)
    active_grad = jnp.einsum("te,fe->tf", grad_all, down_weight, preferred_element_type=jnp.float32)
    hidden_grad = gelu_back(active_grad)[0].astype(jnp.bfloat16)
    down_dweight = jnp.einsum("tf,te->fe", active_low, grad_all, preferred_element_type=jnp.float32)
    up_dweight = jnp.einsum(
        "td,tf->df", second_all, hidden_grad, preferred_element_type=jnp.float32
    )
    up_dbias = jnp.sum(hidden_grad.astype(jnp.float32), axis=0)
    second_part = jnp.einsum(
        "tf,df->td", hidden_grad, up_weight, preferred_element_type=jnp.float32
    )
    ffn_sum, second_grad = (
        lax.psum_scatter(ffn_part, "fsdp", scatter_dimension=0, tiled=True),
        lax.psum_scatter(second_part, "fsdp", scatter_dimension=0, tiled=True),
    )
    branch_ffn = ffn_sum + bias_down.astype(jnp.float32)
    layer_out = (tokens32 + branch_att + branch_ffn).astype(jnp.bfloat16).reshape(tokens.shape)
    out_dweight = jnp.einsum(
        "td,te->de", attended_low, grad_rows, preferred_element_type=jnp.float32
    )
    row_sum = jnp.sum(grad32, axis=0)
    attended_grad = jnp.einsum(
        "te,de->td", grad_rows, mat_out, preferred_element_type=jnp.float32
    ).astype(jnp.bfloat16)
    grad_heads = attended_grad.reshape(own_rows, HEADS, HEAD_DIM)
    grad_parts = (grad_heads[:half_rows], grad_heads[half_rows:])

    def half_inner(query_half, grad_half, pos_half, lse_half, count):

        def inner_step(block_index, totals):
            key_block, value_block, key_pos = key_piece(block_index)
            scores = scores_block(query_half, key_block, pos_half, key_pos)
            probability = jnp.exp(scores - lse_half[:, :, None])
            prob_grad = jnp.einsum(
                "qhd,khd->hqk", grad_half, value_block, preferred_element_type=jnp.float32
            )
            return totals + jnp.sum(probability * prob_grad, axis=-1)

        return lax.fori_loop(0, count, inner_step, jnp.zeros((HEADS, half_rows), jnp.float32))

    inner_parts = [
        half_inner(
            query_parts[half_index],
            grad_parts[half_index],
            pos_parts[half_index],
            lse_parts[half_index],
            counts[half_index],
        )
        for half_index in range(2)
    ]
    half_zeros = jnp.zeros((half_rows, HEADS, HEAD_DIM), jnp.float32)

    def half_back(half_index, carried):
        query_half = query_parts[half_index]
        grad_half = grad_parts[half_index]

        def query_step(block_index, state):
            query_total, key_acc, value_acc = state
            key_block, value_block, key_pos = key_piece(block_index)
            prob_low, score_grad = grad_block(
                query_half,
                grad_half,
                lse_parts[half_index],
                inner_parts[half_index],
                pos_parts[half_index],
                key_block,
                value_block,
                key_pos,
            )
            key_part = jnp.einsum(
                "hqk,qhd->khd", score_grad, query_half, preferred_element_type=jnp.float32
            )
            value_part = jnp.einsum(
                "hqk,qhd->khd", prob_low, grad_half, preferred_element_type=jnp.float32
            )
            start = block_index * block_keys
            key_acc = lax.dynamic_update_slice_in_dim(
                key_acc,
                lax.dynamic_slice_in_dim(key_acc, start, block_keys, 0) + key_part,
                start,
                0,
            )
            value_acc = lax.dynamic_update_slice_in_dim(
                value_acc,
                lax.dynamic_slice_in_dim(value_acc, start, block_keys, 0) + value_part,
                start,
                0,
            )
            query_total = query_total + jnp.einsum(
                "hqk,khd->qhd", score_grad, key_block, preferred_element_type=jnp.float32
            )
            return (query_total, key_acc, value_acc)

        return lax.fori_loop(0, counts[half_index], query_step, carried)

    full_zeros = jnp.zeros((total_rows, HEADS, HEAD_DIM), jnp.float32)
    query_low_sum, key_acc, value_acc = half_back(0, (half_zeros, full_zeros, full_zeros))
    query_high_sum, key_acc, value_acc = half_back(1, (half_zeros, key_acc, value_acc))
    query_sum = jnp.concatenate([query_low_sum, query_high_sum], axis=0)
    key_stored = from_order(key_acc.reshape(total_rows, model_width), ctx_count, half_rows)
    value_stored = from_order(value_acc.reshape(total_rows, model_width), ctx_count, half_rows)
    key_sum, value_sum = (
        lax.psum_scatter(key_stored, "ctx", scatter_dimension=0, tiled=True),
        lax.psum_scatter(value_stored, "ctx", scatter_dimension=0, tiled=True),
    )
    query_grad = query_sum.reshape(own_rows, model_width) / math.sqrt(HEAD_DIM)
    key_grad = key_sum / math.sqrt(HEAD_DIM)
    joined_grad = rotary_back((query_grad, key_grad, value_sum))[0].astype(jnp.bfloat16)
    qkv_dweight = jnp.einsum("td,tf->df", first_in, joined_grad, preferred_element_type=jnp.float32)
    qkv_dbias = jnp.sum(joined_grad.astype(jnp.float32), axis=0)
    first_grad = jnp.einsum("tf,df->td", joined_grad, mat_qkv, preferred_element_type=jnp.float32)
    token_first, att_dgain, att_dshift = first_back(first_grad)
    token_second, ffn_dgain, ffn_dshift = second_back(second_grad)
    input_grad = (grad32 + token_first + token_second).reshape(tokens.shape)
    shares = (
        lax.psum_scatter(att_dgain, "fsdp", scatter_dimension=0, tiled=True),
        lax.psum_scatter(att_dshift, "fsdp", scatter_dimension=0, tiled=True),
        lax.psum_scatter(ffn_dgain, "fsdp", scatter_dimension=0, tiled=True),
        lax.psum_scatter(ffn_dshift, "fsdp", scatter_dimension=0, tiled=True),
        lax.psum_scatter(qkv_dweight, "fsdp", scatter_dimension=0, tiled=True),
        lax.psum_scatter(qkv_dbias, "fsdp", scatter_dimension=0, tiled=True),
        lax.psum_scatter(out_dweight, "fsdp", scatter_dimension=0, tiled=True),
        lax.psum_scatter(row_sum, "fsdp", scatter_dimension=0, tiled=True),
    ) + (up_dweight, up_dbias, down_dweight)
    totals = lax.psum(
        (
            shares[0],
            shares[1],
            shares[2],
            shares[3],
            shares[4],
            shares[5],
            shares[6],
            shares[7],
            shares[8],
            shares[9],
            shares[10],
        ),
        "ctx",
    )
    return (
        layer_out,
        input_grad,
        totals[0],
        totals[1],
        totals[2],
        totals[3],
        totals[4],
        totals[5],
        totals[6],
        totals[7],
        totals[8],
        totals[9],
        totals[10],
        totals[7],
    )


F32 = jnp.float32
BF16 = jnp.bfloat16
GROUPS = 4
GROUP_HEADS = HEADS // GROUPS
GROUP_COLS = GROUP_HEADS * HEAD_DIM
EXTRA = 16


def fits(mesh):
    return mesh.shape["ctx"] == 2 * GROUPS and mesh.shape["fsdp"] == GROUPS


def mm(left, right):
    return jnp.dot(left, right, preferred_element_type=F32)


def mm_nt(left, right):
    return lax.dot_general(left, right, (((1,), (1,)), ((), ())), preferred_element_type=F32)


def mm_tn(left, right):
    return lax.dot_general(left, right, (((0,), (0,)), ((), ())), preferred_element_type=F32)


def local_call(name, body, places, ins, outs, scratch=(), flops=0):
    moved = sum(math.prod(i.shape) * i.dtype.itemsize for i in ins)
    moved += sum(math.prod(s) * jnp.dtype(d).itemsize for s, d in outs)
    return pl.pallas_call(
        body,
        out_shape=[jax.ShapeDtypeStruct(s, d) for s, d in outs],
        in_specs=[pl.BlockSpec(memory_space=pltpu.SMEM)]
        + [pl.BlockSpec(memory_space=pltpu.VMEM)] * len(ins),
        out_specs=[pl.BlockSpec(memory_space=pltpu.VMEM)] * len(outs),
        scratch_shapes=list(scratch),
        compiler_params=pltpu.CompilerParams(vmem_limit_bytes=40 * 2**20),
        cost_estimate=pl.CostEstimate(flops=flops, bytes_accessed=moved, transcendentals=0),
        name=name,
    )(places, *ins)


def normed(values):
    center = values - jnp.mean(values, axis=-1, keepdims=True)
    spread = jnp.mean(center * center, axis=-1, keepdims=True)
    scale = lax.rsqrt(spread + 1e-05)
    return center * scale, scale


def rotary_tables(rows, devices):
    half = rows // 2
    order = np.arange(rows * devices)
    device, within = order // rows, order % rows
    position = np.where(
        within < half, device * half + within, (2 * devices - 1 - device) * half + within - half
    )
    pairs = ROT_DIMS // 2
    inverse = np.power(10000.0, -2.0 * np.arange(pairs) / ROT_DIMS).astype(np.float32)
    angle = (position.astype(np.float32)[:, None] * inverse[None, :]).astype(np.float32)
    cosine = np.ones((rows * devices, HEAD_DIM), np.float32)
    sine = np.zeros((rows * devices, HEAD_DIM), np.float32)
    cosine[:, :pairs] = cosine[:, pairs:ROT_DIMS] = np.cos(angle)
    sine[:, :pairs] = -np.sin(angle)
    sine[:, pairs:ROT_DIMS] = np.sin(angle)
    return np.tile(cosine, (1, 2)), np.tile(sine, (1, 2))


def swapped(values):
    lanes = values.shape[1]
    place = lax.broadcasted_iota(jnp.int32, values.shape, 1) % HEAD_DIM
    return jnp.where(
        place < ROT_DIMS // 2,
        pltpu.roll(values, lanes - ROT_DIMS // 2, 1),
        pltpu.roll(values, ROT_DIMS // 2, 1),
    )


def vector_body(places, p0, p1, p2, p3, vec, bias, box):
    z, group = places[1], places[0] // 2
    rows = p0.shape[0] - EXTRA
    shard = vec.shape[1] // GROUPS
    for k, piece in enumerate((p0, p1, p2, p3)):
        box[z ^ k] = piece[rows:, :].astype(F32)
    units = []
    for owner in range(GROUPS):
        block = box[owner]
        for item in range(6):
            vec[item : item + 1, owner * shard : (owner + 1) * shard] = block[
                item // 3 : item // 3 + 1, (item % 3) * shard : (item % 3 + 1) * shard
            ]
        for unit in range(3):
            units.append(block[2:3, unit * GROUP_COLS : (unit + 1) * GROUP_COLS])
    for slot, base in enumerate((GROUPS, 0, 2 * GROUPS)):
        own = units[base]
        for g in range(1, GROUPS):
            own = jnp.where(group == g, units[base + g], own)
        bias[0:1, slot * GROUP_COLS : (slot + 1) * GROUP_COLS] = own


def qkv_body(places, *refs):
    xs, gs, near, far = refs[0:4], refs[4:8], refs[8:12], refs[12:16]
    vec, bias, out_near, out_far, cos_tab, sin_tab = refs[16:22]
    fi, w, q_out, k_out, v_out, ag_out, ow, g_half, cos, sin = refs[22:]
    c, z = places[0], places[1]
    core = c % 2
    width = w.shape[0]
    shard = width // GROUPS
    part = shard // 2
    rows = xs[0].shape[0]
    half = rows // 2
    for k in range(GROUPS):
        base = (z ^ k) * shard
        w[pl.ds(pl.multiple_of(base + core * part, part), part), :] = near[k][0:part, :]
        w[pl.ds(pl.multiple_of(base + (1 - core) * part, part), part), :] = far[k][0:part, :]
    ow[pl.ds(pl.multiple_of(core * part, part), part), :] = out_near[...]
    ow[pl.ds(pl.multiple_of((1 - core) * part, part), part), :] = out_far[...]
    gain, shift = vec[0:1, :], vec[1:2, :]
    two = 2 * GROUP_COLS
    for side in range(2):
        for j in range(GROUPS):
            source = c ^ (2 * j)
            to = slice((side * GROUPS + j) * half, (side * GROUPS + j + 1) * half)
            at = pl.ds(pl.multiple_of(source * rows + side * half, half), half)
            norm, _ = normed(xs[j][side * half : (side + 1) * half, :].astype(F32))
            fi[to, :] = (norm * gain + shift).astype(BF16)
            g_half[to, :] = gs[j][side * half : (side + 1) * half, :]
            cos[to, :] = cos_tab[at, :]
            sin[to, :] = sin_tab[at, :]
    step = 2 * rows
    for i in range(GROUPS * rows // step):
        at = slice(i * step, (i + 1) * step)
        chunk = fi[at, :]
        kq = mm(chunk, w[:, :two]) + bias[0:1, :two]
        c3 = jnp.concatenate([cos[at, :]] * 3, axis=1)
        s3 = jnp.concatenate([sin[at, :]] * 3, axis=1)
        kq = kq * c3 + swapped(kq) * s3
        k_out[at, :] = kq[:, :GROUP_COLS].astype(BF16)
        q_out[at, :] = (kq[:, GROUP_COLS:] * HEAD_DIM**-0.5).astype(BF16)
        v_out[at, :] = (mm(chunk, w[:, two:]) + bias[0:1, two:]).astype(BF16)
        ag_out[at, :] = mm_nt(g_half[at, :], ow[...]).astype(BF16)


def attend_body(places, *refs):
    q, k, v, k_far, v_far, ag, g_half, ow = refs[0:8]
    batt = refs[8:12]
    dw_keep, dw_send, dkq, dv_out, far_out = refs[12:17]
    kbuf, vbuf, att, dwbuf = refs[17:]
    c = places[0]
    core = c % 2
    rows = batt[0].shape[0]
    half = rows // 2
    low = GROUPS * half
    devices = 2 * GROUPS
    for side in range(2):
        for part, (kr, vr) in enumerate(((k, v), (k_far, v_far))):
            to = slice((2 * side + part) * low, (2 * side + part + 1) * low)
            kbuf[to, :] = kr[side * low : (side + 1) * low, :]
            vbuf[to, :] = vr[side * low : (side + 1) * low, :]

    def token_pos(index, far):
        device = (c ^ (2 * (index // half))) ^ far
        return device * half + index % half

    q_place = token_pos(lax.broadcasted_iota(jnp.int32, (low, 1), 0), 0)
    k_index = lax.broadcasted_iota(jnp.int32, (1, 2 * low), 1)
    k_place = token_pos(k_index % low, k_index // low)

    def mirrored(place):
        return (2 * devices - 1 - place // half) * half + place % half

    allowed = (k_place <= q_place, mirrored(k_place) <= mirrored(q_place))

    for head in range(GROUP_HEADS):
        lanes = slice(head * HEAD_DIM, (head + 1) * HEAD_DIM)
        lanes2 = slice(GROUP_COLS + head * HEAD_DIM, GROUP_COLS + (head + 1) * HEAD_DIM)
        kh, vh = kbuf[:, lanes], vbuf[:, lanes]
        dk_parts, dv_parts = [], []
        for side in range(2):
            at = slice(side * low, (side + 1) * low)
            qh, gh = q[at, lanes], ag[at, lanes]
            spans = [slice(0, 2 * low)] if side == 0 else [slice(0, 2 * low), slice(2 * low, 4 * low)]
            scores = [mm_nt(qh, kh[s]) for s in spans]
            scores[-1] = jnp.where(allowed[side], scores[-1], -1000000000.0)
            top = jnp.max(scores[0], axis=-1, keepdims=True)
            for s in scores[1:]:
                top = jnp.maximum(top, jnp.max(s, axis=-1, keepdims=True))
            raised = [jnp.exp(s - top) for s in scores]
            total = sum(jnp.sum(r, axis=-1, keepdims=True) for r in raised)
            inverse = 1.0 / total
            probs = [r * inverse for r in raised]
            low_probs = [p.astype(BF16) for p in probs]
            mixed = sum(mm(p, vh[s]) for p, s in zip(low_probs, spans))
            att[at, lanes] = mixed.astype(BF16)
            prob_grads = [mm_nt(gh, vh[s]) for s in spans]
            inner = sum(
                jnp.sum(p * d, axis=-1, keepdims=True) for p, d in zip(probs, prob_grads)
            )
            score_grads = [(p * (d - inner)).astype(BF16) for p, d in zip(probs, prob_grads)]
            dkq[at, lanes2] = sum(mm(s, kh[a]) for s, a in zip(score_grads, spans)) * HEAD_DIM**-0.5
            dk_parts.append([mm_tn(s, qh) for s in score_grads])
            dv_parts.append([mm_tn(p, gh) for p in low_probs])
        dk = (dk_parts[0][0] + dk_parts[1][0], dk_parts[1][1])
        dv = (dv_parts[0][0] + dv_parts[1][0], dv_parts[1][1])
        for side in range(2):
            at = slice(side * low, (side + 1) * low)
            dkq[at, lanes] = dk[side][:low]
            dv_out[at, lanes] = dv[side][:low]
            far_out[at, lanes] = dk[side][low:].astype(BF16)
            far_out[at, lanes2] = dv[side][low:].astype(BF16)
    for side in range(2):
        at = slice(side * low, (side + 1) * low)
        branch = mm(att[at, :], ow[...])
        for j in range(GROUPS):
            batt[j][side * half : (side + 1) * half, :] = branch[
                j * half : (j + 1) * half, :
            ].astype(batt[j].dtype)
    dwbuf[...] = mm_tn(att[...], g_half[...])
    part = GROUP_COLS // 2
    dw_keep[...] = dwbuf[pl.ds(pl.multiple_of(core * part, part), part), :]
    dw_send[...] = dwbuf[pl.ds(pl.multiple_of((1 - core) * part, part), part), :].astype(BF16)


def joined_body(places, *refs):
    dkq, dv, far, w, fi, cos, sin, vec, ffn_vec = refs[0:9]
    xs, g_own = refs[9:13], refs[13]
    cas = refs[14:18]
    keep, send = refs[18:20]
    jgkq, jgv, dwbuf, first, ext = refs[20:]
    c, z = places[0], places[1]
    core, group = c % 2, c // 2
    rows = g_own.shape[0]
    half = rows // 2
    width = w.shape[0]
    shard = width // GROUPS
    part = shard // 2
    two = 2 * GROUP_COLS
    step = 2 * rows
    gain = vec[0:1, :]
    bias_kq = jnp.zeros((1, two), F32)
    bias_v = jnp.zeros((1, GROUP_COLS), F32)
    for i in range(GROUPS * rows // step):
        at = slice(i * step, (i + 1) * step)
        other = far[at, :].astype(F32)
        dk = dkq[at, :GROUP_COLS] + other[:, :GROUP_COLS]
        kq = jnp.concatenate([dk, dkq[at, GROUP_COLS:]], axis=1)
        c3 = jnp.concatenate([cos[at, :]] * 3, axis=1)
        s3 = jnp.concatenate([sin[at, :]] * 3, axis=1)
        low_kq = (kq * c3 - swapped(kq) * s3).astype(BF16)
        low_v = (dv[at, :] + other[:, GROUP_COLS:]).astype(BF16)
        jgkq[at, :] = low_kq
        jgv[at, :] = low_v
        bias_kq += jnp.sum(low_kq.astype(F32), axis=0, keepdims=True)
        bias_v += jnp.sum(low_v.astype(F32), axis=0, keepdims=True)
        first[at, :] = mm_nt(low_kq, w[:, :two]) + mm_nt(low_v, w[:, two:])
    dgain = jnp.zeros((1, width), F32)
    dshift = jnp.zeros((1, width), F32)
    for side in range(2):
        for j in range(GROUPS):
            at = slice((side * GROUPS + j) * half, (side * GROUPS + j + 1) * half)
            mine = slice(side * half, (side + 1) * half)
            norm, _ = normed(xs[j][mine, :].astype(F32))
            grad = first[at, :]
            dgain += jnp.sum(grad * norm, axis=0, keepdims=True)
            dshift += jnp.sum(grad, axis=0, keepdims=True)
            cas[j][mine, :] = (grad * gain).astype(cas[j].dtype)
    gsum = jnp.sum(g_own[...].astype(F32), axis=0, keepdims=True)
    dwbuf[:, :two] = mm_tn(fi[...], jgkq[...])
    dwbuf[:, two:] = mm_tn(fi[...], jgv[...])
    ext[...] = jnp.zeros_like(ext)
    for owner in range(GROUPS):
        own = slice(owner * shard, (owner + 1) * shard)
        for slot in range(3):
            unit = owner * 3 + slot
            kind = unit // GROUPS
            vector = (bias_kq[:, GROUP_COLS:], bias_kq[:, :GROUP_COLS], bias_v)[kind]
            to = slice(slot * GROUP_COLS, (slot + 1) * GROUP_COLS)
            ext[owner, 0:1, to] = jnp.where(group == unit % GROUPS, vector, 0.0)
        here = z == owner
        for slot, vector in enumerate((dgain[:, own], dshift[:, own], gsum[:, own])):
            ext[owner, 1:2, slot * shard : (slot + 1) * shard] = vector
        ext[owner, 2:3, 0:shard] = ffn_vec[0:1, own]
        ext[owner, 2:3, shard : 2 * shard] = ffn_vec[1:2, own]
        ext[owner, 2:3, 2 * shard : 3 * shard] = jnp.where(here, ffn_vec[2:3, 0:shard], 0.0)
        ext[owner, 3:4, :] = jnp.where(here, ffn_vec[2:3, shard:], 0.0)
    for k in range(GROUPS):
        owner = z ^ k
        base = owner * shard
        keep[k, 0:part, :] = dwbuf[pl.ds(pl.multiple_of(base + core * part, part), part), :]
        send[k, 0:part, :] = dwbuf[
            pl.ds(pl.multiple_of(base + (1 - core) * part, part), part), :
        ].astype(BF16)
        keep[k, part:, :] = ext[owner].astype(BF16).astype(F32)
        send[k, part:, :] = ext[owner].astype(BF16)


def split_sum_body(places, keep, got, own, *sends):
    for k in range(GROUPS):
        total = keep[k] + got[k].astype(F32)
        if k == 0:
            own[...] = total
        else:
            sends[k - 1][...] = total.astype(BF16)


def sum_body(places, own, a, b, c, out):
    out[...] = (own[...] + a[...].astype(F32) + b[...].astype(F32) + c[...].astype(F32)).astype(
        out.dtype
    )


def ffn_body(places, *refs):
    xs, gs = refs[0:4], refs[4:8]
    up_w, down_w, up_b, vec = refs[8:12]
    parts, cas = refs[12:16], refs[16:20]
    keep, send, sums = refs[20:23]
    si, gb, active, hidden_grad, second, dwbuf = refs[23:]
    c, z = places[0], places[1]
    rows = xs[0].shape[0]
    width = up_w.shape[0]
    hid = up_w.shape[1]
    gain, shift = vec[2:3, :], vec[3:4, :]
    for k in range(GROUPS):
        at = slice(k * rows, (k + 1) * rows)
        norm, _ = normed(xs[k][...].astype(F32))
        si[at, :] = (norm * gain + shift).astype(BF16)
        gb[at, :] = gs[k][...]
    step = 2 * rows
    bias_sum = jnp.zeros((1, hid), F32)
    for i in range(GROUPS * rows // step):
        at = slice(i * step, (i + 1) * step)
        hidden = mm(si[at, :], up_w[...]) + up_b[...].astype(F32)
        cdf = 0.5 + 0.5 * lax.erf(hidden * (0.5**0.5))
        density = jnp.exp(hidden * hidden * -0.5) * (1.0 / math.sqrt(2.0 * math.pi))
        active[at, :] = (hidden * cdf).astype(BF16)
        grad = (mm_nt(gb[at, :], down_w[...]) * (cdf + hidden * density)).astype(BF16)
        hidden_grad[at, :] = grad
        bias_sum += jnp.sum(grad.astype(F32), axis=0, keepdims=True)
        part = mm(active[at, :], down_w[...])
        second[at, :] = mm_nt(grad, up_w[...])
        for k in range(2):
            piece = parts[2 * i + k]
            piece[...] = part[k * rows : (k + 1) * rows, :].astype(piece.dtype)
    dgain = jnp.zeros((1, width), F32)
    dshift = jnp.zeros((1, width), F32)
    for k in range(GROUPS):
        at = slice(k * rows, (k + 1) * rows)
        norm, _ = normed(xs[k][...].astype(F32))
        grad = second[at, :]
        dgain += jnp.sum(grad * norm, axis=0, keepdims=True)
        dshift += jnp.sum(grad, axis=0, keepdims=True)
        cas[k][...] = (grad * gain).astype(cas[k].dtype)
    sums[0:1, :] = dgain
    sums[1:2, :] = dshift
    sums[2:3, :] = bias_sum
    dwbuf[0:width, :] = mm_tn(si[...], hidden_grad[...])
    dwbuf[width:, :] = mm_tn(active[...], gb[...])
    chunk = (width + hid) // (2 * GROUPS)
    for j in range(GROUPS):
        near = c ^ (2 * j)
        keep[j] = dwbuf[pl.ds(pl.multiple_of(near * chunk, chunk), chunk), :]
        far = near ^ 1
        send[j] = dwbuf[pl.ds(pl.multiple_of(far * chunk, chunk), chunk), :].astype(BF16)


def spread_body(places, *refs):
    near, far = refs[0:4], refs[4:8]
    up_dw, down_dw, buf = refs[8:]
    c = places[0]
    chunk = near[0].shape[0]
    for j in range(GROUPS):
        place = c ^ (2 * j)
        buf[pl.ds(pl.multiple_of(place * chunk, chunk), chunk), :] = near[j][...].astype(F32)
        buf[pl.ds(pl.multiple_of((place ^ 1) * chunk, chunk), chunk), :] = far[j][...].astype(F32)
    up_dw[...] = buf[0 : up_dw.shape[0], :]
    down_dw[...] = buf[up_dw.shape[0] :, :]


def finish_body(places, *refs):
    near, far = refs[0:4], refs[4:8]
    qkv_dw, vec, bias, up_db, box, tail = refs[8:]
    c = places[0]
    core, group = c % 2, c // 2
    part = near[0].shape[0] - EXTRA
    shard = 2 * part
    for j in range(GROUPS):
        place = group ^ j
        tail[place] = near[j][part:, :].astype(F32)
        box[place, pl.ds(pl.multiple_of(core * part, part), part), :] = near[j][0:part, :].astype(F32)
        box[place, pl.ds(pl.multiple_of((1 - core) * part, part), part), :] = far[j][
            0:part, :
        ].astype(F32)
    for g in range(GROUPS):
        for kind, slot in enumerate((1, 0, 2)):
            at = (kind * GROUPS + g) * GROUP_COLS
            qkv_dw[:, at : at + GROUP_COLS] = box[
                g, :, slot * GROUP_COLS : (slot + 1) * GROUP_COLS
            ]
    total = tail[0] + tail[1] + tail[2] + tail[3]
    bias[...] = total[0:1, :]
    for slot in range(3):
        vec[slot : slot + 1, :] = total[1:2, slot * shard : (slot + 1) * shard]
    vec[3:4, :] = total[2:3, 0:shard]
    vec[4:5, :] = total[2:3, shard : 2 * shard]
    up_db[0:1, 0:shard] = total[2:3, 2 * shard :]
    up_db[0:1, shard:] = total[3:4, :]


def token_body(places, *refs):
    x, g, vec = refs[0:3]
    outs, grads = refs[3:11], refs[11:19]
    layer_out, input_grad = refs[19:]
    values = x[...].astype(F32)
    total = values + vec[4:5, :] + vec[5:6, :]
    for piece in outs:
        total += piece[...].astype(F32)
    layer_out[...] = total.astype(BF16)
    norm, scale = normed(values)
    cot = grads[0][...]
    for piece in grads[1:]:
        cot += piece[...].astype(F32)
    shifted = cot - jnp.mean(cot, axis=-1, keepdims=True)
    shifted -= norm * jnp.mean(cot * norm, axis=-1, keepdims=True)
    input_grad[...] = g[...].astype(F32) + scale * shifted


def block_shards(
    tokens,
    cotangent,
    att_gain,
    att_shift,
    ffn_gain,
    ffn_shift,
    qkv_weight,
    qkv_bias,
    out_weight,
    out_bias,
    up_weight,
    up_bias,
    down_weight,
    down_bias,
):
    width = tokens.shape[-1]
    x = tokens.reshape(-1, width)
    g = cotangent.reshape(-1, width)
    rows = x.shape[0]
    n_ctx, n_z = lax.axis_size("ctx"), lax.axis_size("fsdp")
    c, z = lax.axis_index("ctx"), lax.axis_index("fsdp")
    core, group = c % 2, c // 2
    shard = width // n_z
    part = shard // 2
    hid = up_weight.shape[1]
    places = jnp.stack([c, z]).astype(jnp.int32)
    three = 3 * GROUP_COLS
    near_rows = GROUPS * rows

    def over_ctx(value, k):
        return lax.ppermute(value, "ctx", [(i, i ^ k) for i in range(n_ctx)])

    def over_z(value, k):
        return lax.ppermute(value, "fsdp", [(i, i ^ k) for i in range(n_z)])

    def over_both(value, pairs):
        return lax.ppermute(
            value, ("ctx", "fsdp"), [(a * n_z + b, d * n_z + e) for a, b, d, e in pairs]
        )

    def chips(value):
        return [value] + [over_ctx(value, 2 * j) for j in range(1, GROUPS)]

    vectors = jnp.concatenate(
        [att_gain, att_shift, ffn_gain, ffn_shift, out_bias, down_bias, qkv_bias]
    ).reshape(3, three)
    columns = [
        lax.dynamic_slice(qkv_weight, (core * part, base * width + group * GROUP_COLS), (part, GROUP_COLS))
        for base in (1, 0, 2)
    ]
    payload = jnp.concatenate(
        [jnp.concatenate(columns, axis=1), jnp.pad(vectors, ((0, EXTRA - 3), (0, 0)))], axis=0
    )
    near_w = [payload] + [over_z(payload, k) for k in range(1, n_z)]
    far_w = [over_ctx(p, 1) for p in near_w]
    own_out = lax.dynamic_slice(out_weight, (core * part, 0), (part, width))
    got = [
        over_both(own_out, [(a, a // 2, a, (a // 2) ^ k) for a in range(n_ctx)]) for k in range(1, n_z)
    ]
    out_near = jnp.where(z == group, own_out, got[0] + got[1] + got[2])
    out_far = over_ctx(out_near, 1)

    x_plane, g_plane = chips(x), chips(g)
    x_line = [x] + [over_z(x, k) for k in range(1, n_z)]
    g_line = [g] + [over_z(g, k) for k in range(1, n_z)]

    vec, bias = local_call(
        "vectors",
        vector_body,
        places,
        near_w,
        [((8, width), F32), ((8, three), F32)],
        [pltpu.VMEM((GROUPS, EXTRA, three), F32)],
    )
    cos_tab, sin_tab = rotary_tables(rows, n_ctx)
    fi, w, q, k, v, ag, ow, g_half, cos, sin = local_call(
        "qkv",
        qkv_body,
        places,
        [*x_plane, *g_plane, *near_w, *far_w, vec, bias, out_near, out_far, cos_tab, sin_tab],
        [
            ((near_rows, width), BF16),
            ((width, three), BF16),
            ((near_rows, GROUP_COLS), BF16),
            ((near_rows, GROUP_COLS), BF16),
            ((near_rows, GROUP_COLS), BF16),
            ((near_rows, GROUP_COLS), BF16),
            ((GROUP_COLS, width), BF16),
            ((near_rows, width), BF16),
            ((near_rows, 128), F32),
            ((near_rows, 128), F32),
        ],
        flops=2 * near_rows * width * 4 * GROUP_COLS,
    )
    k_far, v_far = over_ctx(k, 1), over_ctx(v, 1)
    att_outs = local_call(
        "attend",
        attend_body,
        places,
        [q, k, v, k_far, v_far, ag, g_half, ow],
        [((rows, width), F32)]
        + [((rows, width), BF16)] * 3
        + [
            ((part, width), F32),
            ((part, width), BF16),
            ((near_rows, 2 * GROUP_COLS), F32),
            ((near_rows, GROUP_COLS), F32),
            ((near_rows, 2 * GROUP_COLS), BF16),
        ],
        [
            pltpu.VMEM((2 * near_rows, GROUP_COLS), BF16),
            pltpu.VMEM((2 * near_rows, GROUP_COLS), BF16),
            pltpu.VMEM((near_rows, GROUP_COLS), BF16),
            pltpu.VMEM((GROUP_COLS, width), F32),
        ],
        flops=2 * 7 * 256 * GROUP_HEADS * near_rows * 2 * near_rows,
    )
    batt, (dw_keep, dw_send, dkq, dv, far_dkv) = att_outs[:4], att_outs[4:]
    far_dkv = over_ctx(far_dkv, 1)
    branch_att = [batt[0]] + [over_ctx(batt[j], 2 * j) for j in range(1, GROUPS)]

    ffn_outs = local_call(
        "ffn",
        ffn_body,
        places,
        [*x_line, *g_line, up_weight, down_weight, up_bias.reshape(1, -1), vec],
        ([((rows, width), F32)] + [((rows, width), BF16)] * 3) * 2
        + [
            ((GROUPS, (width + hid) // n_ctx, width), F32),
            ((GROUPS, (width + hid) // n_ctx, width), BF16),
            ((8, width), F32),
        ],
        [
            pltpu.VMEM((near_rows, width), BF16),
            pltpu.VMEM((near_rows, width), BF16),
            pltpu.VMEM((near_rows, hid), BF16),
            pltpu.VMEM((near_rows, hid), BF16),
            pltpu.VMEM((near_rows, width), F32),
            pltpu.VMEM((width + hid, width), F32),
        ],
        flops=2 * 6 * near_rows * width * hid,
    )
    ffn_out, ffn_ca, (ffn_keep, ffn_send, ffn_sums) = ffn_outs[:4], ffn_outs[4:8], ffn_outs[8:]
    branch_ffn = [ffn_out[0]] + [over_z(ffn_out[k], k) for k in range(1, n_z)]
    second = [ffn_ca[0]] + [over_z(ffn_ca[k], k) for k in range(1, n_z)]

    chunk = (width + hid) // n_ctx
    own, *sends = local_call(
        "ffn_pair",
        split_sum_body,
        places,
        [ffn_keep, over_ctx(ffn_send, 1)],
        [((chunk, width), F32)] + [((chunk, width), BF16)] * 3,
    )
    (total,) = local_call(
        "ffn_sum",
        sum_body,
        places,
        [own] + [over_ctx(sends[j - 1], 2 * j) for j in range(1, GROUPS)],
        [((chunk, width), BF16)],
    )
    near = chips(total)
    up_dw, down_dw = local_call(
        "ffn_spread",
        spread_body,
        places,
        near + [over_ctx(p, 1) for p in near],
        [((width, hid), F32), ((hid, width), F32)],
        [pltpu.VMEM((width + hid, width), F32)],
    )

    joined_outs = local_call(
        "joined",
        joined_body,
        places,
        [dkq, dv, far_dkv, w, fi, cos, sin, vec, ffn_sums, *x_plane, g],
        [((rows, width), F32)]
        + [((rows, width), BF16)] * 3
        + [((n_z, part + EXTRA, three), F32), ((n_z, part + EXTRA, three), BF16)],
        [
            pltpu.VMEM((near_rows, 2 * GROUP_COLS), BF16),
            pltpu.VMEM((near_rows, GROUP_COLS), BF16),
            pltpu.VMEM((width, three), F32),
            pltpu.VMEM((near_rows, width), F32),
            pltpu.VMEM((GROUPS, EXTRA, three), F32),
        ],
        flops=2 * 2 * near_rows * width * three,
    )
    ca, (keep, send) = joined_outs[:4], joined_outs[4:]
    first = [ca[0]] + [over_ctx(ca[j], 2 * j) for j in range(1, GROUPS)]
    own, *sends = local_call(
        "qkv_pair",
        split_sum_body,
        places,
        [keep, over_ctx(send, 1)],
        [((part + EXTRA, three), F32)] + [((part + EXTRA, three), BF16)] * 3,
    )
    (total,) = local_call(
        "qkv_sum",
        sum_body,
        places,
        [own] + [over_z(sends[k - 1], k) for k in range(1, n_z)],
        [((part + EXTRA, three), BF16)],
    )
    near = chips(total)
    qkv_dw, sums, qkv_db, up_db = local_call(
        "qkv_finish",
        finish_body,
        places,
        near + [over_ctx(p, 1) for p in near],
        [((shard, 3 * width), F32), ((8, shard), F32), ((1, three), F32), ((1, hid), F32)],
        [pltpu.VMEM((GROUPS, shard, three), F32), pltpu.VMEM((GROUPS, EXTRA, three), F32)],
    )

    mine = (dw_keep + over_ctx(dw_send, 1).astype(F32)).astype(BF16)
    got = [
        over_both(mine, [(a, (a // 2) ^ k, a, a // 2) for a in range(n_ctx)]) for k in range(1, n_z)
    ]
    mine = sum((p.astype(F32) for p in got), mine.astype(F32)).astype(BF16)
    got = [
        over_both(mine, [(a, a // 2, a ^ (2 * j), a // 2) for a in range(n_ctx)])
        for j in range(1, GROUPS)
    ]
    out_near = jnp.where(z == group, mine, got[0] + got[1] + got[2])
    out_far = over_ctx(out_near, 1)
    out_dw = jnp.where(
        core == 0,
        jnp.concatenate([out_near, out_far], axis=0),
        jnp.concatenate([out_far, out_near], axis=0),
    ).astype(F32)

    layer_out, input_grad = local_call(
        "token",
        token_body,
        places,
        [x, g, vec, *branch_att, *branch_ffn, *first, *second],
        [((rows, width), BF16), ((rows, width), F32)],
    )
    return (
        layer_out.reshape(tokens.shape),
        input_grad.reshape(tokens.shape),
        sums[0],
        sums[1],
        sums[3],
        sums[4],
        qkv_dw,
        qkv_db[0],
        out_dw,
        sums[2],
        up_dw,
        up_db[0],
        down_dw,
        sums[2],
    )


def solution(mesh):
    in_specs = (
        P("fsdp", "ctx", None),
        P("fsdp", "ctx", None),
        P("fsdp"),
        P("fsdp"),
        P("fsdp"),
        P("fsdp"),
        P("fsdp", None),
        P("fsdp"),
        P("fsdp", None),
        P("fsdp"),
        P(None, "fsdp"),
        P("fsdp"),
        P("fsdp", None),
        P("fsdp"),
    )
    out_specs = (
        P("fsdp", "ctx", None),
        P("fsdp", "ctx", None),
        P("fsdp"),
        P("fsdp"),
        P("fsdp"),
        P("fsdp"),
        P("fsdp", None),
        P("fsdp"),
        P("fsdp", None),
        P("fsdp"),
        P(None, "fsdp"),
        P("fsdp"),
        P("fsdp", None),
        P("fsdp"),
    )
    per_device = block_shards if fits(mesh) else shards
    return jax.shard_map(per_device, mesh=mesh, in_specs=in_specs, out_specs=out_specs, check_vma=False)
```

```python
import math

import jax
import jax.numpy as jnp
from jax import lax
from jax.experimental import pallas as pl
from jax.experimental.pallas import tpu as pltpu
from jax.sharding import PartitionSpec as P
import numpy as np

HEADS = 12
HEAD_DIM = 64
ROT_DIMS = 16


def layer_norm(values, norm_gain, norm_shift):
    center = values - jnp.mean(values, axis=-1, keepdims=True)
    spread = jnp.mean(center * center, axis=-1, keepdims=True)
    return center * lax.rsqrt(spread + 1e-05) * norm_gain + norm_shift


def exact_gelu(values):
    return jax.nn.gelu(values, approximate=False)


def stored_positions(rows, devices):
    row_order = jnp.arange(rows * devices, dtype=jnp.int32)
    device = row_order // rows
    within = row_order % rows
    half_rows = rows // 2
    return jnp.where(
        within < half_rows,
        device * half_rows + within,
        (2 * devices - 1 - device) * half_rows + within - half_rows,
    )


def rotary_angles(positions):
    half_rot = ROT_DIMS // 2
    inverse = jnp.power(10000.0, -2.0 * jnp.arange(half_rot, dtype=jnp.float32) / ROT_DIMS)
    return positions.astype(jnp.float32)[:, None] * inverse[None, :]


def rotate(heads, angles):
    half_rot = ROT_DIMS // 2
    cosine = jnp.cos(angles)[:, None, :]
    sine_part = jnp.sin(angles)[:, None, :]
    lower_half = heads[..., :half_rot]
    upper_half = heads[..., half_rot:ROT_DIMS]
    return jnp.concatenate(
        [
            lower_half * cosine - upper_half * sine_part,
            upper_half * cosine + lower_half * sine_part,
            heads[..., ROT_DIMS:],
        ],
        axis=-1,
    )


def to_order(stack, ctx_count, half_rows):
    tail = stack.shape[1:]
    shaped = stack.reshape((ctx_count, 2, half_rows) + tail)
    return jnp.concatenate(
        [shaped[:, 0].reshape((-1,) + tail), shaped[::-1, 1].reshape((-1,) + tail)], axis=0
    )


def from_order(stack, ctx_count, half_rows):
    tail = stack.shape[1:]
    middle = stack.shape[0] // 2
    first = stack[:middle].reshape((ctx_count, half_rows) + tail)
    second = stack[middle:].reshape((ctx_count, half_rows) + tail)[::-1]
    return jnp.stack([first, second], axis=1).reshape(stack.shape)


def scores_block(query_heads, key_heads, query_pos, key_pos):
    scores = jnp.einsum(
        "qhd,khd->hqk", query_heads, key_heads, preferred_element_type=jnp.float32
    ) / math.sqrt(HEAD_DIM)
    return jnp.where(key_pos[None, None, :] <= query_pos[None, :, None], scores, -1000000000.0)


def grad_block(
    query_heads, grad_heads, log_total, inner, query_pos, key_heads, value_heads, key_pos
):
    scores = scores_block(query_heads, key_heads, query_pos, key_pos)
    probability = jnp.exp(scores - log_total[:, :, None])
    prob_grad = jnp.einsum(
        "qhd,khd->hqk", grad_heads, value_heads, preferred_element_type=jnp.float32
    )
    score_grad = (probability * (prob_grad - inner[:, :, None])).astype(jnp.bfloat16)
    return (probability.astype(jnp.bfloat16), score_grad)


def shards(
    tokens,
    cotangent,
    att_gain,
    att_shift,
    ffn_gain,
    ffn_shift,
    qkv_weight,
    qkv_bias,
    out_weight,
    out_bias,
    up_weight,
    up_bias,
    down_weight,
    down_bias,
):
    model_width = tokens.shape[-1]
    rows_in = tokens.reshape(-1, model_width)
    grad_rows = cotangent.reshape(-1, model_width)
    own_rows = rows_in.shape[0]
    half_rows = own_rows // 2
    ctx_count = lax.axis_size("ctx")
    ctx_place = lax.axis_index("ctx")
    total_rows = own_rows * ctx_count
    all_pos = stored_positions(own_rows, ctx_count)
    own_pos = lax.dynamic_slice_in_dim(all_pos, ctx_place * own_rows, own_rows, 0)
    (
        gain_attend,
        shift_attend,
        gain_feed,
        shift_feed,
        mat_qkv,
        bias_qkv,
        mat_out,
        bias_out,
        bias_down,
    ) = (
        lax.all_gather(att_gain, "fsdp", axis=0, tiled=True),
        lax.all_gather(att_shift, "fsdp", axis=0, tiled=True),
        lax.all_gather(ffn_gain, "fsdp", axis=0, tiled=True),
        lax.all_gather(ffn_shift, "fsdp", axis=0, tiled=True),
        lax.all_gather(qkv_weight, "fsdp", axis=0, tiled=True),
        lax.all_gather(qkv_bias, "fsdp", axis=0, tiled=True),
        lax.all_gather(out_weight, "fsdp", axis=0, tiled=True),
        lax.all_gather(out_bias, "fsdp", axis=0, tiled=True),
        lax.all_gather(down_bias, "fsdp", axis=0, tiled=True),
    )
    tokens32 = rows_in.astype(jnp.float32)
    grad32 = grad_rows.astype(jnp.float32)
    first_norm, first_back = jax.vjp(
        layer_norm, tokens32, gain_attend.astype(jnp.float32), shift_attend.astype(jnp.float32)
    )
    second_norm, second_back = jax.vjp(
        layer_norm, tokens32, gain_feed.astype(jnp.float32), shift_feed.astype(jnp.float32)
    )
    first_in = first_norm.astype(jnp.bfloat16)
    second_in = second_norm.astype(jnp.bfloat16)
    joined = jnp.dot(first_in, mat_qkv, preferred_element_type=jnp.float32) + bias_qkv.astype(
        jnp.float32
    )
    angles = rotary_angles(own_pos)

    def project_heads(joined_rows):
        queries = rotate(joined_rows[:, :model_width].reshape(own_rows, HEADS, HEAD_DIM), angles)
        keys_rot = rotate(
            joined_rows[:, model_width : 2 * model_width].reshape(own_rows, HEADS, HEAD_DIM), angles
        )
        return (
            queries.reshape(own_rows, model_width),
            keys_rot.reshape(own_rows, model_width),
            joined_rows[:, 2 * model_width :],
        )

    (queries, keys_rot, values_rows), rotary_back = jax.vjp(project_heads, joined)
    query_low = queries.astype(jnp.bfloat16)
    key_low = keys_rot.astype(jnp.bfloat16)
    value_low = values_rows.astype(jnp.bfloat16)
    key_all, value_all = (
        lax.all_gather(key_low, "ctx", axis=0, tiled=True),
        lax.all_gather(value_low, "ctx", axis=0, tiled=True),
    )
    query_heads = query_low.reshape(own_rows, HEADS, HEAD_DIM)
    key_heads = to_order(key_all, ctx_count, half_rows).reshape(total_rows, HEADS, HEAD_DIM)
    value_heads = to_order(value_all, ctx_count, half_rows).reshape(total_rows, HEADS, HEAD_DIM)
    block_keys = min(1024, total_rows)

    def key_piece(block_index):
        start = block_index * block_keys
        return (
            lax.dynamic_slice_in_dim(key_heads, start, block_keys, 0),
            lax.dynamic_slice_in_dim(value_heads, start, block_keys, 0),
            start + jnp.arange(block_keys, dtype=jnp.int32),
        )

    need_low = (ctx_place + 1) * half_rows
    need_high = (2 * ctx_count - ctx_place) * half_rows
    counts = ((need_low + block_keys - 1) // block_keys, (need_high + block_keys - 1) // block_keys)
    query_parts = (query_heads[:half_rows], query_heads[half_rows:])
    pos_parts = (own_pos[:half_rows], own_pos[half_rows:])

    def half_lse(query_half, pos_half, count):

        def lse_step(block_index, carried):
            row_top, exp_total = carried
            key_block, value_skip, key_pos = key_piece(block_index)
            scores = scores_block(query_half, key_block, pos_half, key_pos)
            new_top = jnp.maximum(row_top, jnp.max(scores, axis=-1))
            exp_total = exp_total * jnp.exp(row_top - new_top) + jnp.sum(
                jnp.exp(scores - new_top[:, :, None]), axis=-1
            )
            return (new_top, exp_total)

        start_top = jnp.full((HEADS, half_rows), -1e30, jnp.float32)
        start_sum = jnp.zeros((HEADS, half_rows), jnp.float32)
        row_top, exp_total = lax.fori_loop(0, count, lse_step, (start_top, start_sum))
        return row_top + jnp.log(exp_total)

    lse_parts = [
        half_lse(query_parts[half_index], pos_parts[half_index], counts[half_index])
        for half_index in range(2)
    ]

    def half_mix(query_half, pos_half, lse_half, count):

        def mix_step(block_index, totals):
            key_block, value_block, key_pos = key_piece(block_index)
            scores = scores_block(query_half, key_block, pos_half, key_pos)
            probability = jnp.exp(scores - lse_half[:, :, None]).astype(jnp.bfloat16)
            return totals + jnp.einsum(
                "hqk,khd->qhd", probability, value_block, preferred_element_type=jnp.float32
            )

        return lax.fori_loop(
            0, count, mix_step, jnp.zeros((half_rows, HEADS, HEAD_DIM), jnp.float32)
        )

    attended = jnp.concatenate(
        [
            half_mix(
                query_parts[half_index],
                pos_parts[half_index],
                lse_parts[half_index],
                counts[half_index],
            )
            for half_index in range(2)
        ],
        axis=0,
    )
    attended_low = attended.reshape(own_rows, model_width).astype(jnp.bfloat16)
    branch_att = jnp.dot(
        attended_low, mat_out, preferred_element_type=jnp.float32
    ) + bias_out.astype(jnp.float32)
    second_all, grad_all = (
        lax.all_gather(second_in, "fsdp", axis=0, tiled=True),
        lax.all_gather(grad_rows, "fsdp", axis=0, tiled=True),
    )
    hidden = jnp.dot(second_all, up_weight, preferred_element_type=jnp.float32) + up_bias.astype(
        jnp.float32
    )
    active, gelu_back = jax.vjp(exact_gelu, hidden)
    active_low = active.astype(jnp.bfloat16)
    ffn_part = jnp.dot(active_low, down_weight, preferred_element_type=jnp.float32)
    active_grad = jnp.einsum("te,fe->tf", grad_all, down_weight, preferred_element_type=jnp.float32)
    hidden_grad = gelu_back(active_grad)[0].astype(jnp.bfloat16)
    down_dweight = jnp.einsum("tf,te->fe", active_low, grad_all, preferred_element_type=jnp.float32)
    up_dweight = jnp.einsum(
        "td,tf->df", second_all, hidden_grad, preferred_element_type=jnp.float32
    )
    up_dbias = jnp.sum(hidden_grad.astype(jnp.float32), axis=0)
    second_part = jnp.einsum(
        "tf,df->td", hidden_grad, up_weight, preferred_element_type=jnp.float32
    )
    ffn_sum, second_grad = (
        lax.psum_scatter(ffn_part, "fsdp", scatter_dimension=0, tiled=True),
        lax.psum_scatter(second_part, "fsdp", scatter_dimension=0, tiled=True),
    )
    branch_ffn = ffn_sum + bias_down.astype(jnp.float32)
    layer_out = (tokens32 + branch_att + branch_ffn).astype(jnp.bfloat16).reshape(tokens.shape)
    out_dweight = jnp.einsum(
        "td,te->de", attended_low, grad_rows, preferred_element_type=jnp.float32
    )
    row_sum = jnp.sum(grad32, axis=0)
    attended_grad = jnp.einsum(
        "te,de->td", grad_rows, mat_out, preferred_element_type=jnp.float32
    ).astype(jnp.bfloat16)
    grad_heads = attended_grad.reshape(own_rows, HEADS, HEAD_DIM)
    grad_parts = (grad_heads[:half_rows], grad_heads[half_rows:])

    def half_inner(query_half, grad_half, pos_half, lse_half, count):

        def inner_step(block_index, totals):
            key_block, value_block, key_pos = key_piece(block_index)
            scores = scores_block(query_half, key_block, pos_half, key_pos)
            probability = jnp.exp(scores - lse_half[:, :, None])
            prob_grad = jnp.einsum(
                "qhd,khd->hqk", grad_half, value_block, preferred_element_type=jnp.float32
            )
            return totals + jnp.sum(probability * prob_grad, axis=-1)

        return lax.fori_loop(0, count, inner_step, jnp.zeros((HEADS, half_rows), jnp.float32))

    inner_parts = [
        half_inner(
            query_parts[half_index],
            grad_parts[half_index],
            pos_parts[half_index],
            lse_parts[half_index],
            counts[half_index],
        )
        for half_index in range(2)
    ]
    half_zeros = jnp.zeros((half_rows, HEADS, HEAD_DIM), jnp.float32)

    def half_back(half_index, carried):
        query_half = query_parts[half_index]
        grad_half = grad_parts[half_index]

        def query_step(block_index, state):
            query_total, key_acc, value_acc = state
            key_block, value_block, key_pos = key_piece(block_index)
            prob_low, score_grad = grad_block(
                query_half,
                grad_half,
                lse_parts[half_index],
                inner_parts[half_index],
                pos_parts[half_index],
                key_block,
                value_block,
                key_pos,
            )
            key_part = jnp.einsum(
                "hqk,qhd->khd", score_grad, query_half, preferred_element_type=jnp.float32
            )
            value_part = jnp.einsum(
                "hqk,qhd->khd", prob_low, grad_half, preferred_element_type=jnp.float32
            )
            start = block_index * block_keys
            key_acc = lax.dynamic_update_slice_in_dim(
                key_acc,
                lax.dynamic_slice_in_dim(key_acc, start, block_keys, 0) + key_part,
                start,
                0,
            )
            value_acc = lax.dynamic_update_slice_in_dim(
                value_acc,
                lax.dynamic_slice_in_dim(value_acc, start, block_keys, 0) + value_part,
                start,
                0,
            )
            query_total = query_total + jnp.einsum(
                "hqk,khd->qhd", score_grad, key_block, preferred_element_type=jnp.float32
            )
            return (query_total, key_acc, value_acc)

        return lax.fori_loop(0, counts[half_index], query_step, carried)

    full_zeros = jnp.zeros((total_rows, HEADS, HEAD_DIM), jnp.float32)
    query_low_sum, key_acc, value_acc = half_back(0, (half_zeros, full_zeros, full_zeros))
    query_high_sum, key_acc, value_acc = half_back(1, (half_zeros, key_acc, value_acc))
    query_sum = jnp.concatenate([query_low_sum, query_high_sum], axis=0)
    key_stored = from_order(key_acc.reshape(total_rows, model_width), ctx_count, half_rows)
    value_stored = from_order(value_acc.reshape(total_rows, model_width), ctx_count, half_rows)
    key_sum, value_sum = (
        lax.psum_scatter(key_stored, "ctx", scatter_dimension=0, tiled=True),
        lax.psum_scatter(value_stored, "ctx", scatter_dimension=0, tiled=True),
    )
    query_grad = query_sum.reshape(own_rows, model_width) / math.sqrt(HEAD_DIM)
    key_grad = key_sum / math.sqrt(HEAD_DIM)
    joined_grad = rotary_back((query_grad, key_grad, value_sum))[0].astype(jnp.bfloat16)
    qkv_dweight = jnp.einsum("td,tf->df", first_in, joined_grad, preferred_element_type=jnp.float32)
    qkv_dbias = jnp.sum(joined_grad.astype(jnp.float32), axis=0)
    first_grad = jnp.einsum("tf,df->td", joined_grad, mat_qkv, preferred_element_type=jnp.float32)
    token_first, att_dgain, att_dshift = first_back(first_grad)
    token_second, ffn_dgain, ffn_dshift = second_back(second_grad)
    input_grad = (grad32 + token_first + token_second).reshape(tokens.shape)
    shares = (
        lax.psum_scatter(att_dgain, "fsdp", scatter_dimension=0, tiled=True),
        lax.psum_scatter(att_dshift, "fsdp", scatter_dimension=0, tiled=True),
        lax.psum_scatter(ffn_dgain, "fsdp", scatter_dimension=0, tiled=True),
        lax.psum_scatter(ffn_dshift, "fsdp", scatter_dimension=0, tiled=True),
        lax.psum_scatter(qkv_dweight, "fsdp", scatter_dimension=0, tiled=True),
        lax.psum_scatter(qkv_dbias, "fsdp", scatter_dimension=0, tiled=True),
        lax.psum_scatter(out_dweight, "fsdp", scatter_dimension=0, tiled=True),
        lax.psum_scatter(row_sum, "fsdp", scatter_dimension=0, tiled=True),
    ) + (up_dweight, up_dbias, down_dweight)
    totals = lax.psum(
        (
            shares[0],
            shares[1],
            shares[2],
            shares[3],
            shares[4],
            shares[5],
            shares[6],
            shares[7],
            shares[8],
            shares[9],
            shares[10],
        ),
        "ctx",
    )
    return (
        layer_out,
        input_grad,
        totals[0],
        totals[1],
        totals[2],
        totals[3],
        totals[4],
        totals[5],
        totals[6],
        totals[7],
        totals[8],
        totals[9],
        totals[10],
        totals[7],
    )


F32 = jnp.float32
BF16 = jnp.bfloat16
GROUPS = 4
GROUP_HEADS = HEADS // GROUPS
GROUP_COLS = GROUP_HEADS * HEAD_DIM
EXTRA = 16


def fits(mesh):
    return mesh.shape["ctx"] == 2 * GROUPS and mesh.shape["fsdp"] == GROUPS


def mm(left, right):
    return jnp.dot(left, right, preferred_element_type=F32)


def mm_nt(left, right):
    return lax.dot_general(left, right, (((1,), (1,)), ((), ())), preferred_element_type=F32)


def mm_tn(left, right):
    return lax.dot_general(left, right, (((0,), (0,)), ((), ())), preferred_element_type=F32)


def local_call(
    name, body, places, ins, outs, scratch=(), flops=0, whole=(), after=(), through=(), vmem=28
):
    waits = len(after) + len(through)
    inner, first, last = body, 1 + waits, 1 + waits + len(ins) + len(whole)

    def body(*refs):
        given = refs[first:last]
        given = given[len(whole) :][::-1] + given[: len(whole)][::-1]
        made = refs[last : last + len(outs)]
        inner(refs[0], *given, *made, *refs[last + len(outs) + len(through) :])

    moved = sum(math.prod(i.shape) * i.dtype.itemsize for i in ins)
    moved += sum(math.prod(s) * jnp.dtype(d).itemsize for s, d in outs)
    return pl.pallas_call(
        body,
        out_shape=[jax.ShapeDtypeStruct(s, d) for s, d in outs]
        + [jax.ShapeDtypeStruct(t.shape, t.dtype) for t in through],
        in_specs=[pl.BlockSpec(memory_space=pltpu.SMEM)]
        + [pl.BlockSpec(memory_space=pl.ANY)] * (waits + len(whole))
        + [pl.BlockSpec(memory_space=pltpu.VMEM)] * len(ins),
        out_specs=[pl.BlockSpec(memory_space=pltpu.VMEM)] * len(outs)
        + [pl.BlockSpec(memory_space=pl.ANY)] * len(through),
        input_output_aliases={1 + len(after) + i: len(outs) + i for i in range(len(through))},
        scratch_shapes=list(scratch),
        compiler_params=pltpu.CompilerParams(vmem_limit_bytes=vmem * 2**20),
        cost_estimate=pl.CostEstimate(flops=flops, bytes_accessed=moved, transcendentals=0),
        name=name,
    )(places, *after, *through, *whole[::-1], *ins[::-1])


def normed(values):
    center = values - jnp.mean(values, axis=-1, keepdims=True)
    spread = jnp.mean(center * center, axis=-1, keepdims=True)
    scale = lax.rsqrt(spread + 1e-05)
    return center * scale, scale


def rotary_tables(rows, devices):
    half = rows // 2
    order = np.arange(rows * devices)
    device, within = order // rows, order % rows
    position = np.where(
        within < half, device * half + within, (2 * devices - 1 - device) * half + within - half
    )
    pairs = ROT_DIMS // 2
    inverse = np.power(10000.0, -2.0 * np.arange(pairs) / ROT_DIMS).astype(np.float32)
    angle = (position.astype(np.float32)[:, None] * inverse[None, :]).astype(np.float32)
    cosine = np.ones((rows * devices, HEAD_DIM), np.float32)
    sine = np.zeros((rows * devices, HEAD_DIM), np.float32)
    cosine[:, :pairs] = cosine[:, pairs:ROT_DIMS] = np.cos(angle)
    sine[:, :pairs] = -np.sin(angle)
    sine[:, pairs:ROT_DIMS] = np.sin(angle)
    return np.tile(cosine, (1, 2)), np.tile(sine, (1, 2))


def swapped(values):
    lanes = values.shape[1]
    place = lax.broadcasted_iota(jnp.int32, values.shape, 1) % HEAD_DIM
    return jnp.where(
        place < ROT_DIMS // 2,
        pltpu.roll(values, lanes - ROT_DIMS // 2, 1),
        pltpu.roll(values, ROT_DIMS // 2, 1),
    )


def pack_body(places, *refs):
    vectors, (qkv_w, x, g, out_w) = refs[0:7], refs[7:11]
    payload, xg, xg_line, out_half, box, rows_w, sems = refs[11:]
    core, group = places[0] % 2, places[0] // 2
    part = rows_w.shape[0]
    width = xg.shape[1]
    rows = x.shape[0]
    copies = [
        pltpu.make_async_copy(
            qkv_w.at[pl.ds(pl.multiple_of(core * part, part), part), :], rows_w, sems.at[0]
        ),
        pltpu.make_async_copy(x, xg.at[pl.ds(0, rows), :], sems.at[1]),
        pltpu.make_async_copy(g, xg.at[pl.ds(rows, rows), :], sems.at[2]),
        pltpu.make_async_copy(
            out_w.at[pl.ds(pl.multiple_of(core * part, part), part), :], out_half, sems.at[3]
        ),
        pltpu.make_async_copy(x, xg_line.at[pl.ds(0, rows), :], sems.at[4]),
        pltpu.make_async_copy(g, xg_line.at[pl.ds(rows, rows), :], sems.at[5]),
    ]
    for copy in copies:
        copy.start()
    box[...] = jnp.zeros_like(box)
    shard = vectors[0].shape[0]
    for item in range(6):
        box[item // 3 : item // 3 + 1, (item % 3) * shard : (item % 3 + 1) * shard] = (
            vectors[item][...].astype(F32).reshape(1, shard)
        )
    box[2:3, :] = vectors[6][...].astype(F32).reshape(1, 3 * shard)
    payload[part:, :] = box[...].astype(BF16)
    copies[0].wait()
    for owner in range(GROUPS):

        @pl.when(group == owner)
        def _():
            for slot, base in enumerate((1, 0, 2)):
                at = base * width + owner * GROUP_COLS
                payload[0:part, slot * GROUP_COLS : (slot + 1) * GROUP_COLS] = rows_w[
                    :, at : at + GROUP_COLS
                ]

    for copy in copies[1:]:
        copy.wait()


def collect_body(places, p0, p1, p2, p3, stack, vec, bias, box):
    z, group = places[1], places[0] // 2
    part = p0.shape[0] - EXTRA
    three = p0.shape[1]
    shard = vec.shape[1] // GROUPS
    for k, piece in enumerate((p0, p1, p2, p3)):
        stack[k * part : (k + 1) * part, :] = piece[0:part, :]
        box[z ^ k] = piece[part:, :].astype(F32)
    units = []
    for owner in range(GROUPS):
        block = box[owner]
        for item in range(6):
            vec[item : item + 1, owner * shard : (owner + 1) * shard] = block[
                item // 3 : item // 3 + 1, (item % 3) * shard : (item % 3 + 1) * shard
            ]
        for unit in range(3):
            units.append(block[2:3, unit * GROUP_COLS : (unit + 1) * GROUP_COLS])
    for slot, base in enumerate((GROUPS, 0, 2 * GROUPS)):
        own = units[base]
        for g in range(1, GROUPS):
            own = jnp.where(group == g, units[base + g], own)
        bias[0:1, slot * GROUP_COLS : (slot + 1) * GROUP_COLS] = own


def qkv_body(places, *refs):
    xs, (near, far, vec, bias, cos_tab, sin_tab) = refs[0:4], refs[4:10]
    fi, w, q_out, kv_out, cos, sin = refs[10:]
    c, z = places[0], places[1]
    core = c % 2
    width = w.shape[0]
    shard = width // GROUPS
    part = shard // 2
    rows = xs[0].shape[0] // 2
    half = rows // 2
    near_rows = GROUPS * rows
    for side, stack in ((core, near), (1 - core, far)):
        for k in range(GROUPS):
            base = (z ^ k) * shard + side * part
            w[pl.ds(pl.multiple_of(base, part), part), :] = stack[k * part : (k + 1) * part, :]
    gain, shift = vec[0:1, :], vec[1:2, :]
    two = 2 * GROUP_COLS
    for side in range(2):
        for j in range(GROUPS):
            source = c ^ (2 * j)
            to = slice((side * GROUPS + j) * half, (side * GROUPS + j + 1) * half)
            at = pl.ds(pl.multiple_of(source * rows + side * half, half), half)
            norm, _ = normed(xs[j][side * half : (side + 1) * half, :].astype(F32))
            fi[to, :] = (norm * gain + shift).astype(BF16)
            cos[to, :] = cos_tab[at, :]
            sin[to, :] = sin_tab[at, :]
    step = 2 * rows
    for i in range(near_rows // step):
        at = slice(i * step, (i + 1) * step)
        chunk = fi[at, :]
        kq = mm(chunk, w[:, :two]) + bias[0:1, :two]
        c3 = jnp.concatenate([cos[at, :]] * 3, axis=1)
        s3 = jnp.concatenate([sin[at, :]] * 3, axis=1)
        kq = kq * c3 + swapped(kq) * s3
        kv_out[at, :] = kq[:, :GROUP_COLS].astype(BF16)
        q_out[at, :] = (kq[:, GROUP_COLS:] * HEAD_DIM**-0.5).astype(BF16)
        kv_out[near_rows + i * step : near_rows + (i + 1) * step, :] = (
            mm(chunk, w[:, two:]) + bias[0:1, two:]
        ).astype(BF16)


def key_order(kv, kv_far, kbuf, vbuf, low):
    near_rows = 2 * low
    for side in range(2):
        for part, source in enumerate((kv, kv_far)):
            to = slice((2 * side + part) * low, (2 * side + part + 1) * low)
            kbuf[to, :] = source[side * low : (side + 1) * low, :]
            vbuf[to, :] = source[near_rows + side * low : near_rows + (side + 1) * low, :]


def visible(c, low):
    half = low // GROUPS
    devices = 2 * GROUPS

    def token_pos(index, far):
        device = (c ^ (2 * (index // half))) ^ far
        return device * half + index % half

    q_place = token_pos(lax.broadcasted_iota(jnp.int32, (low, 1), 0), 0)
    k_index = lax.broadcasted_iota(jnp.int32, (1, 2 * low), 1)
    k_place = token_pos(k_index % low, k_index // low)

    def mirrored(place):
        return (2 * devices - 1 - place // half) * half + place % half

    return (k_place <= q_place, mirrored(k_place) <= mirrored(q_place))


def masked_scores(query, keys, side, spans, allowed):
    scores = [mm_nt(query, keys[s]) for s in spans]
    scores[-1] = jnp.where(allowed[side], scores[-1], -1000000000.0)
    return scores


def key_spans(side, low):
    return [slice(0, 2 * low), slice(2 * low, 4 * low)][: side + 1]


def attend_body(places, *refs):
    q, kv, kv_far = refs[0:3]
    xgs, (ow_near, ow_far) = refs[3:7], refs[7:9]
    sends, (dkq, dv_out, far_out) = refs[9:13], refs[13:16]
    kbuf, vbuf, att, ag, ow, g_half, pieces = refs[16:]
    c, z = places[0], places[1]
    core = c % 2
    rows = sends[0].shape[0]
    near_rows = GROUPS * rows
    half = rows // 2
    low = GROUPS * half
    part = GROUP_COLS // 2
    key_order(kv, kv_far, kbuf, vbuf, low)
    ow[pl.ds(pl.multiple_of(core * part, part), part), :] = ow_near[...]
    ow[pl.ds(pl.multiple_of((1 - core) * part, part), part), :] = ow_far[...]
    for side in range(2):
        for j in range(GROUPS):
            g_half[(side * GROUPS + j) * half : (side * GROUPS + j + 1) * half, :] = xgs[j][
                rows + side * half : rows + (side + 1) * half, :
            ]
    ag[...] = mm_nt(g_half[...], ow[...]).astype(BF16)
    allowed = visible(c, low)
    for head in range(GROUP_HEADS):
        lanes = slice(head * HEAD_DIM, (head + 1) * HEAD_DIM)
        lanes2 = slice(GROUP_COLS + head * HEAD_DIM, GROUP_COLS + (head + 1) * HEAD_DIM)
        kh, vh = kbuf[:, lanes], vbuf[:, lanes]
        dk_parts, dv_parts = [], []
        for side in range(2):
            at = slice(side * low, (side + 1) * low)
            qh, gh = q[at, lanes], ag[at, lanes]
            spans = [slice(0, 2 * low), slice(2 * low, 4 * low)][: side + 1]
            scores = [mm_nt(qh, kh[s]) for s in spans]
            scores[-1] = jnp.where(allowed[side], scores[-1], -1000000000.0)
            top = jnp.max(scores[0], axis=-1, keepdims=True)
            for s in scores[1:]:
                top = jnp.maximum(top, jnp.max(s, axis=-1, keepdims=True))
            raised = [jnp.exp(s - top) for s in scores]
            inverse = 1.0 / sum(jnp.sum(r, axis=-1, keepdims=True) for r in raised)
            probs = [r * inverse for r in raised]
            low_probs = [p.astype(BF16) for p in probs]
            mixed = sum(mm(p, vh[s]) for p, s in zip(low_probs, spans))
            att[at, lanes] = mixed.astype(BF16)
            prob_grads = [mm_nt(gh, vh[s]) for s in spans]
            inner = sum(
                jnp.sum(p * d, axis=-1, keepdims=True) for p, d in zip(probs, prob_grads)
            )
            score_grads = [(p * (d - inner)).astype(BF16) for p, d in zip(probs, prob_grads)]
            dkq[at, lanes2] = sum(mm(s, kh[a]) for s, a in zip(score_grads, spans)) * HEAD_DIM**-0.5
            dk_parts.append([mm_tn(s, qh) for s in score_grads])
            dv_parts.append([mm_tn(p, gh) for p in low_probs])
        dk = (dk_parts[0][0] + dk_parts[1][0], dk_parts[1][1])
        dv = (dv_parts[0][0] + dv_parts[1][0], dv_parts[1][1])
        for side in range(2):
            at = slice(side * low, (side + 1) * low)
            dkq[at, lanes] = dk[side][:low]
            dv_out[at, lanes] = dv[side][:low]
            far_out[at, lanes] = dk[side][low:].astype(BF16)
            far_out[at, lanes2] = dv[side][low:].astype(BF16)
    for side in range(2):
        for j in range(GROUPS):
            pieces[j, side * half : (side + 1) * half, :] = att[
                (side * GROUPS + j) * half : (side * GROUPS + j + 1) * half, :
            ]
    for m in range(GROUPS):
        sends[m][...] = pieces[(c // 2) ^ z ^ m]


def joined_body(places, *refs):
    dkq, dv, far, w, fi, cos, sin, vec = refs[0:8]
    xs, g_own = refs[8:12], refs[12]
    ca, sends, keep, send = refs[13], refs[14:17], refs[17], refs[18]
    jgkq, jgv, dwbuf, first, ext = refs[19:]
    c, z = places[0], places[1]
    core, group = c % 2, c // 2
    rows = ca.shape[0]
    half = rows // 2
    width = w.shape[0]
    shard = width // GROUPS
    part = shard // 2
    two = 2 * GROUP_COLS
    step = 2 * rows
    gain = vec[0:1, :]
    bias_kq = jnp.zeros((1, two), F32)
    bias_v = jnp.zeros((1, GROUP_COLS), F32)
    for i in range(GROUPS * rows // step):
        at = slice(i * step, (i + 1) * step)
        other = far[at, :].astype(F32)
        dk = dkq[at, :GROUP_COLS] + other[:, :GROUP_COLS]
        kq = jnp.concatenate([dk, dkq[at, GROUP_COLS:]], axis=1)
        c3 = jnp.concatenate([cos[at, :]] * 3, axis=1)
        s3 = jnp.concatenate([sin[at, :]] * 3, axis=1)
        low_kq = (kq * c3 - swapped(kq) * s3).astype(BF16)
        low_v = (dv[at, :] + other[:, GROUP_COLS:]).astype(BF16)
        jgkq[at, :] = low_kq
        jgv[at, :] = low_v
        bias_kq += jnp.sum(low_kq.astype(F32), axis=0, keepdims=True)
        bias_v += jnp.sum(low_v.astype(F32), axis=0, keepdims=True)
        first[at, :] = mm_nt(low_kq, w[:, :two]) + mm_nt(low_v, w[:, two:])
    dgain = jnp.zeros((1, width), F32)
    dshift = jnp.zeros((1, width), F32)
    for side in range(2):
        for j in range(GROUPS):
            at = slice((side * GROUPS + j) * half, (side * GROUPS + j + 1) * half)
            mine = slice(side * half, (side + 1) * half)
            norm, _ = normed(xs[j][mine, :].astype(F32))
            grad = first[at, :]
            dgain += jnp.sum(grad * norm, axis=0, keepdims=True)
            dshift += jnp.sum(grad, axis=0, keepdims=True)
            if j == 0:
                ca[mine, :] = grad * gain
            else:
                sends[j - 1][mine, :] = (grad * gain).astype(BF16)
    gsum = jnp.sum(g_own[...].astype(F32), axis=0, keepdims=True)
    dwbuf[:, :two] = mm_tn(fi[...], jgkq[...])
    dwbuf[:, two:] = mm_tn(fi[...], jgv[...])
    ext[...] = jnp.zeros_like(ext)
    for owner in range(GROUPS):
        own = slice(owner * shard, (owner + 1) * shard)
        for slot in range(3):
            unit = owner * 3 + slot
            kind = unit // GROUPS
            vector = (bias_kq[:, GROUP_COLS:], bias_kq[:, :GROUP_COLS], bias_v)[kind]
            to = slice(slot * GROUP_COLS, (slot + 1) * GROUP_COLS)
            ext[owner, 0:1, to] = jnp.where(group == unit % GROUPS, vector, 0.0)
        for slot, vector in enumerate((dgain[:, own], dshift[:, own], gsum[:, own])):
            ext[owner, 1:2, slot * shard : (slot + 1) * shard] = vector
    for k in range(GROUPS):
        owner = z ^ k
        base = owner * shard
        keep[k, 0:part, :] = dwbuf[pl.ds(pl.multiple_of(base + core * part, part), part), :]
        send[k, 0:part, :] = dwbuf[
            pl.ds(pl.multiple_of(base + (1 - core) * part, part), part), :
        ].astype(BF16)
        keep[k, part:, :] = ext[owner].astype(BF16).astype(F32)
        send[k, part:, :] = ext[owner].astype(BF16)


def ffn_pair_body(places, keep, got, own, *sends):
    chunk = own.shape[0]
    for j in range(GROUPS):
        total = keep[j * chunk : (j + 1) * chunk, :] + got[j * chunk : (j + 1) * chunk, :].astype(F32)
        if j == 0:
            own[...] = total
        else:
            sends[j - 1][...] = total.astype(BF16)


def qkv_pair_body(places, keep, got, own, *sends):
    for k in range(GROUPS):
        total = keep[k] + got[k].astype(F32)
        if k == 0:
            own[...] = total
        else:
            sends[k - 1][...] = total.astype(BF16)


def plane_sum_body(places, own, a, b, c, out):
    out[...] = own[...] + a[...].astype(F32) + b[...].astype(F32) + c[...].astype(F32)


def ffn_sum_body(places, own, a, b, c, sums, s1, s2, s3, out):
    rows = own.shape[0]
    total = own[...] + a[...].astype(F32) + b[...].astype(F32) + c[...].astype(F32)
    out[0:rows, :] = total.astype(BF16)
    mine = sums[...].astype(F32)
    line = mine + s1[...].astype(F32) + s2[...].astype(F32) + s3[...].astype(F32)
    row = lax.broadcasted_iota(jnp.int32, mine.shape, 0)
    out[rows:, :] = jnp.where(row < 2, line, mine).astype(BF16)


def sum_body(places, own, a, b, c, out):
    out[...] = (own[...] + a[...].astype(F32) + b[...].astype(F32) + c[...].astype(F32)).astype(
        out.dtype
    )


def ffn_body(places, *refs):
    line = refs[0:7]
    up_w, down_w, up_b, vec, out_w = refs[7:12]
    atts = refs[12:16]
    outs = refs[16:20]
    sums, si, gb, active, hidden_grad, att = refs[20:26]
    second, norms = refs[26:]
    c, z = places[0], places[1]
    rows = line[0].shape[0] // 2
    width = up_w.shape[0]
    hid = up_w.shape[1]
    gain, shift = vec[2:3, :], vec[3:4, :]
    for k in range(GROUPS):
        at = slice(k * rows, (k + 1) * rows)
        piece = line[0] if k == 0 else line[k][...] + line[7 - k][...]
        norm, _ = normed(piece[0:rows, :].astype(F32))
        norms[at, :] = norm
        si[at, :] = (norm * gain + shift).astype(BF16)
        gb[at, :] = piece[rows:, :]
    for m in range(GROUPS):
        slot = (z - ((c // 2) ^ m)) % GROUPS
        att[pl.ds(pl.multiple_of(slot * rows, rows), rows), :] = atts[m][...]
    step = 2 * rows
    bias_sum = jnp.zeros((1, hid), F32)
    for i in range(GROUPS * rows // step):
        at = slice(i * step, (i + 1) * step)
        hidden = mm(si[at, :], up_w[...]) + up_b[...].astype(F32)
        cdf = 0.5 + 0.5 * lax.erf(hidden * (0.5**0.5))
        density = jnp.exp(hidden * hidden * -0.5) * (1.0 / math.sqrt(2.0 * math.pi))
        active[at, :] = (hidden * cdf).astype(BF16)
        grad = (mm_nt(gb[at, :], down_w[...]) * (cdf + hidden * density)).astype(BF16)
        hidden_grad[at, :] = grad
        bias_sum += jnp.sum(grad.astype(F32), axis=0, keepdims=True)
        part = mm(active[at, :], down_w[...]) + mm(att[at, :], out_w[...])
        second[at, :] = mm_nt(grad, up_w[...])
        for k in range(2):
            piece = outs[2 * i + k]
            piece[0:rows, :] = part[k * rows : (k + 1) * rows, :].astype(piece.dtype)
    dgain = jnp.zeros((1, width), F32)
    dshift = jnp.zeros((1, width), F32)
    for k in range(GROUPS):
        at = slice(k * rows, (k + 1) * rows)
        norm = norms[at, :]
        grad = second[at, :]
        dgain += jnp.sum(grad * norm, axis=0, keepdims=True)
        dshift += jnp.sum(grad, axis=0, keepdims=True)
        outs[k][rows:, :] = (grad * gain).astype(outs[k].dtype)
    row = lax.broadcasted_iota(jnp.int32, sums.shape, 0)
    vectors = jnp.where(row == 0, dgain, jnp.where(row == 1, dshift, bias_sum))
    sums[...] = jnp.where(row < 3, vectors, 0.0).astype(BF16)


def ffn_dw_body(places, si, gb, active, hidden_grad, att, keep, send, dwbuf):
    c = places[0]
    width, hid, shard = si.shape[1], active.shape[1], att.shape[1]
    dwbuf[0:width, :] = mm_tn(si[...], hidden_grad[...])
    dwbuf[width : width + hid, :] = mm_tn(active[...], gb[...])
    dwbuf[width + hid : width + hid + shard, :] = mm_tn(att[...], gb[...])
    dwbuf[width + hid + shard :, :] = jnp.zeros_like(dwbuf[width + hid + shard :, :])
    chunk = dwbuf.shape[0] // (2 * GROUPS)
    for j in range(GROUPS):
        to = slice(j * chunk, (j + 1) * chunk)
        near = c ^ (2 * j)
        keep[to, :] = dwbuf[pl.ds(pl.multiple_of(near * chunk, chunk), chunk), :]
        far = near ^ 1
        send[to, :] = dwbuf[pl.ds(pl.multiple_of(far * chunk, chunk), chunk), :].astype(BF16)


def spread_body(places, *refs):
    near, far = refs[0:4], refs[4:8]
    up_dw, down_dw, out_dw, vec, up_db, buf, box = refs[8:]
    c, z = places[0], places[1]
    chunk = near[0].shape[0] - EXTRA
    for j in range(GROUPS):
        for place, piece in ((c ^ (2 * j), near[j]), ((c ^ (2 * j)) ^ 1, far[j])):
            buf[pl.ds(pl.multiple_of(place * chunk, chunk), chunk), :] = piece[0:chunk, :].astype(F32)
            box[place] = piece[chunk:, :].astype(F32)
    up_dw[...] = buf[0 : up_dw.shape[0], :]
    last = up_dw.shape[0] + down_dw.shape[0]
    down_dw[...] = buf[up_dw.shape[0] : last, :]
    out_dw[...] = buf[last : last + out_dw.shape[0], :]
    total = box[0]
    for place in range(1, 2 * GROUPS):
        total = total + box[place]
    up_db[...] = total[2:3, :]
    shard = vec.shape[1]
    block = total[:, 0:shard]
    for owner in range(1, GROUPS):
        block = jnp.where(z == owner, total[:, owner * shard : (owner + 1) * shard], block)
    vec[...] = block[0 : vec.shape[0], :]


def finish_body(places, *refs):
    near, far = refs[0:4], refs[4:8]
    qkv_dw, vec, bias, box, tail = refs[8:]
    c = places[0]
    core, group = c % 2, c // 2
    part = near[0].shape[0] - EXTRA
    shard = 2 * part
    for j in range(GROUPS):
        place = group ^ j
        tail[place] = near[j][part:, :].astype(F32)
        box[place, pl.ds(pl.multiple_of(core * part, part), part), :] = near[j][0:part, :].astype(F32)
        box[place, pl.ds(pl.multiple_of((1 - core) * part, part), part), :] = far[j][
            0:part, :
        ].astype(F32)
    for g in range(GROUPS):
        for kind, slot in enumerate((1, 0, 2)):
            at = (kind * GROUPS + g) * GROUP_COLS
            qkv_dw[:, at : at + GROUP_COLS] = box[
                g, :, slot * GROUP_COLS : (slot + 1) * GROUP_COLS
            ]
    total = tail[0] + tail[1] + tail[2] + tail[3]
    bias[...] = total[0:1, :]
    for slot in range(3):
        vec[slot : slot + 1, :] = total[1:2, slot * shard : (slot + 1) * shard]


def token_body(places, xg, vec, ca, ffn, *refs):
    from_line = refs[0:3]
    layer_out, input_grad = refs[3:]
    rows = ca.shape[0]
    values = xg[0:rows, :].astype(F32)
    total = values + vec[4:5, :] + vec[5:6, :] + ffn[0:rows, :]
    cot = ca[...] + ffn[rows:, :]
    for piece in from_line:
        total += piece[0:rows, :].astype(F32)
        cot += piece[rows:, :].astype(F32)
    layer_out[...] = total.astype(BF16)
    norm, scale = normed(values)
    shifted = cot - jnp.mean(cot, axis=-1, keepdims=True)
    shifted -= norm * jnp.mean(cot * norm, axis=-1, keepdims=True)
    input_grad[...] = xg[rows:, :].astype(F32) + scale * shifted


def block_shards(
    tokens,
    cotangent,
    att_gain,
    att_shift,
    ffn_gain,
    ffn_shift,
    qkv_weight,
    qkv_bias,
    out_weight,
    out_bias,
    up_weight,
    up_bias,
    down_weight,
    down_bias,
):
    width = tokens.shape[-1]
    x = tokens.reshape(-1, width)
    g = cotangent.reshape(-1, width)
    rows = x.shape[0]
    n_ctx, n_z = lax.axis_size("ctx"), lax.axis_size("fsdp")
    c, z = lax.axis_index("ctx"), lax.axis_index("fsdp")
    group = c // 2
    shard = width // n_z
    part = shard // 2
    hid = up_weight.shape[1]
    places = jnp.stack([c, z]).astype(jnp.int32)
    three = 3 * GROUP_COLS
    near_rows = GROUPS * rows
    pair = 2 * rows

    def over_ctx(value, k):
        return lax.ppermute(value, "ctx", [(i, i ^ k) for i in range(n_ctx)])

    def over_z(value, k):
        return lax.ppermute(value, "fsdp", [(i, i ^ k) for i in range(n_z)])

    def around_z(value, k):
        return lax.ppermute(value, "fsdp", [(i, (i + k) % n_z) for i in range(n_z)])

    def along_z(value, k, first):
        pairs = [(i, i + 1) for i in range(first, n_z - 1)]
        if k < 0:
            pairs = [(n_z - 1 - a, n_z - 1 - b) for a, b in pairs]
        return lax.ppermute(value, "fsdp", pairs)

    def over_both(value, pairs):
        return lax.ppermute(
            value, ("ctx", "fsdp"), [(a * n_z + b, d * n_z + e) for a, b, d, e in pairs]
        )

    def chips(value):
        return [value] + [over_ctx(value, 2 * j) for j in range(1, GROUPS)]

    payload, xg, xg_line, out_half = local_call(
        "pack",
        pack_body,
        places,
        [att_gain, att_shift, ffn_gain, ffn_shift, out_bias, down_bias, qkv_bias],
        [((part + EXTRA, three), BF16)] + [((pair, width), BF16)] * 2 + [((part, width), BF16)],
        [
            pltpu.VMEM((EXTRA, three), F32),
            pltpu.VMEM((part, 3 * width), BF16),
            pltpu.SemaphoreType.DMA((6,)),
        ],
        whole=[qkv_weight, x, g, out_weight],
        vmem=60,
    )
    near_w = [payload] + [over_z(payload, k) for k in range(1, n_z)]
    plane = chips(xg)
    by_place = [(a, b, a, b ^ (a // 2)) for a in range(n_ctx) for b in range(n_z)]
    by_plane = [(a, b, a ^ (2 * b), b) for a in range(n_ctx) for b in range(n_z)]
    ow_near = over_both(over_both(out_half, by_place), by_plane)
    stack, vec, bias, xg_line = local_call(
        "collect",
        collect_body,
        places,
        near_w,
        [((GROUPS * part, three), BF16), ((8, width), F32), ((8, three), F32)],
        [pltpu.VMEM((GROUPS, EXTRA, three), F32)],
        after=plane[1:],
        through=[xg_line],
    )
    up, down = [xg_line], [xg_line]
    for i in range(n_z - 1):
        up.append(along_z(up[-1], 1, i))
        down.append(along_z(down[-1], -1, i))
    line = up + down[1:]
    cos_tab, sin_tab = rotary_tables(rows, n_ctx)
    fi, w, q, kv, cos, sin = local_call(
        "qkv",
        qkv_body,
        places,
        [*plane, stack, over_ctx(stack, 1), vec, bias, cos_tab, sin_tab],
        [
            ((near_rows, width), BF16),
            ((width, three), BF16),
            ((near_rows, GROUP_COLS), BF16),
            ((2 * near_rows, GROUP_COLS), BF16),
            ((near_rows, 128), F32),
            ((near_rows, 128), F32),
        ],
        flops=2 * near_rows * width * 4 * GROUP_COLS,
    )
    *att, dkq, dv, far = local_call(
        "attend",
        attend_body,
        places,
        [q, kv, over_ctx(kv, 1), *plane, ow_near, over_ctx(ow_near, 1)],
        [((rows, GROUP_COLS), BF16)] * GROUPS
        + [
            ((near_rows, 2 * GROUP_COLS), F32),
            ((near_rows, GROUP_COLS), F32),
            ((near_rows, 2 * GROUP_COLS), BF16),
        ],
        [
            pltpu.VMEM((2 * near_rows, GROUP_COLS), BF16),
            pltpu.VMEM((2 * near_rows, GROUP_COLS), BF16),
            pltpu.VMEM((near_rows, GROUP_COLS), BF16),
            pltpu.VMEM((near_rows, GROUP_COLS), BF16),
            pltpu.VMEM((GROUP_COLS, width), BF16),
            pltpu.VMEM((near_rows, width), BF16),
            pltpu.VMEM((GROUPS, rows, GROUP_COLS), BF16),
        ],
        flops=2 * 7 * 256 * GROUP_HEADS * near_rows * 2 * near_rows,
    )
    att = [
        over_both(
            att[m], [(a, b, 2 * (b ^ m) + a % 2, a // 2) for a in range(n_ctx) for b in range(n_z)]
        )
        for m in range(GROUPS)
    ]

    ca, *sends, keep, send = local_call(
        "joined",
        joined_body,
        places,
        [dkq, dv, over_ctx(far, 1), w, fi, cos, sin, vec, *plane, g],
        [((rows, width), F32)]
        + [((rows, width), BF16)] * 3
        + [
            ((n_z, part + EXTRA, three), F32),
            ((n_z, part + EXTRA, three), BF16),
        ],
        [
            pltpu.VMEM((near_rows, 2 * GROUP_COLS), BF16),
            pltpu.VMEM((near_rows, GROUP_COLS), BF16),
            pltpu.VMEM((width, three), F32),
            pltpu.VMEM((near_rows, width), F32),
            pltpu.VMEM((GROUPS, EXTRA, three), F32),
        ],
        flops=2 * 2 * near_rows * width * three,
    )
    (plane_total,) = local_call(
        "plane_sum",
        plane_sum_body,
        places,
        [ca] + [over_ctx(sends[j - 1], 2 * j) for j in range(1, GROUPS)],
        [((rows, width), F32)],
    )
    own, *sends = local_call(
        "qkv_pair",
        qkv_pair_body,
        places,
        [keep, over_ctx(send, 1)],
        [((part + EXTRA, three), F32)] + [((part + EXTRA, three), BF16)] * 3,
    )
    (qkv_total,) = local_call(
        "qkv_sum",
        sum_body,
        places,
        [own] + [over_z(sends[k - 1], k) for k in range(1, n_z)],
        [((part + EXTRA, three), BF16)],
    )

    chunk = -(-(width + hid + shard) // (n_ctx * EXTRA)) * EXTRA
    *ffn_outs, ffn_sums, si, gb, active, hidden_grad, att = local_call(
        "ffn",
        ffn_body,
        places,
        [*line, up_weight, down_weight, up_bias.reshape(1, -1), vec, out_weight, *att],
        [((pair, width), F32)]
        + [((pair, width), BF16)] * 3
        + [((EXTRA, width), BF16)]
        + [((near_rows, n), BF16) for n in (width, width, hid, hid, GROUP_COLS)],
        [pltpu.VMEM((near_rows, width), F32), pltpu.VMEM((near_rows, width), F32)],
        flops=2 * 4 * near_rows * width * hid,
        after=[plane_total],
    )
    from_line = [around_z(ffn_outs[k], -k) for k in range(1, n_z)]
    ffn_keep, ffn_send = local_call(
        "ffn_dw",
        ffn_dw_body,
        places,
        [si, gb, active, hidden_grad, att],
        [((GROUPS * chunk, width), F32), ((GROUPS * chunk, width), BF16)],
        [pltpu.VMEM((n_ctx * chunk, width), F32)],
        flops=2 * 2 * near_rows * width * hid,
    )

    own, *sends = local_call(
        "ffn_pair",
        ffn_pair_body,
        places,
        [ffn_keep, over_ctx(ffn_send, 1)],
        [((chunk, width), F32)] + [((chunk, width), BF16)] * 3,
    )
    (ffn_total,) = local_call(
        "ffn_sum",
        ffn_sum_body,
        places,
        [own]
        + [over_ctx(sends[j - 1], 2 * j) for j in range(1, GROUPS)]
        + [ffn_sums]
        + [over_z(ffn_sums, k) for k in range(1, n_z)],
        [((chunk + EXTRA, width), BF16)],
    )
    near = chips(ffn_total)
    up_dw, down_dw, out_dw, ffn_vec, up_db = local_call(
        "ffn_spread",
        spread_body,
        places,
        near + [over_ctx(p, 1) for p in near],
        [
            ((width, hid), F32),
            ((hid, width), F32),
            ((shard, width), F32),
            ((8, shard), F32),
            ((1, hid), F32),
        ],
        [pltpu.VMEM((n_ctx * chunk, width), F32), pltpu.VMEM((n_ctx, EXTRA, width), F32)],
    )
    near = chips(qkv_total)
    qkv_dw, sums, qkv_db = local_call(
        "qkv_finish",
        finish_body,
        places,
        near + [over_ctx(p, 1) for p in near],
        [((shard, 3 * width), F32), ((8, shard), F32), ((1, three), F32)],
        [pltpu.VMEM((GROUPS, shard, three), F32), pltpu.VMEM((GROUPS, EXTRA, three), F32)],
    )

    layer_out, input_grad = local_call(
        "token",
        token_body,
        places,
        [xg, vec, plane_total, ffn_outs[0], *from_line],
        [((rows, width), BF16), ((rows, width), F32)],
        after=[ffn_total],
    )
    return (
        layer_out.reshape(tokens.shape),
        input_grad.reshape(tokens.shape),
        sums[0],
        sums[1],
        ffn_vec[0],
        ffn_vec[1],
        qkv_dw,
        qkv_db[0],
        out_dw,
        sums[2],
        up_dw,
        up_db[0],
        down_dw,
        sums[2],
    )


def solution(mesh):
    in_specs = (
        P("fsdp", "ctx", None),
        P("fsdp", "ctx", None),
        P("fsdp"),
        P("fsdp"),
        P("fsdp"),
        P("fsdp"),
        P("fsdp", None),
        P("fsdp"),
        P("fsdp", None),
        P("fsdp"),
        P(None, "fsdp"),
        P("fsdp"),
        P("fsdp", None),
        P("fsdp"),
    )
    out_specs = (
        P("fsdp", "ctx", None),
        P("fsdp", "ctx", None),
        P("fsdp"),
        P("fsdp"),
        P("fsdp"),
        P("fsdp"),
        P("fsdp", None),
        P("fsdp"),
        P("fsdp", None),
        P("fsdp"),
        P(None, "fsdp"),
        P("fsdp"),
        P("fsdp", None),
        P("fsdp"),
    )
    per_device = block_shards if fits(mesh) else shards
    return jax.shard_map(per_device, mesh=mesh, in_specs=in_specs, out_specs=out_specs, check_vma=False)
```

```python
import math

import jax
import jax.numpy as jnp
from jax import lax
from jax.experimental import pallas as pl
from jax.experimental.pallas import tpu as pltpu
from jax.sharding import PartitionSpec as P
import numpy as np

HEADS = 12
HEAD_DIM = 64
ROT_DIMS = 16


def layer_norm(values, norm_gain, norm_shift):
    center = values - jnp.mean(values, axis=-1, keepdims=True)
    spread = jnp.mean(center * center, axis=-1, keepdims=True)
    return center * lax.rsqrt(spread + 1e-05) * norm_gain + norm_shift


def exact_gelu(values):
    return jax.nn.gelu(values, approximate=False)


def stored_positions(rows, devices):
    row_order = jnp.arange(rows * devices, dtype=jnp.int32)
    device = row_order // rows
    within = row_order % rows
    half_rows = rows // 2
    return jnp.where(
        within < half_rows,
        device * half_rows + within,
        (2 * devices - 1 - device) * half_rows + within - half_rows,
    )


def rotary_angles(positions):
    half_rot = ROT_DIMS // 2
    inverse = jnp.power(10000.0, -2.0 * jnp.arange(half_rot, dtype=jnp.float32) / ROT_DIMS)
    return positions.astype(jnp.float32)[:, None] * inverse[None, :]


def rotate(heads, angles):
    half_rot = ROT_DIMS // 2
    cosine = jnp.cos(angles)[:, None, :]
    sine_part = jnp.sin(angles)[:, None, :]
    lower_half = heads[..., :half_rot]
    upper_half = heads[..., half_rot:ROT_DIMS]
    return jnp.concatenate(
        [
            lower_half * cosine - upper_half * sine_part,
            upper_half * cosine + lower_half * sine_part,
            heads[..., ROT_DIMS:],
        ],
        axis=-1,
    )


def to_order(stack, ctx_count, half_rows):
    tail = stack.shape[1:]
    shaped = stack.reshape((ctx_count, 2, half_rows) + tail)
    return jnp.concatenate(
        [shaped[:, 0].reshape((-1,) + tail), shaped[::-1, 1].reshape((-1,) + tail)], axis=0
    )


def from_order(stack, ctx_count, half_rows):
    tail = stack.shape[1:]
    middle = stack.shape[0] // 2
    first = stack[:middle].reshape((ctx_count, half_rows) + tail)
    second = stack[middle:].reshape((ctx_count, half_rows) + tail)[::-1]
    return jnp.stack([first, second], axis=1).reshape(stack.shape)


def scores_block(query_heads, key_heads, query_pos, key_pos):
    scores = jnp.einsum(
        "qhd,khd->hqk", query_heads, key_heads, preferred_element_type=jnp.float32
    ) / math.sqrt(HEAD_DIM)
    return jnp.where(key_pos[None, None, :] <= query_pos[None, :, None], scores, -1000000000.0)


def grad_block(
    query_heads, grad_heads, log_total, inner, query_pos, key_heads, value_heads, key_pos
):
    scores = scores_block(query_heads, key_heads, query_pos, key_pos)
    probability = jnp.exp(scores - log_total[:, :, None])
    prob_grad = jnp.einsum(
        "qhd,khd->hqk", grad_heads, value_heads, preferred_element_type=jnp.float32
    )
    score_grad = (probability * (prob_grad - inner[:, :, None])).astype(jnp.bfloat16)
    return (probability.astype(jnp.bfloat16), score_grad)


def shards(
    tokens,
    cotangent,
    att_gain,
    att_shift,
    ffn_gain,
    ffn_shift,
    qkv_weight,
    qkv_bias,
    out_weight,
    out_bias,
    up_weight,
    up_bias,
    down_weight,
    down_bias,
):
    model_width = tokens.shape[-1]
    rows_in = tokens.reshape(-1, model_width)
    grad_rows = cotangent.reshape(-1, model_width)
    own_rows = rows_in.shape[0]
    half_rows = own_rows // 2
    ctx_count = lax.axis_size("ctx")
    ctx_place = lax.axis_index("ctx")
    total_rows = own_rows * ctx_count
    all_pos = stored_positions(own_rows, ctx_count)
    own_pos = lax.dynamic_slice_in_dim(all_pos, ctx_place * own_rows, own_rows, 0)
    (
        gain_attend,
        shift_attend,
        gain_feed,
        shift_feed,
        mat_qkv,
        bias_qkv,
        mat_out,
        bias_out,
        bias_down,
    ) = (
        lax.all_gather(att_gain, "fsdp", axis=0, tiled=True),
        lax.all_gather(att_shift, "fsdp", axis=0, tiled=True),
        lax.all_gather(ffn_gain, "fsdp", axis=0, tiled=True),
        lax.all_gather(ffn_shift, "fsdp", axis=0, tiled=True),
        lax.all_gather(qkv_weight, "fsdp", axis=0, tiled=True),
        lax.all_gather(qkv_bias, "fsdp", axis=0, tiled=True),
        lax.all_gather(out_weight, "fsdp", axis=0, tiled=True),
        lax.all_gather(out_bias, "fsdp", axis=0, tiled=True),
        lax.all_gather(down_bias, "fsdp", axis=0, tiled=True),
    )
    tokens32 = rows_in.astype(jnp.float32)
    grad32 = grad_rows.astype(jnp.float32)
    first_norm, first_back = jax.vjp(
        layer_norm, tokens32, gain_attend.astype(jnp.float32), shift_attend.astype(jnp.float32)
    )
    second_norm, second_back = jax.vjp(
        layer_norm, tokens32, gain_feed.astype(jnp.float32), shift_feed.astype(jnp.float32)
    )
    first_in = first_norm.astype(jnp.bfloat16)
    second_in = second_norm.astype(jnp.bfloat16)
    joined = jnp.dot(first_in, mat_qkv, preferred_element_type=jnp.float32) + bias_qkv.astype(
        jnp.float32
    )
    angles = rotary_angles(own_pos)

    def project_heads(joined_rows):
        queries = rotate(joined_rows[:, :model_width].reshape(own_rows, HEADS, HEAD_DIM), angles)
        keys_rot = rotate(
            joined_rows[:, model_width : 2 * model_width].reshape(own_rows, HEADS, HEAD_DIM), angles
        )
        return (
            queries.reshape(own_rows, model_width),
            keys_rot.reshape(own_rows, model_width),
            joined_rows[:, 2 * model_width :],
        )

    (queries, keys_rot, values_rows), rotary_back = jax.vjp(project_heads, joined)
    query_low = queries.astype(jnp.bfloat16)
    key_low = keys_rot.astype(jnp.bfloat16)
    value_low = values_rows.astype(jnp.bfloat16)
    key_all, value_all = (
        lax.all_gather(key_low, "ctx", axis=0, tiled=True),
        lax.all_gather(value_low, "ctx", axis=0, tiled=True),
    )
    query_heads = query_low.reshape(own_rows, HEADS, HEAD_DIM)
    key_heads = to_order(key_all, ctx_count, half_rows).reshape(total_rows, HEADS, HEAD_DIM)
    value_heads = to_order(value_all, ctx_count, half_rows).reshape(total_rows, HEADS, HEAD_DIM)
    block_keys = min(1024, total_rows)

    def key_piece(block_index):
        start = block_index * block_keys
        return (
            lax.dynamic_slice_in_dim(key_heads, start, block_keys, 0),
            lax.dynamic_slice_in_dim(value_heads, start, block_keys, 0),
            start + jnp.arange(block_keys, dtype=jnp.int32),
        )

    need_low = (ctx_place + 1) * half_rows
    need_high = (2 * ctx_count - ctx_place) * half_rows
    counts = ((need_low + block_keys - 1) // block_keys, (need_high + block_keys - 1) // block_keys)
    query_parts = (query_heads[:half_rows], query_heads[half_rows:])
    pos_parts = (own_pos[:half_rows], own_pos[half_rows:])

    def half_lse(query_half, pos_half, count):

        def lse_step(block_index, carried):
            row_top, exp_total = carried
            key_block, value_skip, key_pos = key_piece(block_index)
            scores = scores_block(query_half, key_block, pos_half, key_pos)
            new_top = jnp.maximum(row_top, jnp.max(scores, axis=-1))
            exp_total = exp_total * jnp.exp(row_top - new_top) + jnp.sum(
                jnp.exp(scores - new_top[:, :, None]), axis=-1
            )
            return (new_top, exp_total)

        start_top = jnp.full((HEADS, half_rows), -1e30, jnp.float32)
        start_sum = jnp.zeros((HEADS, half_rows), jnp.float32)
        row_top, exp_total = lax.fori_loop(0, count, lse_step, (start_top, start_sum))
        return row_top + jnp.log(exp_total)

    lse_parts = [
        half_lse(query_parts[half_index], pos_parts[half_index], counts[half_index])
        for half_index in range(2)
    ]

    def half_mix(query_half, pos_half, lse_half, count):

        def mix_step(block_index, totals):
            key_block, value_block, key_pos = key_piece(block_index)
            scores = scores_block(query_half, key_block, pos_half, key_pos)
            probability = jnp.exp(scores - lse_half[:, :, None]).astype(jnp.bfloat16)
            return totals + jnp.einsum(
                "hqk,khd->qhd", probability, value_block, preferred_element_type=jnp.float32
            )

        return lax.fori_loop(
            0, count, mix_step, jnp.zeros((half_rows, HEADS, HEAD_DIM), jnp.float32)
        )

    attended = jnp.concatenate(
        [
            half_mix(
                query_parts[half_index],
                pos_parts[half_index],
                lse_parts[half_index],
                counts[half_index],
            )
            for half_index in range(2)
        ],
        axis=0,
    )
    attended_low = attended.reshape(own_rows, model_width).astype(jnp.bfloat16)
    branch_att = jnp.dot(
        attended_low, mat_out, preferred_element_type=jnp.float32
    ) + bias_out.astype(jnp.float32)
    second_all, grad_all = (
        lax.all_gather(second_in, "fsdp", axis=0, tiled=True),
        lax.all_gather(grad_rows, "fsdp", axis=0, tiled=True),
    )
    hidden = jnp.dot(second_all, up_weight, preferred_element_type=jnp.float32) + up_bias.astype(
        jnp.float32
    )
    active, gelu_back = jax.vjp(exact_gelu, hidden)
    active_low = active.astype(jnp.bfloat16)
    ffn_part = jnp.dot(active_low, down_weight, preferred_element_type=jnp.float32)
    active_grad = jnp.einsum("te,fe->tf", grad_all, down_weight, preferred_element_type=jnp.float32)
    hidden_grad = gelu_back(active_grad)[0].astype(jnp.bfloat16)
    down_dweight = jnp.einsum("tf,te->fe", active_low, grad_all, preferred_element_type=jnp.float32)
    up_dweight = jnp.einsum(
        "td,tf->df", second_all, hidden_grad, preferred_element_type=jnp.float32
    )
    up_dbias = jnp.sum(hidden_grad.astype(jnp.float32), axis=0)
    second_part = jnp.einsum(
        "tf,df->td", hidden_grad, up_weight, preferred_element_type=jnp.float32
    )
    ffn_sum, second_grad = (
        lax.psum_scatter(ffn_part, "fsdp", scatter_dimension=0, tiled=True),
        lax.psum_scatter(second_part, "fsdp", scatter_dimension=0, tiled=True),
    )
    branch_ffn = ffn_sum + bias_down.astype(jnp.float32)
    layer_out = (tokens32 + branch_att + branch_ffn).astype(jnp.bfloat16).reshape(tokens.shape)
    out_dweight = jnp.einsum(
        "td,te->de", attended_low, grad_rows, preferred_element_type=jnp.float32
    )
    row_sum = jnp.sum(grad32, axis=0)
    attended_grad = jnp.einsum(
        "te,de->td", grad_rows, mat_out, preferred_element_type=jnp.float32
    ).astype(jnp.bfloat16)
    grad_heads = attended_grad.reshape(own_rows, HEADS, HEAD_DIM)
    grad_parts = (grad_heads[:half_rows], grad_heads[half_rows:])

    def half_inner(query_half, grad_half, pos_half, lse_half, count):

        def inner_step(block_index, totals):
            key_block, value_block, key_pos = key_piece(block_index)
            scores = scores_block(query_half, key_block, pos_half, key_pos)
            probability = jnp.exp(scores - lse_half[:, :, None])
            prob_grad = jnp.einsum(
                "qhd,khd->hqk", grad_half, value_block, preferred_element_type=jnp.float32
            )
            return totals + jnp.sum(probability * prob_grad, axis=-1)

        return lax.fori_loop(0, count, inner_step, jnp.zeros((HEADS, half_rows), jnp.float32))

    inner_parts = [
        half_inner(
            query_parts[half_index],
            grad_parts[half_index],
            pos_parts[half_index],
            lse_parts[half_index],
            counts[half_index],
        )
        for half_index in range(2)
    ]
    half_zeros = jnp.zeros((half_rows, HEADS, HEAD_DIM), jnp.float32)

    def half_back(half_index, carried):
        query_half = query_parts[half_index]
        grad_half = grad_parts[half_index]

        def query_step(block_index, state):
            query_total, key_acc, value_acc = state
            key_block, value_block, key_pos = key_piece(block_index)
            prob_low, score_grad = grad_block(
                query_half,
                grad_half,
                lse_parts[half_index],
                inner_parts[half_index],
                pos_parts[half_index],
                key_block,
                value_block,
                key_pos,
            )
            key_part = jnp.einsum(
                "hqk,qhd->khd", score_grad, query_half, preferred_element_type=jnp.float32
            )
            value_part = jnp.einsum(
                "hqk,qhd->khd", prob_low, grad_half, preferred_element_type=jnp.float32
            )
            start = block_index * block_keys
            key_acc = lax.dynamic_update_slice_in_dim(
                key_acc,
                lax.dynamic_slice_in_dim(key_acc, start, block_keys, 0) + key_part,
                start,
                0,
            )
            value_acc = lax.dynamic_update_slice_in_dim(
                value_acc,
                lax.dynamic_slice_in_dim(value_acc, start, block_keys, 0) + value_part,
                start,
                0,
            )
            query_total = query_total + jnp.einsum(
                "hqk,khd->qhd", score_grad, key_block, preferred_element_type=jnp.float32
            )
            return (query_total, key_acc, value_acc)

        return lax.fori_loop(0, counts[half_index], query_step, carried)

    full_zeros = jnp.zeros((total_rows, HEADS, HEAD_DIM), jnp.float32)
    query_low_sum, key_acc, value_acc = half_back(0, (half_zeros, full_zeros, full_zeros))
    query_high_sum, key_acc, value_acc = half_back(1, (half_zeros, key_acc, value_acc))
    query_sum = jnp.concatenate([query_low_sum, query_high_sum], axis=0)
    key_stored = from_order(key_acc.reshape(total_rows, model_width), ctx_count, half_rows)
    value_stored = from_order(value_acc.reshape(total_rows, model_width), ctx_count, half_rows)
    key_sum, value_sum = (
        lax.psum_scatter(key_stored, "ctx", scatter_dimension=0, tiled=True),
        lax.psum_scatter(value_stored, "ctx", scatter_dimension=0, tiled=True),
    )
    query_grad = query_sum.reshape(own_rows, model_width) / math.sqrt(HEAD_DIM)
    key_grad = key_sum / math.sqrt(HEAD_DIM)
    joined_grad = rotary_back((query_grad, key_grad, value_sum))[0].astype(jnp.bfloat16)
    qkv_dweight = jnp.einsum("td,tf->df", first_in, joined_grad, preferred_element_type=jnp.float32)
    qkv_dbias = jnp.sum(joined_grad.astype(jnp.float32), axis=0)
    first_grad = jnp.einsum("tf,df->td", joined_grad, mat_qkv, preferred_element_type=jnp.float32)
    token_first, att_dgain, att_dshift = first_back(first_grad)
    token_second, ffn_dgain, ffn_dshift = second_back(second_grad)
    input_grad = (grad32 + token_first + token_second).reshape(tokens.shape)
    shares = (
        lax.psum_scatter(att_dgain, "fsdp", scatter_dimension=0, tiled=True),
        lax.psum_scatter(att_dshift, "fsdp", scatter_dimension=0, tiled=True),
        lax.psum_scatter(ffn_dgain, "fsdp", scatter_dimension=0, tiled=True),
        lax.psum_scatter(ffn_dshift, "fsdp", scatter_dimension=0, tiled=True),
        lax.psum_scatter(qkv_dweight, "fsdp", scatter_dimension=0, tiled=True),
        lax.psum_scatter(qkv_dbias, "fsdp", scatter_dimension=0, tiled=True),
        lax.psum_scatter(out_dweight, "fsdp", scatter_dimension=0, tiled=True),
        lax.psum_scatter(row_sum, "fsdp", scatter_dimension=0, tiled=True),
    ) + (up_dweight, up_dbias, down_dweight)
    totals = lax.psum(
        (
            shares[0],
            shares[1],
            shares[2],
            shares[3],
            shares[4],
            shares[5],
            shares[6],
            shares[7],
            shares[8],
            shares[9],
            shares[10],
        ),
        "ctx",
    )
    return (
        layer_out,
        input_grad,
        totals[0],
        totals[1],
        totals[2],
        totals[3],
        totals[4],
        totals[5],
        totals[6],
        totals[7],
        totals[8],
        totals[9],
        totals[10],
        totals[7],
    )


F32 = jnp.float32
BF16 = jnp.bfloat16
GROUPS = 4
GROUP_HEADS = HEADS // GROUPS
GROUP_COLS = GROUP_HEADS * HEAD_DIM
EXTRA = 16


def fits(mesh):
    return mesh.shape["ctx"] == 2 * GROUPS and mesh.shape["fsdp"] == GROUPS


def mm(left, right):
    return jnp.dot(left, right, preferred_element_type=F32)


def mm_nt(left, right):
    return lax.dot_general(left, right, (((1,), (1,)), ((), ())), preferred_element_type=F32)


def mm_tn(left, right):
    return lax.dot_general(left, right, (((0,), (0,)), ((), ())), preferred_element_type=F32)


def local_call(
    name, body, places, ins, outs, scratch=(), flops=0, whole=(), after=(), through=(), vmem=28
):
    waits = len(after) + len(through)
    inner, first, last = body, 1 + waits, 1 + waits + len(ins) + len(whole)

    def body(*refs):
        given = refs[first:last]
        given = given[len(whole) :][::-1] + given[: len(whole)][::-1]
        made = refs[last : last + len(outs)]
        inner(refs[0], *given, *made, *refs[last + len(outs) + len(through) :])

    moved = sum(math.prod(i.shape) * i.dtype.itemsize for i in ins)
    moved += sum(math.prod(s) * jnp.dtype(d).itemsize for s, d in outs)
    return pl.pallas_call(
        body,
        out_shape=[jax.ShapeDtypeStruct(s, d) for s, d in outs]
        + [jax.ShapeDtypeStruct(t.shape, t.dtype) for t in through],
        in_specs=[pl.BlockSpec(memory_space=pltpu.SMEM)]
        + [pl.BlockSpec(memory_space=pl.ANY)] * (waits + len(whole))
        + [pl.BlockSpec(memory_space=pltpu.VMEM)] * len(ins),
        out_specs=[pl.BlockSpec(memory_space=pltpu.VMEM)] * len(outs)
        + [pl.BlockSpec(memory_space=pl.ANY)] * len(through),
        input_output_aliases={1 + len(after) + i: len(outs) + i for i in range(len(through))},
        scratch_shapes=list(scratch),
        compiler_params=pltpu.CompilerParams(vmem_limit_bytes=vmem * 2**20),
        cost_estimate=pl.CostEstimate(flops=flops, bytes_accessed=moved, transcendentals=0),
        name=name,
    )(places, *after, *through, *whole[::-1], *ins[::-1])


def normed(values):
    center = values - jnp.mean(values, axis=-1, keepdims=True)
    spread = jnp.mean(center * center, axis=-1, keepdims=True)
    scale = lax.rsqrt(spread + 1e-05)
    return center * scale, scale


def rotary_tables(rows, devices):
    half = rows // 2
    order = np.arange(rows * devices)
    device, within = order // rows, order % rows
    position = np.where(
        within < half, device * half + within, (2 * devices - 1 - device) * half + within - half
    )
    pairs = ROT_DIMS // 2
    inverse = np.power(10000.0, -2.0 * np.arange(pairs) / ROT_DIMS).astype(np.float32)
    angle = (position.astype(np.float32)[:, None] * inverse[None, :]).astype(np.float32)
    cosine = np.ones((rows * devices, HEAD_DIM), np.float32)
    sine = np.zeros((rows * devices, HEAD_DIM), np.float32)
    cosine[:, :pairs] = cosine[:, pairs:ROT_DIMS] = np.cos(angle)
    sine[:, :pairs] = -np.sin(angle)
    sine[:, pairs:ROT_DIMS] = np.sin(angle)
    return np.tile(cosine, (1, 2)), np.tile(sine, (1, 2))


def swapped(values):
    lanes = values.shape[1]
    place = lax.broadcasted_iota(jnp.int32, values.shape, 1) % HEAD_DIM
    return jnp.where(
        place < ROT_DIMS // 2,
        pltpu.roll(values, lanes - ROT_DIMS // 2, 1),
        pltpu.roll(values, ROT_DIMS // 2, 1),
    )


def pack_body(places, *refs):
    vectors, (qkv_w, x, g, out_w) = refs[0:7], refs[7:11]
    payload, xg, xg_line, out_half, box, rows_w, sems = refs[11:]
    core, group = places[0] % 2, places[0] // 2
    part = rows_w.shape[0]
    width = xg.shape[1]
    rows = x.shape[0]
    copies = [
        pltpu.make_async_copy(
            qkv_w.at[pl.ds(pl.multiple_of(core * part, part), part), :], rows_w, sems.at[0]
        ),
        pltpu.make_async_copy(x, xg.at[pl.ds(0, rows), :], sems.at[1]),
        pltpu.make_async_copy(g, xg.at[pl.ds(rows, rows), :], sems.at[2]),
        pltpu.make_async_copy(
            out_w.at[pl.ds(pl.multiple_of(core * part, part), part), :], out_half, sems.at[3]
        ),
        pltpu.make_async_copy(x, xg_line.at[pl.ds(0, rows), :], sems.at[4]),
        pltpu.make_async_copy(g, xg_line.at[pl.ds(rows, rows), :], sems.at[5]),
    ]
    for copy in copies:
        copy.start()
    box[...] = jnp.zeros_like(box)
    shard = vectors[0].shape[0]
    for item in range(6):
        box[item // 3 : item // 3 + 1, (item % 3) * shard : (item % 3 + 1) * shard] = (
            vectors[item][...].astype(F32).reshape(1, shard)
        )
    box[2:3, :] = vectors[6][...].astype(F32).reshape(1, 3 * shard)
    payload[part:, :] = box[...].astype(BF16)
    copies[0].wait()
    for owner in range(GROUPS):

        @pl.when(group == owner)
        def _():
            for slot, base in enumerate((1, 0, 2)):
                at = base * width + owner * GROUP_COLS
                payload[0:part, slot * GROUP_COLS : (slot + 1) * GROUP_COLS] = rows_w[
                    :, at : at + GROUP_COLS
                ]

    for copy in copies[1:]:
        copy.wait()


def collect_body(places, p0, p1, p2, p3, stack, vec, bias, box):
    z, group = places[1], places[0] // 2
    part = p0.shape[0] - EXTRA
    three = p0.shape[1]
    shard = vec.shape[1] // GROUPS
    for k, piece in enumerate((p0, p1, p2, p3)):
        stack[k * part : (k + 1) * part, :] = piece[0:part, :]
        box[z ^ k] = piece[part:, :].astype(F32)
    units = []
    for owner in range(GROUPS):
        block = box[owner]
        for item in range(6):
            vec[item : item + 1, owner * shard : (owner + 1) * shard] = block[
                item // 3 : item // 3 + 1, (item % 3) * shard : (item % 3 + 1) * shard
            ]
        for unit in range(3):
            units.append(block[2:3, unit * GROUP_COLS : (unit + 1) * GROUP_COLS])
    for slot, base in enumerate((GROUPS, 0, 2 * GROUPS)):
        own = units[base]
        for g in range(1, GROUPS):
            own = jnp.where(group == g, units[base + g], own)
        bias[0:1, slot * GROUP_COLS : (slot + 1) * GROUP_COLS] = own


def qkv_body(places, *refs):
    xs, (near, far, vec, bias, cos_tab, sin_tab) = refs[0:4], refs[4:10]
    fi, w, q_out, kv_out, cos, sin = refs[10:]
    c, z = places[0], places[1]
    core = c % 2
    width = w.shape[0]
    shard = width // GROUPS
    part = shard // 2
    rows = xs[0].shape[0] // 2
    half = rows // 2
    near_rows = GROUPS * rows
    for side, stack in ((core, near), (1 - core, far)):
        for k in range(GROUPS):
            base = (z ^ k) * shard + side * part
            w[pl.ds(pl.multiple_of(base, part), part), :] = stack[k * part : (k + 1) * part, :]
    gain, shift = vec[0:1, :], vec[1:2, :]
    two = 2 * GROUP_COLS
    for side in range(2):
        for j in range(GROUPS):
            source = c ^ (2 * j)
            to = slice((side * GROUPS + j) * half, (side * GROUPS + j + 1) * half)
            at = pl.ds(pl.multiple_of(source * rows + side * half, half), half)
            norm, _ = normed(xs[j][side * half : (side + 1) * half, :].astype(F32))
            fi[to, :] = (norm * gain + shift).astype(BF16)
            cos[to, :] = cos_tab[at, :]
            sin[to, :] = sin_tab[at, :]
    step = 2 * rows
    for i in range(near_rows // step):
        at = slice(i * step, (i + 1) * step)
        chunk = fi[at, :]
        kq = mm(chunk, w[:, :two]) + bias[0:1, :two]
        c3 = jnp.concatenate([cos[at, :]] * 3, axis=1)
        s3 = jnp.concatenate([sin[at, :]] * 3, axis=1)
        kq = kq * c3 + swapped(kq) * s3
        kv_out[at, :] = kq[:, :GROUP_COLS].astype(BF16)
        q_out[at, :] = (kq[:, GROUP_COLS:] * HEAD_DIM**-0.5).astype(BF16)
        kv_out[near_rows + i * step : near_rows + (i + 1) * step, :] = (
            mm(chunk, w[:, two:]) + bias[0:1, two:]
        ).astype(BF16)


def key_order(kv, kv_far, kbuf, vbuf, low):
    near_rows = 2 * low
    for side in range(2):
        for part, source in enumerate((kv, kv_far)):
            to = slice((2 * side + part) * low, (2 * side + part + 1) * low)
            kbuf[to, :] = source[side * low : (side + 1) * low, :]
            vbuf[to, :] = source[near_rows + side * low : near_rows + (side + 1) * low, :]


def visible(c, low):
    half = low // GROUPS
    devices = 2 * GROUPS

    def token_pos(index, far):
        device = (c ^ (2 * (index // half))) ^ far
        return device * half + index % half

    q_place = token_pos(lax.broadcasted_iota(jnp.int32, (low, 1), 0), 0)
    k_index = lax.broadcasted_iota(jnp.int32, (1, 2 * low), 1)
    k_place = token_pos(k_index % low, k_index // low)

    def mirrored(place):
        return (2 * devices - 1 - place // half) * half + place % half

    return (k_place <= q_place, mirrored(k_place) <= mirrored(q_place))


def masked_scores(query, keys, side, spans, allowed):
    scores = [mm_nt(query, keys[s]) for s in spans]
    scores[-1] = jnp.where(allowed[side], scores[-1], -1000000000.0)
    return scores


def key_spans(side, low):
    return [slice(0, 2 * low), slice(2 * low, 4 * low)][: side + 1]


def attend_body(places, *refs):
    q, kv, kv_far = refs[0:3]
    xgs, (ow_near, ow_far) = refs[3:7], refs[7:9]
    sends, (dkq, dv_out, far_out) = refs[9:13], refs[13:16]
    kbuf, vbuf, att, ag, ow, g_half, pieces = refs[16:]
    c, z = places[0], places[1]
    core = c % 2
    rows = sends[0].shape[0]
    near_rows = GROUPS * rows
    half = rows // 2
    low = GROUPS * half
    part = GROUP_COLS // 2
    key_order(kv, kv_far, kbuf, vbuf, low)
    ow[pl.ds(pl.multiple_of(core * part, part), part), :] = ow_near[...]
    ow[pl.ds(pl.multiple_of((1 - core) * part, part), part), :] = ow_far[...]
    for side in range(2):
        for j in range(GROUPS):
            g_half[(side * GROUPS + j) * half : (side * GROUPS + j + 1) * half, :] = xgs[j][
                rows + side * half : rows + (side + 1) * half, :
            ]
    ag[...] = mm_nt(g_half[...], ow[...]).astype(BF16)
    allowed = visible(c, low)
    for head in range(GROUP_HEADS):
        lanes = slice(head * HEAD_DIM, (head + 1) * HEAD_DIM)
        lanes2 = slice(GROUP_COLS + head * HEAD_DIM, GROUP_COLS + (head + 1) * HEAD_DIM)
        kh, vh = kbuf[:, lanes], vbuf[:, lanes]
        dk_parts, dv_parts = [], []
        for side in range(2):
            at = slice(side * low, (side + 1) * low)
            qh, gh = q[at, lanes], ag[at, lanes]
            spans = [slice(0, 2 * low), slice(2 * low, 4 * low)][: side + 1]
            scores = [mm_nt(qh, kh[s]) for s in spans]
            scores[-1] = jnp.where(allowed[side], scores[-1], -1000000000.0)
            top = jnp.max(scores[0], axis=-1, keepdims=True)
            for s in scores[1:]:
                top = jnp.maximum(top, jnp.max(s, axis=-1, keepdims=True))
            raised = [jnp.exp(s - top) for s in scores]
            inverse = 1.0 / sum(jnp.sum(r, axis=-1, keepdims=True) for r in raised)
            probs = [r * inverse for r in raised]
            low_probs = [p.astype(BF16) for p in probs]
            mixed = sum(mm(p, vh[s]) for p, s in zip(low_probs, spans))
            att[at, lanes] = mixed.astype(BF16)
            prob_grads = [mm_nt(gh, vh[s]) for s in spans]
            inner = sum(
                jnp.sum(p * d, axis=-1, keepdims=True) for p, d in zip(probs, prob_grads)
            )
            score_grads = [(p * (d - inner)).astype(BF16) for p, d in zip(probs, prob_grads)]
            dkq[at, lanes2] = sum(mm(s, kh[a]) for s, a in zip(score_grads, spans)) * HEAD_DIM**-0.5
            dk_parts.append([mm_tn(s, qh) for s in score_grads])
            dv_parts.append([mm_tn(p, gh) for p in low_probs])
        dk = (dk_parts[0][0] + dk_parts[1][0], dk_parts[1][1])
        dv = (dv_parts[0][0] + dv_parts[1][0], dv_parts[1][1])
        for side in range(2):
            at = slice(side * low, (side + 1) * low)
            dkq[at, lanes] = dk[side][:low]
            dv_out[at, lanes] = dv[side][:low]
            far_out[at, lanes] = dk[side][low:].astype(BF16)
            far_out[at, lanes2] = dv[side][low:].astype(BF16)
    for side in range(2):
        for j in range(GROUPS):
            pieces[j, side * half : (side + 1) * half, :] = att[
                (side * GROUPS + j) * half : (side * GROUPS + j + 1) * half, :
            ]
    for m in range(GROUPS):
        sends[m][...] = pieces[(c // 2) ^ z ^ m]


def joined_body(places, *refs):
    dkq, dv, far, w, fi, cos, sin, vec = refs[0:8]
    xs, g_own = refs[8:12], refs[12]
    ca, sends, keep, send = refs[13], refs[14:17], refs[17], refs[18]
    jgkq, jgv, dwbuf, first, ext = refs[19:]
    c, z = places[0], places[1]
    core, group = c % 2, c // 2
    rows = ca.shape[0]
    half = rows // 2
    width = w.shape[0]
    shard = width // GROUPS
    part = shard // 2
    two = 2 * GROUP_COLS
    step = 2 * rows
    gain = vec[0:1, :]
    bias_kq = jnp.zeros((1, two), F32)
    bias_v = jnp.zeros((1, GROUP_COLS), F32)
    for i in range(GROUPS * rows // step):
        at = slice(i * step, (i + 1) * step)
        other = far[at, :].astype(F32)
        dk = dkq[at, :GROUP_COLS] + other[:, :GROUP_COLS]
        kq = jnp.concatenate([dk, dkq[at, GROUP_COLS:]], axis=1)
        c3 = jnp.concatenate([cos[at, :]] * 3, axis=1)
        s3 = jnp.concatenate([sin[at, :]] * 3, axis=1)
        low_kq = (kq * c3 - swapped(kq) * s3).astype(BF16)
        low_v = (dv[at, :] + other[:, GROUP_COLS:]).astype(BF16)
        jgkq[at, :] = low_kq
        jgv[at, :] = low_v
        bias_kq += jnp.sum(low_kq.astype(F32), axis=0, keepdims=True)
        bias_v += jnp.sum(low_v.astype(F32), axis=0, keepdims=True)
        first[at, :] = mm_nt(low_kq, w[:, :two]) + mm_nt(low_v, w[:, two:])
    dgain = jnp.zeros((1, width), F32)
    dshift = jnp.zeros((1, width), F32)
    for side in range(2):
        for j in range(GROUPS):
            at = slice((side * GROUPS + j) * half, (side * GROUPS + j + 1) * half)
            mine = slice(side * half, (side + 1) * half)
            norm, _ = normed(xs[j][mine, :].astype(F32))
            grad = first[at, :]
            dgain += jnp.sum(grad * norm, axis=0, keepdims=True)
            dshift += jnp.sum(grad, axis=0, keepdims=True)
            if j == 0:
                ca[mine, :] = grad * gain
            else:
                sends[j - 1][mine, :] = (grad * gain).astype(BF16)
    gsum = jnp.sum(g_own[...].astype(F32), axis=0, keepdims=True)
    dwbuf[:, :two] = mm_tn(fi[...], jgkq[...])
    dwbuf[:, two:] = mm_tn(fi[...], jgv[...])
    ext[...] = jnp.zeros_like(ext)
    for owner in range(GROUPS):
        own = slice(owner * shard, (owner + 1) * shard)
        for slot in range(3):
            unit = owner * 3 + slot
            kind = unit // GROUPS
            vector = (bias_kq[:, GROUP_COLS:], bias_kq[:, :GROUP_COLS], bias_v)[kind]
            to = slice(slot * GROUP_COLS, (slot + 1) * GROUP_COLS)
            ext[owner, 0:1, to] = jnp.where(group == unit % GROUPS, vector, 0.0)
        for slot, vector in enumerate((dgain[:, own], dshift[:, own], gsum[:, own])):
            ext[owner, 1:2, slot * shard : (slot + 1) * shard] = vector
    for k in range(GROUPS):
        owner = z ^ k
        base = owner * shard
        keep[k, 0:part, :] = dwbuf[pl.ds(pl.multiple_of(base + core * part, part), part), :]
        send[k, 0:part, :] = dwbuf[
            pl.ds(pl.multiple_of(base + (1 - core) * part, part), part), :
        ].astype(BF16)
        keep[k, part:, :] = ext[owner].astype(BF16).astype(F32)
        send[k, part:, :] = ext[owner].astype(BF16)


def ffn_pair_body(places, keep, got, c1, c2, c3, own, *sends):
    chunk = own.shape[0]
    for j in range(GROUPS):
        total = keep[j * chunk : (j + 1) * chunk, :] + got[j * chunk : (j + 1) * chunk, :].astype(F32)
        if j == 0:
            own[...] = total
        else:
            sends[j - 1][0:chunk, :] = total.astype(BF16)
            sends[j - 1][chunk:, :] = (c1, c2, c3)[j - 1][...]


def qkv_pair_body(places, keep, got, sums, sums_far, own, *rest):
    sends, ext = rest[:-1], rest[-1]
    z = places[1]
    part = own.shape[0] - EXTRA
    first = sums_far.shape[0] - EXTRA
    vector = sums[...].astype(F32) + sums_far[first:, :].astype(F32)
    shard = vector.shape[1] // GROUPS
    ext[...] = jnp.zeros_like(ext)
    for owner in range(GROUPS):
        at = slice(owner * shard, (owner + 1) * shard)
        here = z == owner
        ext[owner, 2:3, 0:shard] = vector[0:1, at]
        ext[owner, 2:3, shard : 2 * shard] = vector[1:2, at]
        ext[owner, 2:3, 2 * shard : 3 * shard] = jnp.where(here, vector[2:3, 0:shard], 0.0)
        ext[owner, 3:4, :] = jnp.where(here, vector[2:3, shard:], 0.0)
    for k in range(GROUPS):
        total = keep[k] + got[k].astype(F32)
        tail = total[part:, :] + ext[z ^ k]
        if k == 0:
            own[0:part, :] = total[0:part, :]
            own[part:, :] = tail
        else:
            sends[k - 1][0:part, :] = total[0:part, :].astype(BF16)
            sends[k - 1][part:, :] = tail.astype(BF16)


def ffn_sum_body(places, own, a, b, c, qkv, out):
    rows = own.shape[0]
    total = own[...]
    for piece in (a, b, c):
        total += piece[0:rows, :].astype(F32)
    out[0:rows, :] = total.astype(BF16)
    most = qkv.shape[0] - 2 * EXTRA
    block = qkv.shape[1] // 3
    out[rows:, :] = jnp.zeros((out.shape[0] - rows, 4 * block), BF16)
    out[rows : rows + most, 0 : 3 * block] = qkv[0:most, :]
    for i in range(3):
        out[rows + i * EXTRA : rows + (i + 1) * EXTRA, 3 * block :] = qkv[
            most : most + EXTRA, i * block : (i + 1) * block
        ]
    out[rows + most :, 0 : 3 * block] = qkv[most + EXTRA :, :]


def sum_body(places, own, a, b, c, out):
    out[...] = (own[...] + a[...].astype(F32) + b[...].astype(F32) + c[...].astype(F32)).astype(
        out.dtype
    )


def ffn_body(places, *refs):
    line = refs[0:7]
    up_w, down_w, up_b, vec, out_w = refs[7:12]
    atts = refs[12:16]
    outs = refs[16:20]
    sums, si, gb, active, hidden_grad, att = refs[20:26]
    second, norms = refs[26:]
    c, z = places[0], places[1]
    rows = line[0].shape[0] // 2
    width = up_w.shape[0]
    hid = up_w.shape[1]
    gain, shift = vec[2:3, :], vec[3:4, :]
    for k in range(GROUPS):
        at = slice(k * rows, (k + 1) * rows)
        piece = line[0] if k == 0 else line[k][...] + line[7 - k][...]
        norm, _ = normed(piece[0:rows, :].astype(F32))
        norms[at, :] = norm
        si[at, :] = (norm * gain + shift).astype(BF16)
        gb[at, :] = piece[rows:, :]
    for m in range(GROUPS):
        slot = (z - ((c // 2) ^ m)) % GROUPS
        att[pl.ds(pl.multiple_of(slot * rows, rows), rows), :] = atts[m][...]
    step = 2 * rows
    bias_sum = jnp.zeros((1, hid), F32)
    for i in range(GROUPS * rows // step):
        at = slice(i * step, (i + 1) * step)
        hidden = mm(si[at, :], up_w[...]) + up_b[...].astype(F32)
        cdf = 0.5 + 0.5 * lax.erf(hidden * (0.5**0.5))
        density = jnp.exp(hidden * hidden * -0.5) * (1.0 / math.sqrt(2.0 * math.pi))
        active[at, :] = (hidden * cdf).astype(BF16)
        grad = (mm_nt(gb[at, :], down_w[...]) * (cdf + hidden * density)).astype(BF16)
        hidden_grad[at, :] = grad
        bias_sum += jnp.sum(grad.astype(F32), axis=0, keepdims=True)
        part = mm(active[at, :], down_w[...]) + mm(att[at, :], out_w[...])
        second[at, :] = mm_nt(grad, up_w[...])
        for k in range(2):
            piece = outs[2 * i + k]
            piece[0:rows, :] = part[k * rows : (k + 1) * rows, :].astype(piece.dtype)
    dgain = jnp.zeros((1, width), F32)
    dshift = jnp.zeros((1, width), F32)
    for k in range(GROUPS):
        at = slice(k * rows, (k + 1) * rows)
        norm = norms[at, :]
        grad = second[at, :]
        dgain += jnp.sum(grad * norm, axis=0, keepdims=True)
        dshift += jnp.sum(grad, axis=0, keepdims=True)
        outs[k][rows:, :] = (grad * gain).astype(outs[k].dtype)
    row = lax.broadcasted_iota(jnp.int32, sums.shape, 0)
    vectors = jnp.where(row == 0, dgain, jnp.where(row == 1, dshift, bias_sum))
    sums[...] = jnp.where(row < 3, vectors, 0.0).astype(BF16)


def ffn_dw_body(places, si, gb, active, hidden_grad, att, sums, keep, send, dwbuf):
    c = places[0]
    width, hid, shard = si.shape[1], active.shape[1], att.shape[1]
    dwbuf[0:width, :] = mm_tn(si[...], hidden_grad[...])
    dwbuf[width : width + hid, :] = mm_tn(active[...], gb[...])
    dwbuf[width + hid : width + hid + shard, :] = mm_tn(att[...], gb[...])
    dwbuf[width + hid + shard :, :] = jnp.zeros_like(dwbuf[width + hid + shard :, :])
    chunk = dwbuf.shape[0] // (2 * GROUPS)
    for j in range(GROUPS):
        to = slice(j * chunk, (j + 1) * chunk)
        near = c ^ (2 * j)
        keep[to, :] = dwbuf[pl.ds(pl.multiple_of(near * chunk, chunk), chunk), :]
        far = near ^ 1
        send[to, :] = dwbuf[pl.ds(pl.multiple_of(far * chunk, chunk), chunk), :].astype(BF16)
    send[GROUPS * chunk :, :] = sums[...]


def stack_body(places, a, b, c, d, out):
    rows = a.shape[0]
    for j, piece in enumerate((a, b, c, d)):
        out[j * rows : (j + 1) * rows, :] = piece[...]


def spread_body(places, near, far, *refs):
    up_dw, down_dw, out_dw, qkv_dw, vec, up_db, bias, buf, box, qkv_box = refs
    c = places[0]
    core, group = c % 2, c // 2
    shard = out_dw.shape[0]
    part = shard // 2
    rows = near.shape[0] // GROUPS
    chunk = rows - part
    most = part - EXTRA
    three = 3 * GROUP_COLS
    for j in range(GROUPS):
        for side, stack in ((core, near), (1 - core, far)):
            place = 2 * (group ^ j) + side
            base = j * rows
            buf[pl.ds(pl.multiple_of(place * chunk, chunk), chunk), :] = stack[
                base : base + chunk, :
            ].astype(F32)
            base += chunk
            at = pl.multiple_of(side * part, part)
            qkv_box[group ^ j, pl.ds(at, most), :] = stack[base : base + most, 0:three].astype(F32)
            for i in range(3):
                qkv_box[
                    group ^ j,
                    pl.ds(pl.multiple_of(at + most, EXTRA), EXTRA),
                    i * GROUP_COLS : (i + 1) * GROUP_COLS,
                ] = stack[base + i * EXTRA : base + (i + 1) * EXTRA, three:].astype(F32)
        box[group ^ j] = near[j * rows + chunk + most : (j + 1) * rows, 0:three].astype(F32)
    last = up_dw.shape[0] + down_dw.shape[0]
    up_dw[...] = buf[0 : up_dw.shape[0], :]
    down_dw[...] = buf[up_dw.shape[0] : last, :]
    out_dw[...] = buf[last : last + shard, :]
    for g in range(GROUPS):
        for kind, slot in enumerate((1, 0, 2)):
            at = (kind * GROUPS + g) * GROUP_COLS
            qkv_dw[:, at : at + GROUP_COLS] = qkv_box[
                g, :, slot * GROUP_COLS : (slot + 1) * GROUP_COLS
            ]
    total = box[0] + box[1] + box[2] + box[3]
    bias[...] = total[0:1, :]
    for slot in range(3):
        vec[slot : slot + 1, :] = total[1:2, slot * shard : (slot + 1) * shard]
    vec[3:4, :] = total[2:3, 0:shard]
    vec[4:5, :] = total[2:3, shard : 2 * shard]
    up_db[0:1, 0:shard] = total[2:3, 2 * shard :]
    up_db[0:1, shard:] = total[3:4, :]


def token_body(places, xg, vec, ca, ffn, *refs):
    from_plane, from_line = refs[0:3], refs[3:6]
    layer_out, input_grad = refs[6:]
    rows = ca.shape[0]
    values = xg[0:rows, :].astype(F32)
    total = values + vec[4:5, :] + vec[5:6, :] + ffn[0:rows, :]
    cot = ca[...] + ffn[rows:, :]
    for piece in from_plane:
        cot += piece[piece.shape[0] - rows :, :].astype(F32)
    for piece in from_line:
        total += piece[0:rows, :].astype(F32)
        cot += piece[rows:, :].astype(F32)
    layer_out[...] = total.astype(BF16)
    norm, scale = normed(values)
    shifted = cot - jnp.mean(cot, axis=-1, keepdims=True)
    shifted -= norm * jnp.mean(cot * norm, axis=-1, keepdims=True)
    input_grad[...] = xg[rows:, :].astype(F32) + scale * shifted


def block_shards(
    tokens,
    cotangent,
    att_gain,
    att_shift,
    ffn_gain,
    ffn_shift,
    qkv_weight,
    qkv_bias,
    out_weight,
    out_bias,
    up_weight,
    up_bias,
    down_weight,
    down_bias,
):
    width = tokens.shape[-1]
    x = tokens.reshape(-1, width)
    g = cotangent.reshape(-1, width)
    rows = x.shape[0]
    n_ctx, n_z = lax.axis_size("ctx"), lax.axis_size("fsdp")
    c, z = lax.axis_index("ctx"), lax.axis_index("fsdp")
    group = c // 2
    shard = width // n_z
    part = shard // 2
    hid = up_weight.shape[1]
    places = jnp.stack([c, z]).astype(jnp.int32)
    three = 3 * GROUP_COLS
    near_rows = GROUPS * rows
    pair = 2 * rows

    def over_ctx(value, k):
        return lax.ppermute(value, "ctx", [(i, i ^ k) for i in range(n_ctx)])

    def over_z(value, k):
        return lax.ppermute(value, "fsdp", [(i, i ^ k) for i in range(n_z)])

    def around_z(value, k):
        return lax.ppermute(value, "fsdp", [(i, (i + k) % n_z) for i in range(n_z)])

    def along_z(value, k, first):
        pairs = [(i, i + 1) for i in range(first, n_z - 1)]
        if k < 0:
            pairs = [(n_z - 1 - a, n_z - 1 - b) for a, b in pairs]
        return lax.ppermute(value, "fsdp", pairs)

    def over_both(value, pairs):
        return lax.ppermute(
            value, ("ctx", "fsdp"), [(a * n_z + b, d * n_z + e) for a, b, d, e in pairs]
        )

    def chips(value):
        return [value] + [over_ctx(value, 2 * j) for j in range(1, GROUPS)]

    payload, xg, xg_line, out_half = local_call(
        "pack",
        pack_body,
        places,
        [att_gain, att_shift, ffn_gain, ffn_shift, out_bias, down_bias, qkv_bias],
        [((part + EXTRA, three), BF16)] + [((pair, width), BF16)] * 2 + [((part, width), BF16)],
        [
            pltpu.VMEM((EXTRA, three), F32),
            pltpu.VMEM((part, 3 * width), BF16),
            pltpu.SemaphoreType.DMA((6,)),
        ],
        whole=[qkv_weight, x, g, out_weight],
        vmem=60,
    )
    near_w = [payload] + [over_z(payload, k) for k in range(1, n_z)]
    plane = chips(xg)
    by_place = [(a, b, a, b ^ (a // 2)) for a in range(n_ctx) for b in range(n_z)]
    by_plane = [(a, b, a ^ (2 * b), b) for a in range(n_ctx) for b in range(n_z)]
    ow_first = over_both(out_half, by_place)
    ow_near = over_both(ow_first, by_plane)
    stack, vec, bias, xg_line = local_call(
        "collect",
        collect_body,
        places,
        near_w,
        [((GROUPS * part, three), BF16), ((8, width), F32), ((8, three), F32)],
        [pltpu.VMEM((GROUPS, EXTRA, three), F32)],
        after=plane[1:],
        through=[xg_line],
    )
    up, down = [xg_line], [xg_line]
    for i in range(n_z - 1):
        up.append(along_z(up[-1], 1, i))
        down.append(along_z(down[-1], -1, i))
    line = up + down[1:]
    cos_tab, sin_tab = rotary_tables(rows, n_ctx)
    fi, w, q, kv, cos, sin = local_call(
        "qkv",
        qkv_body,
        places,
        [*plane, stack, over_ctx(stack, 1), vec, bias, cos_tab, sin_tab],
        [
            ((near_rows, width), BF16),
            ((width, three), BF16),
            ((near_rows, GROUP_COLS), BF16),
            ((2 * near_rows, GROUP_COLS), BF16),
            ((near_rows, 128), F32),
            ((near_rows, 128), F32),
        ],
        flops=2 * near_rows * width * 4 * GROUP_COLS,
    )
    *att, dkq, dv, far = local_call(
        "attend",
        attend_body,
        places,
        [q, kv, over_ctx(kv, 1), *plane, ow_near, over_ctx(ow_near, 1)],
        [((rows, GROUP_COLS), BF16)] * GROUPS
        + [
            ((near_rows, 2 * GROUP_COLS), F32),
            ((near_rows, GROUP_COLS), F32),
            ((near_rows, 2 * GROUP_COLS), BF16),
        ],
        [
            pltpu.VMEM((2 * near_rows, GROUP_COLS), BF16),
            pltpu.VMEM((2 * near_rows, GROUP_COLS), BF16),
            pltpu.VMEM((near_rows, GROUP_COLS), BF16),
            pltpu.VMEM((near_rows, GROUP_COLS), BF16),
            pltpu.VMEM((GROUP_COLS, width), BF16),
            pltpu.VMEM((near_rows, width), BF16),
            pltpu.VMEM((GROUPS, rows, GROUP_COLS), BF16),
        ],
        flops=2 * 7 * 256 * GROUP_HEADS * near_rows * 2 * near_rows,
    )
    att = [
        over_both(
            att[m], [(a, b, 2 * (b ^ m) + a % 2, a // 2) for a in range(n_ctx) for b in range(n_z)]
        )
        for m in range(GROUPS)
    ]

    ca, *sends, keep, send = local_call(
        "joined",
        joined_body,
        places,
        [dkq, dv, over_ctx(far, 1), w, fi, cos, sin, vec, *plane, g],
        [((rows, width), F32)]
        + [((rows, width), BF16)] * 3
        + [
            ((n_z, part + EXTRA, three), F32),
            ((n_z, part + EXTRA, three), BF16),
        ],
        [
            pltpu.VMEM((near_rows, 2 * GROUP_COLS), BF16),
            pltpu.VMEM((near_rows, GROUP_COLS), BF16),
            pltpu.VMEM((width, three), F32),
            pltpu.VMEM((near_rows, width), F32),
            pltpu.VMEM((GROUPS, EXTRA, three), F32),
        ],
        flops=2 * 2 * near_rows * width * three,
    )
    ca_sends = sends
    chunk = -(-(width + hid + shard) // (n_ctx * EXTRA)) * EXTRA
    *ffn_outs, ffn_sums, si, gb, active, hidden_grad, att = local_call(
        "ffn",
        ffn_body,
        places,
        [*line, up_weight, down_weight, up_bias.reshape(1, -1), vec, out_weight, *att],
        [((pair, width), F32)]
        + [((pair, width), BF16)] * 3
        + [((EXTRA, width), BF16)]
        + [((near_rows, n), BF16) for n in (width, width, hid, hid, GROUP_COLS)],
        [pltpu.VMEM((near_rows, width), F32), pltpu.VMEM((near_rows, width), F32)],
        flops=2 * 4 * near_rows * width * hid,
        after=[keep],
    )
    ffn_keep, ffn_send = local_call(
        "ffn_dw",
        ffn_dw_body,
        places,
        [si, gb, active, hidden_grad, att, ffn_sums],
        [((GROUPS * chunk, width), F32), ((GROUPS * chunk + EXTRA, width), BF16)],
        [pltpu.VMEM((n_ctx * chunk, width), F32)],
        flops=2 * 2 * near_rows * width * hid,
    )

    ffn_far = over_ctx(ffn_send, 1)
    own_qkv, *sends = local_call(
        "qkv_pair",
        qkv_pair_body,
        places,
        [keep, over_ctx(send, 1), ffn_sums, ffn_far],
        [((part + EXTRA, three), F32)] + [((part + EXTRA, three), BF16)] * 3,
        [pltpu.VMEM((GROUPS, EXTRA, three), F32)],
    )
    qkv_total, *line_sends = local_call(
        "qkv_sum",
        sum_body,
        places,
        [own_qkv] + [over_z(sends[k - 1], k) for k in range(1, n_z)],
        [((part + EXTRA, three), BF16)],
        through=ffn_outs[1:],
    )
    from_line = [around_z(line_sends[k - 1], -k) for k in range(1, n_z)]
    own, *sends = local_call(
        "ffn_pair",
        ffn_pair_body,
        places,
        [ffn_keep, ffn_far, *ca_sends],
        [((chunk, width), F32)] + [((chunk + rows, width), BF16)] * 3,
    )
    from_plane = [over_ctx(sends[j - 1], 2 * j) for j in range(1, GROUPS)]
    (ffn_total,) = local_call(
        "plane_share",
        ffn_sum_body,
        places,
        [own, *from_plane, qkv_total],
        [((chunk + part, width), BF16)],
    )
    (near,) = local_call(
        "stack",
        stack_body,
        places,
        chips(ffn_total),
        [((GROUPS * (chunk + part), width), BF16)],
        after=from_line,
    )
    up_dw, down_dw, out_dw, qkv_dw, sums, up_db, qkv_db = local_call(
        "spread",
        spread_body,
        places,
        [near, over_ctx(near, 1)],
        [
            ((width, hid), F32),
            ((hid, width), F32),
            ((shard, width), F32),
            ((shard, 3 * width), F32),
            ((8, shard), F32),
            ((1, hid), F32),
            ((1, three), F32),
        ],
        [
            pltpu.VMEM((n_ctx * chunk, width), F32),
            pltpu.VMEM((GROUPS, EXTRA, three), F32),
            pltpu.VMEM((GROUPS, shard, three), F32),
        ],
        vmem=36,
    )

    layer_out, input_grad = local_call(
        "token",
        token_body,
        places,
        [xg, vec, ca, ffn_outs[0], *from_plane, *from_line],
        [((rows, width), BF16), ((rows, width), F32)],
        after=[near],
    )
    return (
        layer_out.reshape(tokens.shape),
        input_grad.reshape(tokens.shape),
        sums[0],
        sums[1],
        sums[3],
        sums[4],
        qkv_dw,
        qkv_db[0],
        out_dw,
        sums[2],
        up_dw,
        up_db[0],
        down_dw,
        sums[2],
    )


def solution(mesh):
    in_specs = (
        P("fsdp", "ctx", None),
        P("fsdp", "ctx", None),
        P("fsdp"),
        P("fsdp"),
        P("fsdp"),
        P("fsdp"),
        P("fsdp", None),
        P("fsdp"),
        P("fsdp", None),
        P("fsdp"),
        P(None, "fsdp"),
        P("fsdp"),
        P("fsdp", None),
        P("fsdp"),
    )
    out_specs = (
        P("fsdp", "ctx", None),
        P("fsdp", "ctx", None),
        P("fsdp"),
        P("fsdp"),
        P("fsdp"),
        P("fsdp"),
        P("fsdp", None),
        P("fsdp"),
        P("fsdp", None),
        P("fsdp"),
        P(None, "fsdp"),
        P("fsdp"),
        P("fsdp", None),
        P("fsdp"),
    )
    per_device = block_shards if fits(mesh) else shards
    return jax.shard_map(per_device, mesh=mesh, in_specs=in_specs, out_specs=out_specs, check_vma=False)
```

```python
import math

import jax
import jax.numpy as jnp
from jax import lax
from jax.experimental import pallas as pl
from jax.experimental.pallas import tpu as pltpu
from jax.sharding import PartitionSpec as P
import numpy as np

HEADS = 12
HEAD_DIM = 64
ROT_DIMS = 16


def layer_norm(values, norm_gain, norm_shift):
    center = values - jnp.mean(values, axis=-1, keepdims=True)
    spread = jnp.mean(center * center, axis=-1, keepdims=True)
    return center * lax.rsqrt(spread + 1e-05) * norm_gain + norm_shift


def exact_gelu(values):
    return jax.nn.gelu(values, approximate=False)


def stored_positions(rows, devices):
    row_order = jnp.arange(rows * devices, dtype=jnp.int32)
    device = row_order // rows
    within = row_order % rows
    half_rows = rows // 2
    return jnp.where(
        within < half_rows,
        device * half_rows + within,
        (2 * devices - 1 - device) * half_rows + within - half_rows,
    )


def rotary_angles(positions):
    half_rot = ROT_DIMS // 2
    inverse = jnp.power(10000.0, -2.0 * jnp.arange(half_rot, dtype=jnp.float32) / ROT_DIMS)
    return positions.astype(jnp.float32)[:, None] * inverse[None, :]


def rotate(heads, angles):
    half_rot = ROT_DIMS // 2
    cosine = jnp.cos(angles)[:, None, :]
    sine_part = jnp.sin(angles)[:, None, :]
    lower_half = heads[..., :half_rot]
    upper_half = heads[..., half_rot:ROT_DIMS]
    return jnp.concatenate(
        [
            lower_half * cosine - upper_half * sine_part,
            upper_half * cosine + lower_half * sine_part,
            heads[..., ROT_DIMS:],
        ],
        axis=-1,
    )


def to_order(stack, ctx_count, half_rows):
    tail = stack.shape[1:]
    shaped = stack.reshape((ctx_count, 2, half_rows) + tail)
    return jnp.concatenate(
        [shaped[:, 0].reshape((-1,) + tail), shaped[::-1, 1].reshape((-1,) + tail)], axis=0
    )


def from_order(stack, ctx_count, half_rows):
    tail = stack.shape[1:]
    middle = stack.shape[0] // 2
    first = stack[:middle].reshape((ctx_count, half_rows) + tail)
    second = stack[middle:].reshape((ctx_count, half_rows) + tail)[::-1]
    return jnp.stack([first, second], axis=1).reshape(stack.shape)


def scores_block(query_heads, key_heads, query_pos, key_pos):
    scores = jnp.einsum(
        "qhd,khd->hqk", query_heads, key_heads, preferred_element_type=jnp.float32
    ) / math.sqrt(HEAD_DIM)
    return jnp.where(key_pos[None, None, :] <= query_pos[None, :, None], scores, -1000000000.0)


def grad_block(
    query_heads, grad_heads, log_total, inner, query_pos, key_heads, value_heads, key_pos
):
    scores = scores_block(query_heads, key_heads, query_pos, key_pos)
    probability = jnp.exp(scores - log_total[:, :, None])
    prob_grad = jnp.einsum(
        "qhd,khd->hqk", grad_heads, value_heads, preferred_element_type=jnp.float32
    )
    score_grad = (probability * (prob_grad - inner[:, :, None])).astype(jnp.bfloat16)
    return (probability.astype(jnp.bfloat16), score_grad)


def shards(
    tokens,
    cotangent,
    att_gain,
    att_shift,
    ffn_gain,
    ffn_shift,
    qkv_weight,
    qkv_bias,
    out_weight,
    out_bias,
    up_weight,
    up_bias,
    down_weight,
    down_bias,
):
    model_width = tokens.shape[-1]
    rows_in = tokens.reshape(-1, model_width)
    grad_rows = cotangent.reshape(-1, model_width)
    own_rows = rows_in.shape[0]
    half_rows = own_rows // 2
    ctx_count = lax.axis_size("ctx")
    ctx_place = lax.axis_index("ctx")
    total_rows = own_rows * ctx_count
    all_pos = stored_positions(own_rows, ctx_count)
    own_pos = lax.dynamic_slice_in_dim(all_pos, ctx_place * own_rows, own_rows, 0)
    (
        gain_attend,
        shift_attend,
        gain_feed,
        shift_feed,
        mat_qkv,
        bias_qkv,
        mat_out,
        bias_out,
        bias_down,
    ) = (
        lax.all_gather(att_gain, "fsdp", axis=0, tiled=True),
        lax.all_gather(att_shift, "fsdp", axis=0, tiled=True),
        lax.all_gather(ffn_gain, "fsdp", axis=0, tiled=True),
        lax.all_gather(ffn_shift, "fsdp", axis=0, tiled=True),
        lax.all_gather(qkv_weight, "fsdp", axis=0, tiled=True),
        lax.all_gather(qkv_bias, "fsdp", axis=0, tiled=True),
        lax.all_gather(out_weight, "fsdp", axis=0, tiled=True),
        lax.all_gather(out_bias, "fsdp", axis=0, tiled=True),
        lax.all_gather(down_bias, "fsdp", axis=0, tiled=True),
    )
    tokens32 = rows_in.astype(jnp.float32)
    grad32 = grad_rows.astype(jnp.float32)
    first_norm, first_back = jax.vjp(
        layer_norm, tokens32, gain_attend.astype(jnp.float32), shift_attend.astype(jnp.float32)
    )
    second_norm, second_back = jax.vjp(
        layer_norm, tokens32, gain_feed.astype(jnp.float32), shift_feed.astype(jnp.float32)
    )
    first_in = first_norm.astype(jnp.bfloat16)
    second_in = second_norm.astype(jnp.bfloat16)
    joined = jnp.dot(first_in, mat_qkv, preferred_element_type=jnp.float32) + bias_qkv.astype(
        jnp.float32
    )
    angles = rotary_angles(own_pos)

    def project_heads(joined_rows):
        queries = rotate(joined_rows[:, :model_width].reshape(own_rows, HEADS, HEAD_DIM), angles)
        keys_rot = rotate(
            joined_rows[:, model_width : 2 * model_width].reshape(own_rows, HEADS, HEAD_DIM), angles
        )
        return (
            queries.reshape(own_rows, model_width),
            keys_rot.reshape(own_rows, model_width),
            joined_rows[:, 2 * model_width :],
        )

    (queries, keys_rot, values_rows), rotary_back = jax.vjp(project_heads, joined)
    query_low = queries.astype(jnp.bfloat16)
    key_low = keys_rot.astype(jnp.bfloat16)
    value_low = values_rows.astype(jnp.bfloat16)
    key_all, value_all = (
        lax.all_gather(key_low, "ctx", axis=0, tiled=True),
        lax.all_gather(value_low, "ctx", axis=0, tiled=True),
    )
    query_heads = query_low.reshape(own_rows, HEADS, HEAD_DIM)
    key_heads = to_order(key_all, ctx_count, half_rows).reshape(total_rows, HEADS, HEAD_DIM)
    value_heads = to_order(value_all, ctx_count, half_rows).reshape(total_rows, HEADS, HEAD_DIM)
    block_keys = min(1024, total_rows)

    def key_piece(block_index):
        start = block_index * block_keys
        return (
            lax.dynamic_slice_in_dim(key_heads, start, block_keys, 0),
            lax.dynamic_slice_in_dim(value_heads, start, block_keys, 0),
            start + jnp.arange(block_keys, dtype=jnp.int32),
        )

    need_low = (ctx_place + 1) * half_rows
    need_high = (2 * ctx_count - ctx_place) * half_rows
    counts = ((need_low + block_keys - 1) // block_keys, (need_high + block_keys - 1) // block_keys)
    query_parts = (query_heads[:half_rows], query_heads[half_rows:])
    pos_parts = (own_pos[:half_rows], own_pos[half_rows:])

    def half_lse(query_half, pos_half, count):

        def lse_step(block_index, carried):
            row_top, exp_total = carried
            key_block, value_skip, key_pos = key_piece(block_index)
            scores = scores_block(query_half, key_block, pos_half, key_pos)
            new_top = jnp.maximum(row_top, jnp.max(scores, axis=-1))
            exp_total = exp_total * jnp.exp(row_top - new_top) + jnp.sum(
                jnp.exp(scores - new_top[:, :, None]), axis=-1
            )
            return (new_top, exp_total)

        start_top = jnp.full((HEADS, half_rows), -1e30, jnp.float32)
        start_sum = jnp.zeros((HEADS, half_rows), jnp.float32)
        row_top, exp_total = lax.fori_loop(0, count, lse_step, (start_top, start_sum))
        return row_top + jnp.log(exp_total)

    lse_parts = [
        half_lse(query_parts[half_index], pos_parts[half_index], counts[half_index])
        for half_index in range(2)
    ]

    def half_mix(query_half, pos_half, lse_half, count):

        def mix_step(block_index, totals):
            key_block, value_block, key_pos = key_piece(block_index)
            scores = scores_block(query_half, key_block, pos_half, key_pos)
            probability = jnp.exp(scores - lse_half[:, :, None]).astype(jnp.bfloat16)
            return totals + jnp.einsum(
                "hqk,khd->qhd", probability, value_block, preferred_element_type=jnp.float32
            )

        return lax.fori_loop(
            0, count, mix_step, jnp.zeros((half_rows, HEADS, HEAD_DIM), jnp.float32)
        )

    attended = jnp.concatenate(
        [
            half_mix(
                query_parts[half_index],
                pos_parts[half_index],
                lse_parts[half_index],
                counts[half_index],
            )
            for half_index in range(2)
        ],
        axis=0,
    )
    attended_low = attended.reshape(own_rows, model_width).astype(jnp.bfloat16)
    branch_att = jnp.dot(
        attended_low, mat_out, preferred_element_type=jnp.float32
    ) + bias_out.astype(jnp.float32)
    second_all, grad_all = (
        lax.all_gather(second_in, "fsdp", axis=0, tiled=True),
        lax.all_gather(grad_rows, "fsdp", axis=0, tiled=True),
    )
    hidden = jnp.dot(second_all, up_weight, preferred_element_type=jnp.float32) + up_bias.astype(
        jnp.float32
    )
    active, gelu_back = jax.vjp(exact_gelu, hidden)
    active_low = active.astype(jnp.bfloat16)
    ffn_part = jnp.dot(active_low, down_weight, preferred_element_type=jnp.float32)
    active_grad = jnp.einsum("te,fe->tf", grad_all, down_weight, preferred_element_type=jnp.float32)
    hidden_grad = gelu_back(active_grad)[0].astype(jnp.bfloat16)
    down_dweight = jnp.einsum("tf,te->fe", active_low, grad_all, preferred_element_type=jnp.float32)
    up_dweight = jnp.einsum(
        "td,tf->df", second_all, hidden_grad, preferred_element_type=jnp.float32
    )
    up_dbias = jnp.sum(hidden_grad.astype(jnp.float32), axis=0)
    second_part = jnp.einsum(
        "tf,df->td", hidden_grad, up_weight, preferred_element_type=jnp.float32
    )
    ffn_sum, second_grad = (
        lax.psum_scatter(ffn_part, "fsdp", scatter_dimension=0, tiled=True),
        lax.psum_scatter(second_part, "fsdp", scatter_dimension=0, tiled=True),
    )
    branch_ffn = ffn_sum + bias_down.astype(jnp.float32)
    layer_out = (tokens32 + branch_att + branch_ffn).astype(jnp.bfloat16).reshape(tokens.shape)
    out_dweight = jnp.einsum(
        "td,te->de", attended_low, grad_rows, preferred_element_type=jnp.float32
    )
    row_sum = jnp.sum(grad32, axis=0)
    attended_grad = jnp.einsum(
        "te,de->td", grad_rows, mat_out, preferred_element_type=jnp.float32
    ).astype(jnp.bfloat16)
    grad_heads = attended_grad.reshape(own_rows, HEADS, HEAD_DIM)
    grad_parts = (grad_heads[:half_rows], grad_heads[half_rows:])

    def half_inner(query_half, grad_half, pos_half, lse_half, count):

        def inner_step(block_index, totals):
            key_block, value_block, key_pos = key_piece(block_index)
            scores = scores_block(query_half, key_block, pos_half, key_pos)
            probability = jnp.exp(scores - lse_half[:, :, None])
            prob_grad = jnp.einsum(
                "qhd,khd->hqk", grad_half, value_block, preferred_element_type=jnp.float32
            )
            return totals + jnp.sum(probability * prob_grad, axis=-1)

        return lax.fori_loop(0, count, inner_step, jnp.zeros((HEADS, half_rows), jnp.float32))

    inner_parts = [
        half_inner(
            query_parts[half_index],
            grad_parts[half_index],
            pos_parts[half_index],
            lse_parts[half_index],
            counts[half_index],
        )
        for half_index in range(2)
    ]
    half_zeros = jnp.zeros((half_rows, HEADS, HEAD_DIM), jnp.float32)

    def half_back(half_index, carried):
        query_half = query_parts[half_index]
        grad_half = grad_parts[half_index]

        def query_step(block_index, state):
            query_total, key_acc, value_acc = state
            key_block, value_block, key_pos = key_piece(block_index)
            prob_low, score_grad = grad_block(
                query_half,
                grad_half,
                lse_parts[half_index],
                inner_parts[half_index],
                pos_parts[half_index],
                key_block,
                value_block,
                key_pos,
            )
            key_part = jnp.einsum(
                "hqk,qhd->khd", score_grad, query_half, preferred_element_type=jnp.float32
            )
            value_part = jnp.einsum(
                "hqk,qhd->khd", prob_low, grad_half, preferred_element_type=jnp.float32
            )
            start = block_index * block_keys
            key_acc = lax.dynamic_update_slice_in_dim(
                key_acc,
                lax.dynamic_slice_in_dim(key_acc, start, block_keys, 0) + key_part,
                start,
                0,
            )
            value_acc = lax.dynamic_update_slice_in_dim(
                value_acc,
                lax.dynamic_slice_in_dim(value_acc, start, block_keys, 0) + value_part,
                start,
                0,
            )
            query_total = query_total + jnp.einsum(
                "hqk,khd->qhd", score_grad, key_block, preferred_element_type=jnp.float32
            )
            return (query_total, key_acc, value_acc)

        return lax.fori_loop(0, counts[half_index], query_step, carried)

    full_zeros = jnp.zeros((total_rows, HEADS, HEAD_DIM), jnp.float32)
    query_low_sum, key_acc, value_acc = half_back(0, (half_zeros, full_zeros, full_zeros))
    query_high_sum, key_acc, value_acc = half_back(1, (half_zeros, key_acc, value_acc))
    query_sum = jnp.concatenate([query_low_sum, query_high_sum], axis=0)
    key_stored = from_order(key_acc.reshape(total_rows, model_width), ctx_count, half_rows)
    value_stored = from_order(value_acc.reshape(total_rows, model_width), ctx_count, half_rows)
    key_sum, value_sum = (
        lax.psum_scatter(key_stored, "ctx", scatter_dimension=0, tiled=True),
        lax.psum_scatter(value_stored, "ctx", scatter_dimension=0, tiled=True),
    )
    query_grad = query_sum.reshape(own_rows, model_width) / math.sqrt(HEAD_DIM)
    key_grad = key_sum / math.sqrt(HEAD_DIM)
    joined_grad = rotary_back((query_grad, key_grad, value_sum))[0].astype(jnp.bfloat16)
    qkv_dweight = jnp.einsum("td,tf->df", first_in, joined_grad, preferred_element_type=jnp.float32)
    qkv_dbias = jnp.sum(joined_grad.astype(jnp.float32), axis=0)
    first_grad = jnp.einsum("tf,df->td", joined_grad, mat_qkv, preferred_element_type=jnp.float32)
    token_first, att_dgain, att_dshift = first_back(first_grad)
    token_second, ffn_dgain, ffn_dshift = second_back(second_grad)
    input_grad = (grad32 + token_first + token_second).reshape(tokens.shape)
    shares = (
        lax.psum_scatter(att_dgain, "fsdp", scatter_dimension=0, tiled=True),
        lax.psum_scatter(att_dshift, "fsdp", scatter_dimension=0, tiled=True),
        lax.psum_scatter(ffn_dgain, "fsdp", scatter_dimension=0, tiled=True),
        lax.psum_scatter(ffn_dshift, "fsdp", scatter_dimension=0, tiled=True),
        lax.psum_scatter(qkv_dweight, "fsdp", scatter_dimension=0, tiled=True),
        lax.psum_scatter(qkv_dbias, "fsdp", scatter_dimension=0, tiled=True),
        lax.psum_scatter(out_dweight, "fsdp", scatter_dimension=0, tiled=True),
        lax.psum_scatter(row_sum, "fsdp", scatter_dimension=0, tiled=True),
    ) + (up_dweight, up_dbias, down_dweight)
    totals = lax.psum(
        (
            shares[0],
            shares[1],
            shares[2],
            shares[3],
            shares[4],
            shares[5],
            shares[6],
            shares[7],
            shares[8],
            shares[9],
            shares[10],
        ),
        "ctx",
    )
    return (
        layer_out,
        input_grad,
        totals[0],
        totals[1],
        totals[2],
        totals[3],
        totals[4],
        totals[5],
        totals[6],
        totals[7],
        totals[8],
        totals[9],
        totals[10],
        totals[7],
    )


F32 = jnp.float32
BF16 = jnp.bfloat16
GROUPS = 4
GROUP_HEADS = HEADS // GROUPS
GROUP_COLS = GROUP_HEADS * HEAD_DIM
EXTRA = 16


def fits(mesh):
    return mesh.shape["ctx"] == 2 * GROUPS and mesh.shape["fsdp"] == GROUPS


def mm(left, right):
    return jnp.dot(left, right, preferred_element_type=F32)


def mm_nt(left, right):
    return lax.dot_general(left, right, (((1,), (1,)), ((), ())), preferred_element_type=F32)


def mm_tn(left, right):
    return lax.dot_general(left, right, (((0,), (0,)), ((), ())), preferred_element_type=F32)


def local_call(
    name, body, places, ins, outs, scratch=(), flops=0, whole=(), after=(), through=(), vmem=28
):
    waits = len(after) + len(through)
    inner, first, last = body, 1 + waits, 1 + waits + len(ins) + len(whole)

    def body(*refs):
        given = refs[first:last]
        given = given[len(whole) :][::-1] + given[: len(whole)][::-1]
        made = refs[last : last + len(outs)]
        inner(refs[0], *given, *made, *refs[last + len(outs) + len(through) :])

    moved = sum(math.prod(i.shape) * i.dtype.itemsize for i in ins)
    moved += sum(math.prod(s) * jnp.dtype(d).itemsize for s, d in outs)
    return pl.pallas_call(
        body,
        out_shape=[jax.ShapeDtypeStruct(s, d) for s, d in outs]
        + [jax.ShapeDtypeStruct(t.shape, t.dtype) for t in through],
        in_specs=[pl.BlockSpec(memory_space=pltpu.SMEM)]
        + [pl.BlockSpec(memory_space=pl.ANY)] * (waits + len(whole))
        + [pl.BlockSpec(memory_space=pltpu.VMEM)] * len(ins),
        out_specs=[pl.BlockSpec(memory_space=pltpu.VMEM)] * len(outs)
        + [pl.BlockSpec(memory_space=pl.ANY)] * len(through),
        input_output_aliases={1 + len(after) + i: len(outs) + i for i in range(len(through))},
        scratch_shapes=list(scratch),
        compiler_params=pltpu.CompilerParams(vmem_limit_bytes=vmem * 2**20),
        cost_estimate=pl.CostEstimate(flops=flops, bytes_accessed=moved, transcendentals=0),
        name=name,
    )(places, *after, *through, *whole[::-1], *ins[::-1])


def normed(values):
    center = values - jnp.mean(values, axis=-1, keepdims=True)
    spread = jnp.mean(center * center, axis=-1, keepdims=True)
    scale = lax.rsqrt(spread + 1e-05)
    return center * scale, scale


def rotary_tables(rows, devices):
    half = rows // 2
    order = np.arange(rows * devices)
    device, within = order // rows, order % rows
    position = np.where(
        within < half, device * half + within, (2 * devices - 1 - device) * half + within - half
    )
    pairs = ROT_DIMS // 2
    inverse = np.power(10000.0, -2.0 * np.arange(pairs) / ROT_DIMS).astype(np.float32)
    angle = (position.astype(np.float32)[:, None] * inverse[None, :]).astype(np.float32)
    cosine = np.ones((rows * devices, HEAD_DIM), np.float32)
    sine = np.zeros((rows * devices, HEAD_DIM), np.float32)
    cosine[:, :pairs] = cosine[:, pairs:ROT_DIMS] = np.cos(angle)
    sine[:, :pairs] = -np.sin(angle)
    sine[:, pairs:ROT_DIMS] = np.sin(angle)
    return np.tile(cosine, (1, 2)), np.tile(sine, (1, 2))


def swapped(values):
    lanes = values.shape[1]
    place = lax.broadcasted_iota(jnp.int32, values.shape, 1) % HEAD_DIM
    return jnp.where(
        place < ROT_DIMS // 2,
        pltpu.roll(values, lanes - ROT_DIMS // 2, 1),
        pltpu.roll(values, ROT_DIMS // 2, 1),
    )


def pack_body(places, *refs):
    vectors, (qkv_w, x, g, out_w) = refs[0:7], refs[7:11]
    payload, xg, xg_line, out_half, box, rows_w, sems = refs[11:]
    core, group = places[0] % 2, places[0] // 2
    part = rows_w.shape[0]
    width = xg.shape[1]
    rows = x.shape[0]
    copies = [
        pltpu.make_async_copy(
            qkv_w.at[pl.ds(pl.multiple_of(core * part, part), part), :], rows_w, sems.at[0]
        ),
        pltpu.make_async_copy(x, xg.at[pl.ds(0, rows), :], sems.at[1]),
        pltpu.make_async_copy(g, xg.at[pl.ds(rows, rows), :], sems.at[2]),
        pltpu.make_async_copy(
            out_w.at[pl.ds(pl.multiple_of(core * part, part), part), :], out_half, sems.at[3]
        ),
        pltpu.make_async_copy(x, xg_line.at[pl.ds(0, rows), :], sems.at[4]),
        pltpu.make_async_copy(g, xg_line.at[pl.ds(rows, rows), :], sems.at[5]),
    ]
    for copy in copies:
        copy.start()
    box[...] = jnp.zeros_like(box)
    shard = vectors[0].shape[0]
    for item in range(6):
        box[item // 3 : item // 3 + 1, (item % 3) * shard : (item % 3 + 1) * shard] = (
            vectors[item][...].astype(F32).reshape(1, shard)
        )
    box[2:3, :] = vectors[6][...].astype(F32).reshape(1, 3 * shard)
    payload[part:, :] = box[...].astype(BF16)
    copies[0].wait()
    for owner in range(GROUPS):

        @pl.when(group == owner)
        def _():
            for slot, base in enumerate((1, 0, 2)):
                at = base * width + owner * GROUP_COLS
                payload[0:part, slot * GROUP_COLS : (slot + 1) * GROUP_COLS] = rows_w[
                    :, at : at + GROUP_COLS
                ]

    for copy in copies[1:]:
        copy.wait()


def collect_body(places, p0, p1, p2, p3, stack, vec, bias, box):
    z, group = places[1], places[0] // 2
    part = p0.shape[0] - EXTRA
    three = p0.shape[1]
    shard = vec.shape[1] // GROUPS
    for k, piece in enumerate((p0, p1, p2, p3)):
        stack[k * part : (k + 1) * part, :] = piece[0:part, :]
        box[z ^ k] = piece[part:, :].astype(F32)
    units = []
    for owner in range(GROUPS):
        block = box[owner]
        for item in range(6):
            vec[item : item + 1, owner * shard : (owner + 1) * shard] = block[
                item // 3 : item // 3 + 1, (item % 3) * shard : (item % 3 + 1) * shard
            ]
        for unit in range(3):
            units.append(block[2:3, unit * GROUP_COLS : (unit + 1) * GROUP_COLS])
    for slot, base in enumerate((GROUPS, 0, 2 * GROUPS)):
        own = units[base]
        for g in range(1, GROUPS):
            own = jnp.where(group == g, units[base + g], own)
        bias[0:1, slot * GROUP_COLS : (slot + 1) * GROUP_COLS] = own


def qkv_body(places, *refs):
    xs, (near, far, vec, bias, cos_tab, sin_tab) = refs[0:4], refs[4:10]
    fi, w, q_out, kv_out, cos, sin = refs[10:]
    c, z = places[0], places[1]
    core = c % 2
    width = w.shape[0]
    shard = width // GROUPS
    part = shard // 2
    rows = xs[0].shape[0] // 2
    half = rows // 2
    near_rows = GROUPS * rows
    for side, stack in ((core, near), (1 - core, far)):
        for k in range(GROUPS):
            base = (z ^ k) * shard + side * part
            w[pl.ds(pl.multiple_of(base, part), part), :] = stack[k * part : (k + 1) * part, :]
    gain, shift = vec[0:1, :], vec[1:2, :]
    two = 2 * GROUP_COLS
    for side in range(2):
        for j in range(GROUPS):
            source = c ^ (2 * j)
            to = slice((side * GROUPS + j) * half, (side * GROUPS + j + 1) * half)
            at = pl.ds(pl.multiple_of(source * rows + side * half, half), half)
            norm, _ = normed(xs[j][side * half : (side + 1) * half, :].astype(F32))
            fi[to, :] = (norm * gain + shift).astype(BF16)
            cos[to, :] = cos_tab[at, :]
            sin[to, :] = sin_tab[at, :]
    step = 2 * rows
    for i in range(near_rows // step):
        at = slice(i * step, (i + 1) * step)
        chunk = fi[at, :]
        kq = mm(chunk, w[:, :two]) + bias[0:1, :two]
        c3 = jnp.concatenate([cos[at, :]] * 3, axis=1)
        s3 = jnp.concatenate([sin[at, :]] * 3, axis=1)
        kq = kq * c3 + swapped(kq) * s3
        kv_out[at, :] = kq[:, :GROUP_COLS].astype(BF16)
        q_out[at, :] = (kq[:, GROUP_COLS:] * HEAD_DIM**-0.5).astype(BF16)
        kv_out[near_rows + i * step : near_rows + (i + 1) * step, :] = (
            mm(chunk, w[:, two:]) + bias[0:1, two:]
        ).astype(BF16)


def key_order(kv, kv_far, kbuf, vbuf, low):
    near_rows = 2 * low
    for side in range(2):
        for part, source in enumerate((kv, kv_far)):
            to = slice((2 * side + part) * low, (2 * side + part + 1) * low)
            kbuf[to, :] = source[side * low : (side + 1) * low, :]
            vbuf[to, :] = source[near_rows + side * low : near_rows + (side + 1) * low, :]


def visible(c, low):
    half = low // GROUPS
    devices = 2 * GROUPS

    def token_pos(index, far):
        device = (c ^ (2 * (index // half))) ^ far
        return device * half + index % half

    q_place = token_pos(lax.broadcasted_iota(jnp.int32, (low, 1), 0), 0)
    k_index = lax.broadcasted_iota(jnp.int32, (1, 2 * low), 1)
    k_place = token_pos(k_index % low, k_index // low)

    def mirrored(place):
        return (2 * devices - 1 - place // half) * half + place % half

    return (k_place <= q_place, mirrored(k_place) <= mirrored(q_place))


def masked_scores(query, keys, side, spans, allowed):
    scores = [mm_nt(query, keys[s]) for s in spans]
    scores[-1] = jnp.where(allowed[side], scores[-1], -1000000000.0)
    return scores


def key_spans(side, low):
    return [slice(0, 2 * low), slice(2 * low, 4 * low)][: side + 1]


def attend_body(places, *refs):
    q, kv, kv_far = refs[0:3]
    xgs, (ow_near, ow_far) = refs[3:7], refs[7:9]
    sends, (dkq, dv_out, far_out) = refs[9:13], refs[13:16]
    kbuf, vbuf, att, ag, ow, g_half, pieces = refs[16:]
    c, z = places[0], places[1]
    core = c % 2
    rows = sends[0].shape[0]
    near_rows = GROUPS * rows
    half = rows // 2
    low = GROUPS * half
    part = GROUP_COLS // 2
    key_order(kv, kv_far, kbuf, vbuf, low)
    ow[pl.ds(pl.multiple_of(core * part, part), part), :] = ow_near[...]
    ow[pl.ds(pl.multiple_of((1 - core) * part, part), part), :] = ow_far[...]
    for side in range(2):
        for j in range(GROUPS):
            g_half[(side * GROUPS + j) * half : (side * GROUPS + j + 1) * half, :] = xgs[j][
                rows + side * half : rows + (side + 1) * half, :
            ]
    ag[...] = mm_nt(g_half[...], ow[...]).astype(BF16)
    allowed = visible(c, low)
    for head in range(GROUP_HEADS):
        lanes = slice(head * HEAD_DIM, (head + 1) * HEAD_DIM)
        lanes2 = slice(GROUP_COLS + head * HEAD_DIM, GROUP_COLS + (head + 1) * HEAD_DIM)
        kh, vh = kbuf[:, lanes], vbuf[:, lanes]
        dk_parts, dv_parts = [], []
        for side in range(2):
            at = slice(side * low, (side + 1) * low)
            qh, gh = q[at, lanes], ag[at, lanes]
            spans = [slice(0, 2 * low), slice(2 * low, 4 * low)][: side + 1]
            scores = [mm_nt(qh, kh[s]) for s in spans]
            scores[-1] = jnp.where(allowed[side], scores[-1], -1000000000.0)
            top = jnp.max(scores[0], axis=-1, keepdims=True)
            for s in scores[1:]:
                top = jnp.maximum(top, jnp.max(s, axis=-1, keepdims=True))
            raised = [jnp.exp(s - top) for s in scores]
            inverse = 1.0 / sum(jnp.sum(r, axis=-1, keepdims=True) for r in raised)
            probs = [r * inverse for r in raised]
            low_probs = [p.astype(BF16) for p in probs]
            mixed = sum(mm(p, vh[s]) for p, s in zip(low_probs, spans))
            att[at, lanes] = mixed.astype(BF16)
            prob_grads = [mm_nt(gh, vh[s]) for s in spans]
            inner = sum(
                jnp.sum(p * d, axis=-1, keepdims=True) for p, d in zip(probs, prob_grads)
            )
            score_grads = [(p * (d - inner)).astype(BF16) for p, d in zip(probs, prob_grads)]
            dkq[at, lanes2] = sum(mm(s, kh[a]) for s, a in zip(score_grads, spans)) * HEAD_DIM**-0.5
            dk_parts.append([mm_tn(s, qh) for s in score_grads])
            dv_parts.append([mm_tn(p, gh) for p in low_probs])
        dk = (dk_parts[0][0] + dk_parts[1][0], dk_parts[1][1])
        dv = (dv_parts[0][0] + dv_parts[1][0], dv_parts[1][1])
        for side in range(2):
            at = slice(side * low, (side + 1) * low)
            dkq[at, lanes] = dk[side][:low]
            dv_out[at, lanes] = dv[side][:low]
            far_out[at, lanes] = dk[side][low:].astype(BF16)
            far_out[at, lanes2] = dv[side][low:].astype(BF16)
    for side in range(2):
        for j in range(GROUPS):
            pieces[j, side * half : (side + 1) * half, :] = att[
                (side * GROUPS + j) * half : (side * GROUPS + j + 1) * half, :
            ]
    for m in range(GROUPS):
        sends[m][...] = pieces[(c // 2) ^ z ^ m]


def joined_body(places, *refs):
    dkq, dv, far, w, fi, cos, sin, vec = refs[0:8]
    xs, g_own = refs[8:12], refs[12]
    ca, sends, keep, send = refs[13], refs[14:17], refs[17], refs[18]
    jgkq, jgv, dwbuf, first, ext = refs[19:]
    c, z = places[0], places[1]
    core, group = c % 2, c // 2
    rows = ca.shape[0]
    half = rows // 2
    width = w.shape[0]
    shard = width // GROUPS
    part = shard // 2
    two = 2 * GROUP_COLS
    step = 2 * rows
    gain = vec[0:1, :]
    bias_kq = jnp.zeros((1, two), F32)
    bias_v = jnp.zeros((1, GROUP_COLS), F32)
    for i in range(GROUPS * rows // step):
        at = slice(i * step, (i + 1) * step)
        other = far[at, :].astype(F32)
        dk = dkq[at, :GROUP_COLS] + other[:, :GROUP_COLS]
        kq = jnp.concatenate([dk, dkq[at, GROUP_COLS:]], axis=1)
        c3 = jnp.concatenate([cos[at, :]] * 3, axis=1)
        s3 = jnp.concatenate([sin[at, :]] * 3, axis=1)
        low_kq = (kq * c3 - swapped(kq) * s3).astype(BF16)
        low_v = (dv[at, :] + other[:, GROUP_COLS:]).astype(BF16)
        jgkq[at, :] = low_kq
        jgv[at, :] = low_v
        bias_kq += jnp.sum(low_kq.astype(F32), axis=0, keepdims=True)
        bias_v += jnp.sum(low_v.astype(F32), axis=0, keepdims=True)
        first[at, :] = mm_nt(low_kq, w[:, :two]) + mm_nt(low_v, w[:, two:])
    dgain = jnp.zeros((1, width), F32)
    dshift = jnp.zeros((1, width), F32)
    for side in range(2):
        for j in range(GROUPS):
            at = slice((side * GROUPS + j) * half, (side * GROUPS + j + 1) * half)
            mine = slice(side * half, (side + 1) * half)
            norm, _ = normed(xs[j][mine, :].astype(F32))
            grad = first[at, :]
            dgain += jnp.sum(grad * norm, axis=0, keepdims=True)
            dshift += jnp.sum(grad, axis=0, keepdims=True)
            if j == 0:
                ca[mine, :] = grad * gain
            else:
                sends[j - 1][mine, :] = (grad * gain).astype(BF16)
    gsum = jnp.sum(g_own[...].astype(F32), axis=0, keepdims=True)
    dwbuf[:, :two] = mm_tn(fi[...], jgkq[...])
    dwbuf[:, two:] = mm_tn(fi[...], jgv[...])
    ext[...] = jnp.zeros_like(ext)
    for owner in range(GROUPS):
        own = slice(owner * shard, (owner + 1) * shard)
        for slot in range(3):
            unit = owner * 3 + slot
            kind = unit // GROUPS
            vector = (bias_kq[:, GROUP_COLS:], bias_kq[:, :GROUP_COLS], bias_v)[kind]
            to = slice(slot * GROUP_COLS, (slot + 1) * GROUP_COLS)
            ext[owner, 0:1, to] = jnp.where(group == unit % GROUPS, vector, 0.0)
        for slot, vector in enumerate((dgain[:, own], dshift[:, own], gsum[:, own])):
            ext[owner, 1:2, slot * shard : (slot + 1) * shard] = vector
    for k in range(GROUPS):
        owner = z ^ k
        base = owner * shard
        keep[k, 0:part, :] = dwbuf[pl.ds(pl.multiple_of(base + core * part, part), part), :]
        send[k, 0:part, :] = dwbuf[
            pl.ds(pl.multiple_of(base + (1 - core) * part, part), part), :
        ].astype(BF16)
        keep[k, part:, :] = ext[owner].astype(BF16).astype(F32)
        send[k, part:, :] = ext[owner].astype(BF16)


def ffn_pair_body(places, keep, got, c1, c2, c3, own, *sends):
    chunk = own.shape[0]
    for j in range(GROUPS):
        total = keep[j * chunk : (j + 1) * chunk, :] + got[j * chunk : (j + 1) * chunk, :].astype(F32)
        if j == 0:
            own[...] = total
        else:
            sends[j - 1][0:chunk, :] = total.astype(BF16)
            sends[j - 1][chunk:, :] = (c1, c2, c3)[j - 1][...]


def qkv_pair_body(places, keep, got, sums, sums_far, own, *rest):
    sends, ext = rest[:-1], rest[-1]
    z = places[1]
    part = own.shape[0] - EXTRA
    first = sums_far.shape[0] - EXTRA
    vector = sums[...].astype(F32) + sums_far[first:, :].astype(F32)
    shard = vector.shape[1] // GROUPS
    ext[...] = jnp.zeros_like(ext)
    for owner in range(GROUPS):
        at = slice(owner * shard, (owner + 1) * shard)
        here = z == owner
        ext[owner, 2:3, 0:shard] = vector[0:1, at]
        ext[owner, 2:3, shard : 2 * shard] = vector[1:2, at]
        ext[owner, 2:3, 2 * shard : 3 * shard] = jnp.where(here, vector[2:3, 0:shard], 0.0)
        ext[owner, 3:4, :] = jnp.where(here, vector[2:3, shard:], 0.0)
    for k in range(GROUPS):
        total = keep[k] + got[k].astype(F32)
        tail = total[part:, :] + ext[z ^ k]
        if k == 0:
            own[0:part, :] = total[0:part, :]
            own[part:, :] = tail
        else:
            sends[k - 1][0:part, :] = total[0:part, :].astype(BF16)
            sends[k - 1][part:, :] = tail.astype(BF16)


def ffn_sum_body(places, own, a, b, c, qkv, out):
    rows = own.shape[0]
    total = own[...]
    for piece in (a, b, c):
        total += piece[0:rows, :].astype(F32)
    out[0:rows, :] = total.astype(BF16)
    most = qkv.shape[0] - 2 * EXTRA
    block = qkv.shape[1] // 3
    out[rows:, :] = jnp.zeros((out.shape[0] - rows, 4 * block), BF16)
    out[rows : rows + most, 0 : 3 * block] = qkv[0:most, :]
    for i in range(3):
        out[rows + i * EXTRA : rows + (i + 1) * EXTRA, 3 * block :] = qkv[
            most : most + EXTRA, i * block : (i + 1) * block
        ]
    out[rows + most :, 0 : 3 * block] = qkv[most + EXTRA :, :]


def sum_body(places, own, a, b, c, out):
    out[...] = (own[...] + a[...].astype(F32) + b[...].astype(F32) + c[...].astype(F32)).astype(
        out.dtype
    )


def ffn_body(places, *refs):
    line = refs[0:6]
    up_w, down_w, up_b, vec, out_w = refs[6:11]
    atts = refs[11:15]
    outs = refs[15:19]
    sums, si, gb, active, hidden_grad, att = refs[19:25]
    second, norms = refs[25:]
    c, z = places[0], places[1]
    rows = line[0].shape[0] // 2
    width = up_w.shape[0]
    hid = up_w.shape[1]
    gain, shift = vec[2:3, :], vec[3:4, :]
    for k in range(GROUPS):
        at = slice(k * rows, (k + 1) * rows)
        if k == 0:
            piece = line[0]
        elif k == 2:
            piece = line[2][...] + line[5][...]
        else:
            ends = line[3][...]
            here = z == (0 if k == 1 else GROUPS - 1)
            piece = line[1 if k == 1 else 4][...] + jnp.where(here, ends, jnp.zeros_like(ends))
        norm, _ = normed(piece[0:rows, :].astype(F32))
        norms[at, :] = norm
        si[at, :] = (norm * gain + shift).astype(BF16)
        gb[at, :] = piece[rows:, :]
    for m in range(GROUPS):
        slot = (z - ((c // 2) ^ m)) % GROUPS
        att[pl.ds(pl.multiple_of(slot * rows, rows), rows), :] = atts[m][...]
    step = 2 * rows
    bias_sum = jnp.zeros((1, hid), F32)
    for i in range(GROUPS * rows // step):
        at = slice(i * step, (i + 1) * step)
        hidden = mm(si[at, :], up_w[...]) + up_b[...].astype(F32)
        cdf = 0.5 + 0.5 * lax.erf(hidden * (0.5**0.5))
        density = jnp.exp(hidden * hidden * -0.5) * (1.0 / math.sqrt(2.0 * math.pi))
        active[at, :] = (hidden * cdf).astype(BF16)
        grad = (mm_nt(gb[at, :], down_w[...]) * (cdf + hidden * density)).astype(BF16)
        hidden_grad[at, :] = grad
        bias_sum += jnp.sum(grad.astype(F32), axis=0, keepdims=True)
        part = mm(active[at, :], down_w[...]) + mm(att[at, :], out_w[...])
        second[at, :] = mm_nt(grad, up_w[...])
        for k in range(2):
            piece = outs[2 * i + k]
            piece[0:rows, :] = part[k * rows : (k + 1) * rows, :].astype(piece.dtype)
    dgain = jnp.zeros((1, width), F32)
    dshift = jnp.zeros((1, width), F32)
    for k in range(GROUPS):
        at = slice(k * rows, (k + 1) * rows)
        norm = norms[at, :]
        grad = second[at, :]
        dgain += jnp.sum(grad * norm, axis=0, keepdims=True)
        dshift += jnp.sum(grad, axis=0, keepdims=True)
        outs[k][rows:, :] = (grad * gain).astype(outs[k].dtype)
    row = lax.broadcasted_iota(jnp.int32, sums.shape, 0)
    vectors = jnp.where(row == 0, dgain, jnp.where(row == 1, dshift, bias_sum))
    sums[...] = jnp.where(row < 3, vectors, 0.0).astype(BF16)


def ffn_dw_body(places, si, gb, active, hidden_grad, att, sums, keep, send, dwbuf):
    c = places[0]
    width, hid, shard = si.shape[1], active.shape[1], att.shape[1]
    dwbuf[0:width, :] = mm_tn(si[...], hidden_grad[...])
    dwbuf[width : width + hid, :] = mm_tn(active[...], gb[...])
    dwbuf[width + hid : width + hid + shard, :] = mm_tn(att[...], gb[...])
    dwbuf[width + hid + shard :, :] = jnp.zeros_like(dwbuf[width + hid + shard :, :])
    chunk = dwbuf.shape[0] // (2 * GROUPS)
    for j in range(GROUPS):
        to = slice(j * chunk, (j + 1) * chunk)
        near = c ^ (2 * j)
        keep[to, :] = dwbuf[pl.ds(pl.multiple_of(near * chunk, chunk), chunk), :]
        far = near ^ 1
        send[to, :] = dwbuf[pl.ds(pl.multiple_of(far * chunk, chunk), chunk), :].astype(BF16)
    send[GROUPS * chunk :, :] = sums[...]


def stack_body(places, a, b, c, d, out):
    rows = a.shape[0]
    for j, piece in enumerate((a, b, c, d)):
        out[j * rows : (j + 1) * rows, :] = piece[...]


def spread_body(places, near, far, *refs):
    up_dw, down_dw, out_dw, qkv_dw, v0, v1, v2, v3, v4, up_db, bias, buf, box, qkv_box = refs
    c = places[0]
    core, group = c % 2, c // 2
    shard = out_dw.shape[0]
    part = shard // 2
    rows = near.shape[0] // GROUPS
    chunk = rows - part
    most = part - EXTRA
    three = 3 * GROUP_COLS
    for j in range(GROUPS):
        for side, stack in ((core, near), (1 - core, far)):
            place = 2 * (group ^ j) + side
            base = j * rows
            buf[pl.ds(pl.multiple_of(place * chunk, chunk), chunk), :] = stack[
                base : base + chunk, :
            ].astype(F32)
            base += chunk
            at = pl.multiple_of(side * part, part)
            qkv_box[group ^ j, pl.ds(at, most), :] = stack[base : base + most, 0:three].astype(F32)
            for i in range(3):
                qkv_box[
                    group ^ j,
                    pl.ds(pl.multiple_of(at + most, EXTRA), EXTRA),
                    i * GROUP_COLS : (i + 1) * GROUP_COLS,
                ] = stack[base + i * EXTRA : base + (i + 1) * EXTRA, three:].astype(F32)
        box[group ^ j] = near[j * rows + chunk + most : (j + 1) * rows, 0:three].astype(F32)
    last = up_dw.shape[0] + down_dw.shape[0]
    up_dw[...] = buf[0 : up_dw.shape[0], :]
    down_dw[...] = buf[up_dw.shape[0] : last, :]
    out_dw[...] = buf[last : last + shard, :]
    for g in range(GROUPS):
        for kind, slot in enumerate((1, 0, 2)):
            at = (kind * GROUPS + g) * GROUP_COLS
            qkv_dw[:, at : at + GROUP_COLS] = qkv_box[
                g, :, slot * GROUP_COLS : (slot + 1) * GROUP_COLS
            ]
    total = box[0] + box[1] + box[2] + box[3]
    bias[...] = total[0:1, :].reshape(three)
    for slot, vec in enumerate((v0, v1, v2)):
        vec[...] = total[1:2, slot * shard : (slot + 1) * shard].reshape(shard)
    v3[...] = total[2:3, 0:shard].reshape(shard)
    v4[...] = total[2:3, shard : 2 * shard].reshape(shard)
    up_db[...] = jnp.concatenate([total[2:3, 2 * shard :], total[3:4, :]], axis=1).reshape(4 * shard)


def token_body(places, xg, vec, ca, ffn, *refs):
    from_plane, from_line = refs[0:3], refs[3:6]
    layer_out, input_grad = refs[6:]
    rows = ca.shape[0]
    values = xg[0:rows, :].astype(F32)
    total = values + vec[4:5, :] + vec[5:6, :] + ffn[0:rows, :]
    cot = ca[...] + ffn[rows:, :]
    for piece in from_plane:
        cot += piece[piece.shape[0] - rows :, :].astype(F32)
    for piece in from_line:
        total += piece[0:rows, :].astype(F32)
        cot += piece[rows:, :].astype(F32)
    layer_out[...] = total.astype(BF16)
    norm, scale = normed(values)
    shifted = cot - jnp.mean(cot, axis=-1, keepdims=True)
    shifted -= norm * jnp.mean(cot * norm, axis=-1, keepdims=True)
    input_grad[...] = xg[rows:, :].astype(F32) + scale * shifted


def block_shards(
    tokens,
    cotangent,
    att_gain,
    att_shift,
    ffn_gain,
    ffn_shift,
    qkv_weight,
    qkv_bias,
    out_weight,
    out_bias,
    up_weight,
    up_bias,
    down_weight,
    down_bias,
):
    width = tokens.shape[-1]
    x = tokens.reshape(-1, width)
    g = cotangent.reshape(-1, width)
    rows = x.shape[0]
    n_ctx, n_z = lax.axis_size("ctx"), lax.axis_size("fsdp")
    c, z = lax.axis_index("ctx"), lax.axis_index("fsdp")
    group = c // 2
    shard = width // n_z
    part = shard // 2
    hid = up_weight.shape[1]
    places = jnp.stack([c, z]).astype(jnp.int32)
    three = 3 * GROUP_COLS
    near_rows = GROUPS * rows
    pair = 2 * rows

    def over_ctx(value, k):
        return lax.ppermute(value, "ctx", [(i, i ^ k) for i in range(n_ctx)])

    def over_z(value, k):
        return lax.ppermute(value, "fsdp", [(i, i ^ k) for i in range(n_z)])

    def around_z(value, k):
        return lax.ppermute(value, "fsdp", [(i, (i + k) % n_z) for i in range(n_z)])

    def along_z(value, k, first):
        pairs = [(i, i + 1) for i in range(first, n_z - 1)]
        if k < 0:
            pairs = [(n_z - 1 - a, n_z - 1 - b) for a, b in pairs]
        return lax.ppermute(value, "fsdp", pairs)

    def over_both(value, pairs):
        return lax.ppermute(
            value, ("ctx", "fsdp"), [(a * n_z + b, d * n_z + e) for a, b, d, e in pairs]
        )

    def chips(value):
        return [value] + [over_ctx(value, 2 * j) for j in range(1, GROUPS)]

    payload, xg, xg_line, out_half = local_call(
        "pack",
        pack_body,
        places,
        [att_gain, att_shift, ffn_gain, ffn_shift, out_bias, down_bias, qkv_bias],
        [((part + EXTRA, three), BF16)] + [((pair, width), BF16)] * 2 + [((part, width), BF16)],
        [
            pltpu.VMEM((EXTRA, three), F32),
            pltpu.VMEM((part, 3 * width), BF16),
            pltpu.SemaphoreType.DMA((6,)),
        ],
        whole=[qkv_weight, x, g, out_weight],
        vmem=60,
    )
    near_w = [payload] + [over_z(payload, k) for k in range(1, n_z)]
    plane = chips(xg)
    by_place = [(a, b, a, b ^ (a // 2)) for a in range(n_ctx) for b in range(n_z)]
    by_plane = [(a, b, a ^ (2 * b), b) for a in range(n_ctx) for b in range(n_z)]
    ow_first = over_both(out_half, by_place)
    ow_near = over_both(ow_first, by_plane)
    stack, vec, bias, xg_line = local_call(
        "collect",
        collect_body,
        places,
        near_w,
        [((GROUPS * part, three), BF16), ((8, width), F32), ((8, three), F32)],
        [pltpu.VMEM((GROUPS, EXTRA, three), F32)],
        after=plane[1:],
        through=[xg_line],
    )
    up, down = [xg_line], [xg_line]
    for i in range(n_z - 2):
        up.append(along_z(up[-1], 1, i))
        down.append(along_z(down[-1], -1, i))
    ends = lax.ppermute(up[-1] + down[-1], "fsdp", [(n_z - 2, n_z - 1), (1, 0)])
    line = up + [ends] + down[1:]
    cos_tab, sin_tab = rotary_tables(rows, n_ctx)
    fi, w, q, kv, cos, sin = local_call(
        "qkv",
        qkv_body,
        places,
        [*plane, stack, over_ctx(stack, 1), vec, bias, cos_tab, sin_tab],
        [
            ((near_rows, width), BF16),
            ((width, three), BF16),
            ((near_rows, GROUP_COLS), BF16),
            ((2 * near_rows, GROUP_COLS), BF16),
            ((near_rows, 128), F32),
            ((near_rows, 128), F32),
        ],
        flops=2 * near_rows * width * 4 * GROUP_COLS,
    )
    *att, dkq, dv, far = local_call(
        "attend",
        attend_body,
        places,
        [q, kv, over_ctx(kv, 1), *plane, ow_near, over_ctx(ow_near, 1)],
        [((rows, GROUP_COLS), BF16)] * GROUPS
        + [
            ((near_rows, 2 * GROUP_COLS), F32),
            ((near_rows, GROUP_COLS), F32),
            ((near_rows, 2 * GROUP_COLS), BF16),
        ],
        [
            pltpu.VMEM((2 * near_rows, GROUP_COLS), BF16),
            pltpu.VMEM((2 * near_rows, GROUP_COLS), BF16),
            pltpu.VMEM((near_rows, GROUP_COLS), BF16),
            pltpu.VMEM((near_rows, GROUP_COLS), BF16),
            pltpu.VMEM((GROUP_COLS, width), BF16),
            pltpu.VMEM((near_rows, width), BF16),
            pltpu.VMEM((GROUPS, rows, GROUP_COLS), BF16),
        ],
        flops=2 * 7 * 256 * GROUP_HEADS * near_rows * 2 * near_rows,
        after=[up[1], down[1]],
    )
    att = [
        over_both(
            att[m], [(a, b, 2 * (b ^ m) + a % 2, a // 2) for a in range(n_ctx) for b in range(n_z)]
        )
        for m in range(GROUPS)
    ]

    ca, *sends, keep, send = local_call(
        "joined",
        joined_body,
        places,
        [dkq, dv, over_ctx(far, 1), w, fi, cos, sin, vec, *plane, g],
        [((rows, width), F32)]
        + [((rows, width), BF16)] * 3
        + [
            ((n_z, part + EXTRA, three), F32),
            ((n_z, part + EXTRA, three), BF16),
        ],
        [
            pltpu.VMEM((near_rows, 2 * GROUP_COLS), BF16),
            pltpu.VMEM((near_rows, GROUP_COLS), BF16),
            pltpu.VMEM((width, three), F32),
            pltpu.VMEM((near_rows, width), F32),
            pltpu.VMEM((GROUPS, EXTRA, three), F32),
        ],
        flops=2 * 2 * near_rows * width * three,
        after=[up[2], down[2]],
    )
    ca_sends = sends
    chunk = -(-(width + hid + shard) // (n_ctx * EXTRA)) * EXTRA
    *ffn_outs, ffn_sums, si, gb, active, hidden_grad, att = local_call(
        "ffn",
        ffn_body,
        places,
        [*line, up_weight, down_weight, up_bias.reshape(1, -1), vec, out_weight, *att],
        [((pair, width), F32)]
        + [((pair, width), BF16)] * 3
        + [((EXTRA, width), BF16)]
        + [((near_rows, n), BF16) for n in (width, width, hid, hid, GROUP_COLS)],
        [pltpu.VMEM((near_rows, width), F32), pltpu.VMEM((near_rows, width), F32)],
        flops=2 * 4 * near_rows * width * hid,
        after=[keep],
    )
    ffn_keep, ffn_send = local_call(
        "ffn_dw",
        ffn_dw_body,
        places,
        [si, gb, active, hidden_grad, att, ffn_sums],
        [((GROUPS * chunk, width), F32), ((GROUPS * chunk + EXTRA, width), BF16)],
        [pltpu.VMEM((n_ctx * chunk, width), F32)],
        flops=2 * 2 * near_rows * width * hid,
    )

    ffn_far = over_ctx(ffn_send, 1)
    own_qkv, *sends = local_call(
        "qkv_pair",
        qkv_pair_body,
        places,
        [keep, over_ctx(send, 1), ffn_sums, ffn_far],
        [((part + EXTRA, three), F32)] + [((part + EXTRA, three), BF16)] * 3,
        [pltpu.VMEM((GROUPS, EXTRA, three), F32)],
    )
    qkv_total, *line_sends = local_call(
        "qkv_sum",
        sum_body,
        places,
        [own_qkv] + [over_z(sends[k - 1], k) for k in range(1, n_z)],
        [((part + EXTRA, three), BF16)],
        through=ffn_outs[1:],
    )
    from_line = [around_z(line_sends[k - 1], -k) for k in range(1, n_z)]
    own, *sends = local_call(
        "ffn_pair",
        ffn_pair_body,
        places,
        [ffn_keep, ffn_far, *ca_sends],
        [((chunk, width), F32)] + [((chunk + rows, width), BF16)] * 3,
    )
    from_plane = [over_ctx(sends[j - 1], 2 * j) for j in range(1, GROUPS)]
    (ffn_total,) = local_call(
        "plane_share",
        ffn_sum_body,
        places,
        [own, *from_plane, qkv_total],
        [((chunk + part, width), BF16)],
    )
    (near,) = local_call(
        "stack",
        stack_body,
        places,
        chips(ffn_total),
        [((GROUPS * (chunk + part), width), BF16)],
        after=from_line,
    )
    up_dw, down_dw, out_dw, qkv_dw, *sums, up_db, qkv_db = local_call(
        "spread",
        spread_body,
        places,
        [near, over_ctx(near, 1)],
        [
            ((width, hid), F32),
            ((hid, width), F32),
            ((shard, width), F32),
            ((shard, 3 * width), F32),
            *[((shard,), F32)] * 5,
            ((hid,), F32),
            ((three,), F32),
        ],
        [
            pltpu.VMEM((n_ctx * chunk, width), F32),
            pltpu.VMEM((GROUPS, EXTRA, three), F32),
            pltpu.VMEM((GROUPS, shard, three), F32),
        ],
        vmem=36,
    )

    layer_out, input_grad = local_call(
        "token",
        token_body,
        places,
        [xg, vec, ca, ffn_outs[0], *from_plane, *from_line],
        [((rows, width), BF16), ((rows, width), F32)],
        after=[near],
    )
    return (
        layer_out.reshape(tokens.shape),
        input_grad.reshape(tokens.shape),
        sums[0],
        sums[1],
        sums[3],
        sums[4],
        qkv_dw,
        qkv_db,
        out_dw,
        sums[2],
        up_dw,
        up_db,
        down_dw,
        sums[2],
    )


def solution(mesh):
    in_specs = (
        P("fsdp", "ctx", None),
        P("fsdp", "ctx", None),
        P("fsdp"),
        P("fsdp"),
        P("fsdp"),
        P("fsdp"),
        P("fsdp", None),
        P("fsdp"),
        P("fsdp", None),
        P("fsdp"),
        P(None, "fsdp"),
        P("fsdp"),
        P("fsdp", None),
        P("fsdp"),
    )
    out_specs = (
        P("fsdp", "ctx", None),
        P("fsdp", "ctx", None),
        P("fsdp"),
        P("fsdp"),
        P("fsdp"),
        P("fsdp"),
        P("fsdp", None),
        P("fsdp"),
        P("fsdp", None),
        P("fsdp"),
        P(None, "fsdp"),
        P("fsdp"),
        P("fsdp", None),
        P("fsdp"),
    )
    per_device = block_shards if fits(mesh) else shards
    return jax.shard_map(per_device, mesh=mesh, in_specs=in_specs, out_specs=out_specs, check_vma=False)
```
